32 devices in a mesh: rows: 16 (over z, y, x), heads: 2 (over core).
Axes of the slice: x: 2, y: 2, z: 4, core: 2. Of those that a mesh axis runs over, the one named last changes fastest.
Arguments:
- tokens_in: bfloat16 [32768, 384], P('rows')
- neighbours: int32 [32768, 27], P('rows'), may hold values from -129 to 128, as said below
- scene_lengths: int32 [4], replicated, may hold values from 1 to 768, 1024 in all
- window_mask: int32 [32768], P('rows'), may hold values from 0 to 1, as said below
- small_params: float32 [41, 384], replicated
- qkv_weight: bfloat16 [3, 384, 384], P(None, 'heads'), may hold values from -0.3125 to 0.3125
- proj_weight: bfloat16 [384, 384], P('heads'), may hold values from -0.875 to 0.875
- fc1_weight: bfloat16 [1536, 384], P('heads'), may hold values from -0.3125 to 0.3125
- fc2_weight: bfloat16 [1536, 384], P('heads'), may hold values from -0.15625 to 0.15625
- cotangent: float32 [32768, 384], P('rows')
- owners: int32 [144], replicated, may hold values from 0 to 15, as said below
- small_first: float32 [41, 384], replicated
- small_second: float32 [41, 384], replicated
- tile_first: float32 [2, 224, 16, 384], P('heads', 'rows')
- tile_second: float32 [2, 224, 16, 384], P('heads', 'rows')
Outputs:
- output: float32 [32768, 384], P('rows')
- input_grad: float32 [32768, 384], P('rows')
- tile_weight: float32 [2, 224, 16, 384], P('heads', 'rows')
- tile_first_new: float32 [2, 224, 16, 384], P('heads', 'rows')
- tile_second_new: float32 [2, 224, 16, 384], P('heads', 'rows')
- tile_weight_low: bfloat16 [2, 224, 16, 384], P('heads', 'rows')
- small_new: float32 [41, 384], replicated
- small_first_new: float32 [41, 384], replicated
- small_second_new: float32 [41, 384], replicated
The draws below stay inside these ranges and needn't reach their ends.
Inputs may be any that keep to these rules, and one draw needn't show every extreme that they name: `neighbours`: each entry is -128 - 1 (no neighbour) or an offset of -128 to 128 whose row r plus the offset lies among the nodes; entry 13 is 0; entries 0 and 26 are -128 and 128 where those rows exist. `scene_lengths`: lengths count windows of 32 rows and sum to 1024. `window_mask`: the first row of every window is 1. `owners`: no index of rows owns more than 14 tiles; some index owns exactly 14.
All inputs are finite; a program needn't handle non-finite values.
Results may differ from the reference program's by a relative error of at most 0.0049.
Values may be sent and summed in bfloat16 or wider, within the bound.
A program may use at most 192 MiB of HBM per device.

```python
import math
import jax
import jax.numpy as jnp
import numpy as np
from jax import lax

D = 384
HEAD_COUNT = 12
FF = 1536
HEAD_DIM = 32
WIN = 32
HALO = 128
BR = 16
STEP = 3
TOKENS = 32768
WINDOWS = 1024
SCENES = 4
MOST_WIN = 768
NT = 144
CAP = 14
SMALL = 41
N_ROWS = 16
N_HEADS = 2


def rising_rows(key):
    rise = 1.0 + 2.0 * jnp.arange(TOKENS, dtype=jnp.float32)[:, None] / (TOKENS - 1)
    column = jnp.exp(jax.random.uniform(jax.random.fold_in(key, 1), (1, D), minval=-0.7, maxval=0.7))
    base_draw = jax.random.normal(key, (TOKENS, D))
    return base_draw * rise * column


def draw_tokens_in(key, part):
    return rising_rows(jax.random.fold_in(key, 21)).astype(jnp.bfloat16)


def draw_cotangent(key, part):
    return rising_rows(jax.random.fold_in(key, 22))


def draw_neighbours(key, part):
    inner = jax.random.fold_in(key, 23)
    row_ids = jnp.arange(TOKENS, dtype=jnp.int32)[:, None]
    offsets = jax.random.randint(inner, (TOKENS, 27), -HALO, HALO + 1)
    taps = jnp.arange(27, dtype=jnp.int32)[None, :]
    offsets = jnp.where(taps == 13, 0, offsets)
    offsets = jnp.where(taps == 0, -HALO, offsets)
    offsets = jnp.where(taps == 26, HALO, offsets)
    target = row_ids + offsets
    dropped = jax.random.randint(jax.random.fold_in(inner, 1), (TOKENS, 27), 0, 4) == 0
    dropped = dropped & (taps != 13) & (taps != 0) & (taps != 26)
    outside = (target < 0) | (target >= TOKENS)
    return jnp.where(dropped | outside, -HALO - 1, offsets).astype(jnp.int32)


def draw_window_mask(key, part):
    random_bits = jax.random.randint(jax.random.fold_in(key, 24), (TOKENS,), 0, 4) > 0
    first_row = jnp.arange(TOKENS, dtype=jnp.int32) % WIN == 0
    return (random_bits | first_row).astype(jnp.int32)


def draw_owners(key, part):
    inner = jax.random.fold_in(key, 25)
    slot_total = N_ROWS * CAP
    shuffled = jax.random.permutation(inner, slot_total)
    picked_device = jax.random.randint(jax.random.fold_in(inner, 1), (), 0, N_ROWS)
    slot_ids = jnp.arange(slot_total, dtype=jnp.int32)
    scored = jnp.where(shuffled // CAP == picked_device, slot_ids, slot_ids + slot_total)
    ordered = shuffled[jnp.argsort(scored)]
    owner_list = (ordered[:NT] // CAP).astype(jnp.int32)
    return owner_list[jax.random.permutation(jax.random.fold_in(inner, 2), NT)].astype(jnp.int32)


def slot_tiles(key):
    owner_list = draw_owners(key, 0)
    tile_order = jnp.arange(NT, dtype=jnp.int32)
    same_owner = (owner_list[:, None] == owner_list[None, :]) & (tile_order[None, :] < tile_order[:, None])
    rank_in = jnp.sum(same_owner.astype(jnp.int32), axis=1)
    return jnp.full((N_ROWS * CAP,), -1, jnp.int32).at[owner_list * CAP + rank_in].set(tile_order)


def tile_scale(key):
    tile_of = slot_tiles(key)
    row_start = tile_of * BR
    half_d = D // N_HEADS
    half_f = FF // N_HEADS
    kind_scale = jnp.where(row_start < 3 * half_d, 1.0, jnp.where(row_start < 4 * half_d, 0.8, jnp.where(row_start < 4 * half_d + half_f, 0.6, 1.4)))
    kind_scale = jnp.where(tile_of < 0, 1.0, kind_scale)
    return (kind_scale * TOKENS ** 0.5)[None, :, None, None]


def moment_noise(key, shape):
    return jax.random.normal(key, shape)


def draw_tile_first(key, part):
    shape = (N_HEADS, N_ROWS * CAP, BR, D)
    return moment_noise(jax.random.fold_in(key, 26), shape) * tile_scale(key)


def draw_tile_second(key, part):
    shape = (N_HEADS, N_ROWS * CAP, BR, D)
    spread = jnp.exp(jax.random.uniform(jax.random.fold_in(key, 27), shape, minval=-0.6931, maxval=2.0794))
    scale = tile_scale(key)
    return spread * scale * scale


def draw_small_params(key, part):
    inner = jax.random.fold_in(key, 28)
    row_ids = jnp.arange(SMALL, dtype=jnp.int32)[:, None]
    noise = jax.random.normal(inner, (SMALL, D))
    gains = jax.random.uniform(jax.random.fold_in(inner, 1), (SMALL, D), minval=0.6, maxval=1.4)
    is_gain = (row_ids == 27) | (row_ids == 29) | (row_ids == 31)
    scale = jnp.where(row_ids < 27, 0.35, 0.3)
    return jnp.where(is_gain, gains, noise * scale)


def small_scale():
    row_ids = jnp.arange(SMALL, dtype=jnp.int32)[:, None]
    query_row = 7.0 / (HEAD_DIM * WIN ** 0.5)
    value_row = 8.0 / (WIN * HEAD_DIM) ** 0.5
    row_scale = jnp.where(row_ids == 35, query_row, jnp.where(row_ids == 36, value_row, 1.5))
    return row_scale * TOKENS ** 0.5


def draw_small_first(key, part):
    return moment_noise(jax.random.fold_in(key, 29), (SMALL, D)) * small_scale()


def draw_small_second(key, part):
    spread = jnp.exp(jax.random.uniform(jax.random.fold_in(key, 30), (SMALL, D), minval=-0.6931, maxval=2.0794))
    scale = small_scale()
    return spread * scale * scale


def shard_levels(key, shape, split, smallest, top_value):
    level = 1.0
    for dim, parts in split:
        heights = jax.random.uniform(jax.random.fold_in(jax.random.fold_in(key, 6), dim), (parts,), jnp.float32, smallest / len(split), top_value / len(split))
        level = level * jnp.repeat(jnp.exp(heights), shape[dim] // parts).reshape((-1,) + (1,) * (len(shape) - 1 - dim))
    return level


def split_up(count, total, bound, slope):
    loads = [(1 << 20) // math.isqrt(grade ** slope) + 1 for grade in range(2, count + 1)]
    rest, given = total - bound - (count - 1), [1] * (count - 1)
    while rest > 0:
        candidates = [i for i in range(count - 1) if given[i] < bound]
        mass, remaining = sum([loads[i] for i in candidates]), rest
        for i in candidates:
            extra = min(bound - given[i], max(1, remaining * loads[i] // mass), rest)
            given[i] = given[i] + extra
            rest = rest - extra
    return np.array([bound] + given)


def uneven_parts(rng, count, total, limit, skew):
    if count == 2:
        one = jax.random.randint(rng, (), max(1, total - limit), min(limit, total - 1) + 1)
        return jnp.stack([one, total - one])
    sizes = jnp.asarray(split_up(count, total, limit, skew), jnp.int32)
    pairs = (count - 1) // 2
    source_of, receiver = sizes[1:1 + 2 * pairs:2], sizes[2:2 + 2 * pairs:2]
    margin = jnp.minimum(source_of - 1, limit - receiver)
    shifted = jax.random.randint(jax.random.fold_in(rng, 1), (pairs,), 0, 1 << 20) % (margin + 1)
    sizes = sizes.at[1:1 + 2 * pairs:2].set(source_of - shifted).at[2:2 + 2 * pairs:2].set(receiver + shifted)
    return sizes[jax.random.permutation(jax.random.fold_in(rng, 2), count)]


def normal_values(stream_key, dims, width, reach, shards=(), held_as=jnp.bfloat16):
    entries = jax.random.normal(stream_key, dims, jnp.float32) * width
    if len(shards) > 0:
        entries = shard_levels(stream_key, dims, shards, -0.22, 0.18) * entries
    return jnp.clip(entries, min=-reach, max=reach).astype(held_as)


def setup_inputs(seed: int = 0) -> dict:
    key_list = jax.random.split(jax.random.key(seed), 16)
    return {
        "tokens_in": draw_tokens_in(jax.random.fold_in(key_list[15], 71), 0),
        "neighbours": draw_neighbours(jax.random.fold_in(key_list[15], 71), 0),
        "scene_lengths": uneven_parts(key_list[2], SCENES, WINDOWS, MOST_WIN, 2).astype(jnp.int32),
        "window_mask": draw_window_mask(jax.random.fold_in(key_list[15], 71), 0),
        "small_params": draw_small_params(jax.random.fold_in(key_list[15], 71), 0),
        "qkv_weight": normal_values(key_list[5], (3, D, D), D ** -0.5, 0.3125, ((1, 2),)),
        "proj_weight": normal_values(key_list[6], (D, D), (D // 8) ** -0.5, 0.875, ((0, 2),)),
        "fc1_weight": normal_values(key_list[7], (FF, D), D ** -0.5, 0.3125, ((0, 2),)),
        "fc2_weight": normal_values(key_list[8], (FF, D), FF ** -0.5, 0.15625, ((0, 2),)),
        "cotangent": draw_cotangent(jax.random.fold_in(key_list[15], 71), 0),
        "owners": draw_owners(jax.random.fold_in(key_list[15], 71), 0),
        "small_first": draw_small_first(jax.random.fold_in(key_list[15], 71), 0),
        "small_second": draw_small_second(jax.random.fold_in(key_list[15], 71), 0),
        "tile_first": draw_tile_first(jax.random.fold_in(key_list[15], 71), 0),
        "tile_second": draw_tile_second(jax.random.fold_in(key_list[15], 71), 0),
    }


@jax.custom_vjp
def low(v):
    return lax.optimization_barrier(v.astype(jnp.bfloat16)).astype(jnp.float32)

@jax.custom_vjp
def low_back(v):
    return v

def low_keep(v):
    return (low(v), None)

def low_pass(kept, grad):
    return (grad,)

def back_keep(v):
    return (v, None)

def back_low(kept, grad):
    return (low(grad),)
low.defvjp(low_keep, low_pass)
low_back.defvjp(back_keep, back_low)
norm_eps = 1e-05
adam_rate = 0.05
beta_one = 0.5
beta_two = 0.5
adam_eps = 1e-08
decay_rate = 0.05
masked_score = -1e+30
highest = lax.Precision.HIGHEST

def scene_index(positions, scene_ends):
    return lax.optimization_barrier(jnp.sum((positions[..., None] >= scene_ends).astype(jnp.int32), axis=-1))

def layer_norm(values, norm_gain, norm_shift):
    centre = values - lax.optimization_barrier(jnp.mean(values, axis=1, keepdims=True))
    factor = lax.rsqrt(lax.optimization_barrier(jnp.mean(centre * centre, axis=1, keepdims=True)) + norm_eps)
    return centre * factor * norm_gain + norm_shift

def gelu_value(hidden):
    return 0.5 * hidden * (1.0 + lax.erf(hidden * 0.5 ** 0.5))

def adam_step(weight, gradient, first_moment, second_moment, decay_factor):
    first_new = beta_one * first_moment + (1.0 - beta_one) * gradient
    second_new = beta_two * second_moment + (1.0 - beta_two) * gradient * gradient
    first_hat = first_new / (1.0 - beta_one ** STEP)
    second_hat = second_new / (1.0 - beta_two ** STEP)
    weight_new = weight - adam_rate * (first_hat / (jnp.sqrt(second_hat) + adam_eps) + decay_factor * weight)
    return (weight_new, first_new, second_new)

def forward(tokens, params, qkv_full, proj_full, fc1_full, fc2_full, near_index, usable, key_keep):
    filtered = jnp.zeros(tokens.shape, jnp.float32)
    for position in range(27):
        filtered = filtered + usable[:, position:position + 1] * params[position] * tokens[near_index[:, position]]
    centre = lax.optimization_barrier(jnp.mean(filtered, axis=0))
    spread = lax.optimization_barrier(jnp.mean(filtered * filtered, axis=0)) - centre * centre
    cpe = (filtered - centre) * lax.rsqrt(spread + norm_eps) * params[27] + params[28]
    resid = tokens + cpe
    normed_one = low(layer_norm(resid, params[29], params[30]))
    qkv_bias = jnp.stack([params[35], jnp.zeros_like(params[35]), params[36]])
    projected = jnp.einsum('nd,jcd->jnc', normed_one, qkv_full, precision=highest) + qkv_bias[:, None, :]
    qkv_low = low(low_back(projected * HEAD_DIM ** (-0.5)))
    shape_four = (WINDOWS, WIN, HEAD_COUNT, HEAD_DIM)
    queries = qkv_low[0].reshape(shape_four)
    key_part = qkv_low[1].reshape(shape_four)
    value_part = qkv_low[2].reshape(shape_four)
    raw_scores = low_back(jnp.einsum('wqhd,wkhd->whqk', queries, key_part, precision=highest))
    scores = jnp.where(key_keep, raw_scores, masked_score)
    row_top = lax.optimization_barrier(jnp.max(scores, axis=-1, keepdims=True))
    powers = jnp.exp(scores - row_top)
    attn_probs = low(powers / lax.optimization_barrier(jnp.sum(powers, axis=-1, keepdims=True)))
    mixture = jnp.einsum('whqk,wkhd->wqhd', attn_probs, value_part, precision=highest).reshape(TOKENS, D)
    mixture = low(low_back(mixture))
    branch = low_back(jnp.dot(mixture, proj_full, precision=highest) + params[33])
    after_attn = resid + branch
    normed_two = low(layer_norm(after_attn, params[31], params[32]))
    hidden = low_back(jnp.dot(normed_two, fc1_full.T, precision=highest) + params[37:].reshape(FF))
    activation = low(gelu_value(hidden))
    ffn_part = low_back(jnp.dot(activation, fc2_full, precision=highest) + params[34])
    return after_attn + ffn_part

def stacked(qkv_full, proj_full, fc1_full, fc2_full):
    half_d = D // N_HEADS
    half_f = FF // N_HEADS
    pieces = []
    for head_id in range(N_HEADS):
        block = jnp.concatenate([qkv_full[:, head_id * half_d:(head_id + 1) * half_d].reshape(3 * half_d, D), proj_full[head_id * half_d:(head_id + 1) * half_d], fc1_full[head_id * half_f:(head_id + 1) * half_f], fc2_full[head_id * half_f:(head_id + 1) * half_f]], axis=0)
        pieces.append(block.reshape(NT, BR, D))
    return jnp.stack(pieces)

def reference(tokens_in, neighbours, scene_lengths, window_mask, small_params, qkv_weight, proj_weight, fc1_weight, fc2_weight, cotangent, owners, small_first, small_second, tile_first, tile_second):
    scene_ends = (jnp.cumsum(scene_lengths) * WIN).astype(jnp.int32)
    row_ids = jnp.arange(TOKENS, dtype=jnp.int32)
    target = (row_ids[:, None] + neighbours).astype(jnp.int32)
    inside = (neighbours >= -HALO) & (target >= 0) & (target < TOKENS)
    near_index = jnp.clip(target, 0, TOKENS - 1).astype(jnp.int32)
    usable = (inside & (scene_index(near_index, scene_ends) == scene_index(row_ids, scene_ends)[:, None])).astype(jnp.float32)
    key_keep = window_mask.reshape(WINDOWS, 1, 1, WIN) > 0

    def forward_fn(tokens, params, qkv_full, proj_full, fc1_full, fc2_full):
        return forward(tokens, params, qkv_full, proj_full, fc1_full, fc2_full, near_index, usable, key_keep)
    output, pullback = jax.vjp(forward_fn, tokens_in.astype(jnp.float32), small_params, qkv_weight.astype(jnp.float32), proj_weight.astype(jnp.float32), fc1_weight.astype(jnp.float32), fc2_weight.astype(jnp.float32))
    input_grad, small_grad, qkv_grad, proj_grad, fc1_grad, fc2_grad = pullback(cotangent)
    tile_order = jnp.arange(NT, dtype=jnp.int32)
    same_owner = (owners[:, None] == owners[None, :]) & (tile_order[None, :] < tile_order[:, None])
    rank_in = lax.optimization_barrier(jnp.sum(same_owner.astype(jnp.int32), axis=1))
    slot_tile = jnp.full((N_ROWS * CAP,), -1, jnp.int32).at[owners * CAP + rank_in].set(tile_order)
    slot_live = (slot_tile >= 0).astype(jnp.float32)[None, :, None, None]
    chosen = jnp.clip(slot_tile, 0, NT - 1)
    grad_tiles = stacked(qkv_grad, proj_grad, fc1_grad, fc2_grad)[:, chosen] * slot_live
    weight_tiles = stacked(qkv_weight.astype(jnp.float32), proj_weight.astype(jnp.float32), fc1_weight.astype(jnp.float32), fc2_weight.astype(jnp.float32))[:, chosen]
    new_weight, new_first, new_second = adam_step(weight_tiles, grad_tiles, tile_first, tile_second, decay_rate)
    new_weight = new_weight * slot_live
    new_first = new_first * slot_live
    new_second = new_second * slot_live
    small_new, small_first_new, small_second_new = adam_step(small_params, small_grad, small_first, small_second, 0.0)
    return (output, input_grad, new_weight, new_first, new_second, new_weight.astype(jnp.bfloat16), small_new, small_first_new, small_second_new)
```

```python
import functools

import jax
import jax.numpy as jnp
from jax import lax
from jax.experimental import pallas as pl
from jax.experimental.pallas import tpu as pltpu
from jax.sharding import PartitionSpec as P

HEAD_DIM = 32
WIN = 32
HALO = 128
BR = 16
STEP = 3
TAPS = 27
LANES = 128

norm_eps = 1e-05
adam_rate = 0.05
beta_one = 0.5
beta_two = 0.5
adam_eps = 1e-08
decay_rate = 0.05
masked_score = -1e30

F32 = jnp.float32
BF16 = jnp.bfloat16


def adam_step(weight, gradient, first_moment, second_moment, decay_factor):
    first_new = beta_one * first_moment + (1.0 - beta_one) * gradient
    second_new = beta_two * second_moment + (1.0 - beta_two) * gradient * gradient
    first_hat = first_new / (1.0 - beta_one**STEP)
    second_hat = second_new / (1.0 - beta_two**STEP)
    weight_new = weight - adam_rate * (
        first_hat / (jnp.sqrt(second_hat) + adam_eps) + decay_factor * weight
    )
    return (weight_new, first_new, second_new)


def dot_plain(a, b):
    return jnp.dot(a, b, preferred_element_type=F32)


def dot_last(a, b):
    return lax.dot_general(a, b, (((1,), (1,)), ((), ())), preferred_element_type=F32)


def dot_first(a, b):
    return lax.dot_general(a, b, (((0,), (0,)), ((), ())), preferred_element_type=F32)


def col_sum(v):
    return jnp.sum(v, axis=0, keepdims=True)


def layer_norm(v):
    centre = v - jnp.mean(v, axis=1, keepdims=True)
    factor = lax.rsqrt(jnp.mean(centre * centre, axis=1, keepdims=True) + norm_eps)
    return centre * factor, factor


def norm_back(upstream, unit_part, factor, gain):
    scaled = upstream * gain
    return factor * (
        scaled
        - jnp.mean(scaled, axis=1, keepdims=True)
        - unit_part * jnp.mean(scaled * unit_part, axis=1, keepdims=True)
    )


def full_spec(shape):
    zeros = (0,) * len(shape)
    return pl.BlockSpec(shape, lambda i: zeros)


def filter_kernel(x_ref, near_ref, taps_ref, out_ref, stat_ref, *, block):
    i = pl.program_id(0)
    width = block + 2 * HALO

    @pl.when(i == 0)
    def _():
        stat_ref[...] = jnp.zeros_like(stat_ref)

    window = x_ref[pl.ds(pl.multiple_of(i * block, block), width), :]
    place = lax.broadcasted_iota(jnp.int32, (block, TAPS), 0) + near_ref[...] + HALO
    column = lax.broadcasted_iota(jnp.int32, (block, width), 1)
    total = jnp.zeros(out_ref.shape, F32)
    group = 3
    for first in range(0, TAPS, group):
        hot = jnp.concatenate(
            [
                (place[:, k : k + 1] == column).astype(F32).astype(BF16)
                for k in range(first, first + group)
            ],
            axis=0,
        )
        picked = dot_plain(hot, window)
        for j in range(group):
            total += picked[j * block : (j + 1) * block] * taps_ref[first + j : first + j + 1, :]
    out_ref[...] = total
    stat_ref[0:1, :] += col_sum(total)
    stat_ref[1:2, :] += col_sum(total * total)


def filter_forward(extended, near, taps, block=128):
    rows, width = near.shape[0], extended.shape[1]
    outs = [jax.ShapeDtypeStruct((rows, width), F32), jax.ShapeDtypeStruct((8, width), F32)]
    return pl.pallas_call(
        functools.partial(filter_kernel, block=block),
        grid=(rows // block,),
        in_specs=[
            full_spec(extended.shape),
            pl.BlockSpec((block, TAPS), lambda i: (i, 0)),
            full_spec(taps.shape),
        ],
        out_specs=[pl.BlockSpec((block, width), lambda i: (i, 0)), full_spec(outs[1].shape)],
        out_shape=outs,
        compiler_params=pltpu.CompilerParams(vmem_limit_bytes=40 << 20),
    )(extended, near, taps)


def filter_back_kernel(
    x_ref, filt_ref, dres_ref, near_ref, taps_ref, stat_ref, back_ref, params_ref, out_ref,
    tap_grad_ref, *, block, node_total
):
    i = pl.program_id(0)
    width = block + 2 * HALO

    @pl.when(i == 0)
    def _():
        out_ref[...] = jnp.zeros_like(out_ref)
        tap_grad_ref[...] = jnp.zeros_like(tap_grad_ref)

    centre = stat_ref[0:1] / node_total
    inv_std = lax.rsqrt(stat_ref[1:2] / node_total - centre * centre + norm_eps)
    bn_norm = (filt_ref[...] - centre) * inv_std
    grad = (
        params_ref[27:28]
        * inv_std
        * (
            dres_ref[...]
            - back_ref[1:2] * (1.0 / node_total)
            - bn_norm * (back_ref[0:1] * (1.0 / node_total))
        )
    ).astype(BF16)
    window = pl.ds(pl.multiple_of(i * block, block), width)
    place = lax.broadcasted_iota(jnp.int32, (TAPS, block), 1) + near_ref[...] + HALO
    row = lax.broadcasted_iota(jnp.int32, (width, block), 0)
    tokens = x_ref[window, :].astype(F32)
    total = jnp.zeros(tokens.shape, F32)
    for k in range(TAPS):
        hot = (place[k : k + 1, :] == row).astype(F32).astype(BF16)
        spread = dot_plain(hot, grad)
        total += spread * taps_ref[k : k + 1, :]
        tap_grad_ref[k : k + 1, :] += col_sum(spread * tokens)
    out_ref[window, :] += total


def filter_backward(extended, filtered, dres, near_t, taps, stat, back, params, node_total, block=256):
    rows, width = filtered.shape
    outs = [
        jax.ShapeDtypeStruct((rows + 2 * HALO, width), F32),
        jax.ShapeDtypeStruct((32, width), F32),
    ]
    by_rows = pl.BlockSpec((block, width), lambda i: (i, 0))
    return pl.pallas_call(
        functools.partial(filter_back_kernel, block=block, node_total=node_total),
        grid=(rows // block,),
        in_specs=[
            full_spec(extended.shape),
            by_rows,
            by_rows,
            pl.BlockSpec((TAPS, block), lambda i: (0, i)),
            full_spec(taps.shape),
            full_spec(stat.shape),
            full_spec(back.shape),
            full_spec(params.shape),
        ],
        out_specs=[full_spec(outs[0].shape), full_spec(outs[1].shape)],
        out_shape=outs,
        compiler_params=pltpu.CompilerParams(vmem_limit_bytes=48 << 20),
    )(extended, filtered, dres, near_t, taps, stat, back, params)


def block_kernel(
    filt_ref, tok_ref, mask_ref, cot_ref, stat_ref, params_ref, bias_ref, weight_ref,
    out_ref, dres_ref, grad_ref, small_ref, bias_grad_ref, *, node_total, parts, width, units, block
):
    i = pl.program_id(0)

    @pl.when(i == 0)
    def _():
        grad_ref[...] = jnp.zeros_like(grad_ref)
        small_ref[...] = jnp.zeros_like(small_ref)
        bias_grad_ref[...] = jnp.zeros_like(bias_grad_ref)

    part = width // parts
    unit_part = units // parts
    scale = HEAD_DIM**-0.5

    def weight_rows(low, count):
        return jnp.concatenate([weight_ref[h, low : low + count] for h in range(parts)], axis=0)

    def qkv_rows(j):
        return weight_rows(j * part, part)

    def proj_rows():
        return weight_rows(3 * part, part)

    def add_grad(low, value):
        for h in range(parts):
            grad_ref[h, low : low + part] += value[h * part : (h + 1) * part]

    def param(row):
        return params_ref[row : row + 1, :]

    def add_small(row, value):
        small_ref[row : row + 1, :] += value

    centre = stat_ref[0:1] / node_total
    inv_std = lax.rsqrt(stat_ref[1:2] / node_total - centre * centre + norm_eps)
    bn_norm = (filt_ref[...] - centre) * inv_std
    resid = tok_ref[...].astype(F32) + (bn_norm * param(27) + param(28))
    unit_one, factor_one = layer_norm(resid)
    normed_one = (unit_one * param(29) + param(30)).astype(BF16)
    query = ((dot_last(normed_one, qkv_rows(0)) + param(35)) * scale).astype(BF16)
    key = (dot_last(normed_one, qkv_rows(1)) * scale).astype(BF16)
    value = ((dot_last(normed_one, qkv_rows(2)) + param(36)) * scale).astype(BF16)

    side = LANES
    heads = LANES // HEAD_DIM
    groups = width // LANES
    lane_head = lax.broadcasted_iota(jnp.int32, (side, LANES), 1) // HEAD_DIM
    window_q = lax.broadcasted_iota(jnp.int32, (side, side), 0) // WIN
    window_k = lax.broadcasted_iota(jnp.int32, (side, side), 1) // WIN

    def stack_heads(a):
        return jnp.concatenate(
            [jnp.where(lane_head == j, a, jnp.zeros_like(a)) for j in range(heads)], axis=0
        )

    def pick_heads(a):
        picked = a[:side]
        for j in range(1, heads):
            picked = jnp.where(lane_head == j, a[j * side : (j + 1) * side], picked)
        return picked

    def cut(a, s, g):
        return a[s * side : (s + 1) * side, g * LANES : (g + 1) * LANES]

    kept = {}
    mixture = []
    for s in range(block // side):
        keep = (window_q == window_k) & (mask_ref[0:1, s * side : (s + 1) * side] > 0)
        mixed = []
        for g in range(groups):
            query_g = cut(query, s, g)
            keys = stack_heads(cut(key, s, g))
            values = stack_heads(cut(value, s, g))
            scores = dot_last(query_g, keys)
            probs = []
            for j in range(heads):
                score = jnp.where(keep, scores[:, j * side : (j + 1) * side], masked_score)
                power = jnp.exp(score - jnp.max(score, axis=1, keepdims=True))
                probs.append(power / jnp.sum(power, axis=1, keepdims=True))
            probs = jnp.concatenate(probs, axis=1)
            probs_low = probs.astype(BF16)
            mixed.append(dot_plain(probs_low, values))
            kept[s, g] = (query_g, keys, values, probs, probs_low)
        mixture.append(jnp.concatenate(mixed, axis=1))
    mixture = jnp.concatenate(mixture, axis=0).astype(BF16)
    after = resid + (dot_plain(mixture, proj_rows()) + param(33))
    unit_two, factor_two = layer_norm(after)
    normed_two = (unit_two * param(31) + param(32)).astype(BF16)

    cotangent = cot_ref[...]
    grad_ffn = cotangent.astype(BF16)
    ffn = jnp.zeros_like(after)
    grad_normed_two = jnp.zeros_like(after)
    chunk = unit_part // 2
    for h in range(parts):
        for c in range(2):
            low = 4 * part + c * chunk
            unit = h * unit_part + c * chunk
            fc1 = weight_ref[h, low : low + chunk]
            fc2 = weight_ref[h, low + unit_part : low + unit_part + chunk]
            hidden = dot_last(normed_two, fc1) + bias_ref[0:1, unit : unit + chunk]
            cumulative = 0.5 * (1.0 + lax.erf(hidden * 0.5**0.5))
            activation = (hidden * cumulative).astype(BF16)
            density = jnp.exp(-0.5 * hidden * hidden) * (2.0 * jnp.pi) ** (-0.5)
            ffn += dot_plain(activation, fc2)
            grad_hidden = (
                dot_last(grad_ffn, fc2) * (cumulative + hidden * density)
            ).astype(BF16)
            grad_normed_two += dot_plain(grad_hidden, fc1)
            grad_ref[h, low : low + chunk] += dot_first(grad_hidden, normed_two)
            grad_ref[h, low + unit_part : low + unit_part + chunk] += dot_first(activation, grad_ffn)
            bias_grad_ref[0:1, unit : unit + chunk] += col_sum(grad_hidden.astype(F32))
    out_ref[...] = after + (ffn + param(34))
    add_small(34, col_sum(grad_ffn.astype(F32)))

    grad_after = cotangent + norm_back(grad_normed_two, unit_two, factor_two, param(31))
    add_small(31, col_sum(grad_normed_two * unit_two))
    add_small(32, col_sum(grad_normed_two))
    grad_branch = grad_after.astype(BF16)
    add_grad(3 * part, dot_first(mixture, grad_branch))
    add_small(33, col_sum(grad_branch.astype(F32)))
    grad_mixture = dot_last(grad_branch, proj_rows()).astype(BF16)

    grads = ([], [], [])
    for s in range(block // side):
        here = ([], [], [])
        for g in range(groups):
            query_g, keys, values, probs, probs_low = kept[s, g]
            grad_mix = cut(grad_mixture, s, g)
            grad_probs = dot_last(grad_mix, values)
            grad_scores = []
            for j in range(heads):
                prob = probs[:, j * side : (j + 1) * side]
                term = prob * grad_probs[:, j * side : (j + 1) * side]
                grad_scores.append(
                    (term - prob * jnp.sum(term, axis=1, keepdims=True)).astype(BF16)
                )
            grad_scores = jnp.concatenate(grad_scores, axis=1)
            here[0].append(dot_plain(grad_scores, keys))
            here[1].append(pick_heads(dot_first(grad_scores, query_g)))
            here[2].append(pick_heads(dot_first(probs_low, grad_mix)))
        for kind in range(3):
            grads[kind].append(jnp.concatenate(here[kind], axis=1))
    grad_qkv = [jnp.concatenate(kind, axis=0).astype(BF16) for kind in grads]
    grad_normed_one = jnp.zeros_like(resid)
    for j in range(3):
        grad_normed_one += dot_plain(grad_qkv[j], qkv_rows(j))
        add_grad(j * part, scale * dot_first(grad_qkv[j], normed_one))
    grad_normed_one = scale * grad_normed_one
    add_small(35, scale * col_sum(grad_qkv[0].astype(F32)))
    add_small(36, scale * col_sum(grad_qkv[2].astype(F32)))
    dres = grad_after + norm_back(grad_normed_one, unit_one, factor_one, param(29))
    add_small(29, col_sum(grad_normed_one * unit_one))
    add_small(30, col_sum(grad_normed_one))
    add_small(27, col_sum(dres * bn_norm))
    add_small(28, col_sum(dres))
    dres_ref[...] = dres


def block_step(filtered, tokens, mask, cotangent, stat, params, bias, weights, node_total, block=256):
    rows, width = filtered.shape
    parts, units = weights.shape[0], bias.shape[1]
    outs = [
        jax.ShapeDtypeStruct((rows, width), F32),
        jax.ShapeDtypeStruct((rows, width), F32),
        jax.ShapeDtypeStruct(weights.shape, F32),
        jax.ShapeDtypeStruct(params.shape, F32),
        jax.ShapeDtypeStruct(bias.shape, F32),
    ]
    by_rows = pl.BlockSpec((block, width), lambda i: (i, 0))
    return pl.pallas_call(
        functools.partial(
            block_kernel, node_total=node_total, parts=parts, width=width, units=units, block=block
        ),
        grid=(rows // block,),
        in_specs=[
            by_rows,
            by_rows,
            pl.BlockSpec((1, block), lambda i: (0, i)),
            by_rows,
            full_spec(stat.shape),
            full_spec(params.shape),
            full_spec(bias.shape),
            full_spec(weights.shape),
        ],
        out_specs=[by_rows, by_rows] + [full_spec(o.shape) for o in outs[2:]],
        out_shape=outs,
        compiler_params=pltpu.CompilerParams(vmem_limit_bytes=56 << 20),
    )(filtered, tokens, mask, cotangent, stat, params, bias, weights)


def local(
    tokens_in, neighbours, scene_lengths, window_mask, small_params, qkv_weight, proj_weight,
    fc1_weight, fc2_weight, cotangent, owners, small_first, small_second, tile_first, tile_second
):
    rows_here, width = tokens_in.shape
    row_count = lax.axis_size("rows")
    parts = lax.axis_size("heads")
    row_rank = lax.axis_index("rows")
    part_rank = lax.axis_index("heads")
    rows = rows_here // parts
    node_total = rows_here * row_count
    first = part_rank * rows
    both = ("rows", "heads")

    def own(a):
        return lax.dynamic_slice_in_dim(a, first, rows, 0)

    weight_stack = jnp.concatenate(
        [qkv_weight.reshape(-1, width), proj_weight, fc1_weight, fc2_weight], axis=0
    )
    weights = lax.all_gather(weight_stack, "heads")

    up = [(i, i + 1) for i in range(row_count - 1)]
    down = [(j, i) for i, j in up]
    before = lax.ppermute(tokens_in[rows_here - HALO :], "rows", up)
    after = lax.ppermute(tokens_in[:HALO], "rows", down)
    extended = lax.dynamic_slice_in_dim(
        jnp.concatenate([before, tokens_in, after], axis=0), first, rows + 2 * HALO, 0
    )

    scene_ends = (jnp.cumsum(scene_lengths) * WIN).astype(jnp.int32)
    own_rows = row_rank * rows_here + first + jnp.arange(rows, dtype=jnp.int32)
    passed = scene_ends[None, :] <= own_rows[:, None]
    scene_low = jnp.max(jnp.where(passed, scene_ends[None, :], 0), axis=1)
    scene_high = jnp.min(jnp.where(passed, node_total, scene_ends[None, :]), axis=1)
    near = own(neighbours)
    target = own_rows[:, None] + near
    usable = (near >= -HALO) & (target >= scene_low[:, None]) & (target < scene_high[:, None])
    near = jnp.where(usable, near, -8 * HALO)

    taps = small_params[:TAPS]
    filtered, stat = filter_forward(extended, near, taps)
    stat = lax.psum(stat, both)
    bias = small_params[37:].reshape(1, -1)
    output, dres, weight_grad, small_grad, bias_grad = block_step(
        filtered, own(tokens_in), own(window_mask)[None], own(cotangent), stat, small_params, bias,
        weights, node_total
    )
    output = lax.all_gather(output, "heads", axis=0, tiled=True)
    small_rest = lax.psum(
        jnp.concatenate([small_grad[TAPS:37], bias_grad.reshape(-1, width)], axis=0), both
    )

    conv_back, tap_grad = filter_backward(
        extended, filtered, dres, near.T, taps, stat, small_rest[:8], small_params, node_total
    )
    line = [(i, i + 1) for i in range(row_count * parts - 1)]
    back = [(j, i) for i, j in line]
    rims = conv_back.astype(BF16)
    from_before = lax.ppermute(rims[rows + HALO :], both, line).astype(F32)
    from_after = lax.ppermute(rims[:HALO], both, back).astype(F32)
    input_grad = dres + conv_back[HALO : HALO + rows]
    input_grad = jnp.concatenate(
        [
            input_grad[:HALO] + from_before,
            input_grad[HALO : rows - HALO],
            input_grad[rows - HALO :] + from_after,
        ],
        axis=0,
    )
    input_grad = lax.all_gather(input_grad, "heads", axis=0, tiled=True)

    small_all = jnp.concatenate([lax.psum(tap_grad[:TAPS], both), small_rest], axis=0)
    small_new, small_first_new, small_second_new = adam_step(
        small_params, small_all, small_first, small_second, 0.0
    )

    tile_count = owners.shape[0]
    slot_cap = tile_first.shape[1]
    tile_order = jnp.arange(tile_count, dtype=jnp.int32)
    same_owner = (owners[:, None] == owners[None, :]) & (tile_order[None, :] < tile_order[:, None])
    slot_of = owners * slot_cap + jnp.sum(same_owner.astype(jnp.int32), axis=1)
    slot_ids = jnp.arange(row_count * slot_cap, dtype=jnp.int32)
    found = slot_of[None, :] == slot_ids[:, None]
    slot_tile = jnp.max(jnp.where(found, tile_order[None, :], -1), axis=1)
    live = (slot_tile >= 0).astype(F32)[:, None, None]
    chosen = jnp.clip(slot_tile, 0, tile_count - 1)
    own_grad = lax.psum_scatter(weight_grad, "heads", scatter_dimension=0, tiled=False)
    grad_slots = jnp.take(own_grad.reshape(tile_count, BR, width), chosen, axis=0) * live
    tile_grad = lax.psum_scatter(grad_slots, "rows", scatter_dimension=0, tiled=True)
    own_slots = lax.dynamic_slice_in_dim(chosen, row_rank * slot_cap, slot_cap)
    own_live = lax.dynamic_slice_in_dim(live, row_rank * slot_cap, slot_cap)
    tile_old = jnp.take(weight_stack.reshape(tile_count, BR, width), own_slots, axis=0).astype(F32)
    new_weight, new_first, new_second = adam_step(
        tile_old, tile_grad, tile_first[0], tile_second[0], decay_rate
    )
    new_weight = new_weight * own_live
    new_first = new_first * own_live
    new_second = new_second * own_live
    return (
        output,
        input_grad,
        new_weight[None],
        new_first[None],
        new_second[None],
        new_weight.astype(BF16)[None],
        small_new,
        small_first_new,
        small_second_new,
    )


def solution(mesh):
    return jax.shard_map(
        local,
        mesh=mesh,
        in_specs=(
            P("rows", None),
            P("rows", None),
            P(),
            P("rows"),
            P(),
            P(None, "heads", None),
            P("heads", None),
            P("heads", None),
            P("heads", None),
            P("rows", None),
            P(),
            P(),
            P(),
            P("heads", "rows", None, None),
            P("heads", "rows", None, None),
        ),
        out_specs=(
            P("rows", None),
            P("rows", None),
            P("heads", "rows", None, None),
            P("heads", "rows", None, None),
            P("heads", "rows", None, None),
            P("heads", "rows", None, None),
            P(),
            P(),
            P(),
        ),
        check_vma=False,
    )
```

```python
import functools

import jax
import jax.numpy as jnp
from jax import lax
from jax.experimental import pallas as pl
from jax.experimental.pallas import tpu as pltpu
from jax.sharding import PartitionSpec as P

HEAD_DIM = 32
WIN = 32
HALO = 128
BR = 16
STEP = 3
TAPS = 27
LANES = 128

norm_eps = 1e-05
adam_rate = 0.05
beta_one = 0.5
beta_two = 0.5
adam_eps = 1e-08
decay_rate = 0.05
masked_score = -1e30

F32 = jnp.float32
BF16 = jnp.bfloat16


def adam_step(weight, gradient, first_moment, second_moment, decay_factor):
    first_new = beta_one * first_moment + (1.0 - beta_one) * gradient
    second_new = beta_two * second_moment + (1.0 - beta_two) * gradient * gradient
    first_hat = first_new / (1.0 - beta_one**STEP)
    second_hat = second_new / (1.0 - beta_two**STEP)
    weight_new = weight - adam_rate * (
        first_hat / (jnp.sqrt(second_hat) + adam_eps) + decay_factor * weight
    )
    return (weight_new, first_new, second_new)


def dot_plain(a, b):
    return jnp.dot(a, b, preferred_element_type=F32)


def dot_last(a, b):
    return lax.dot_general(a, b, (((1,), (1,)), ((), ())), preferred_element_type=F32)


def dot_first(a, b):
    return lax.dot_general(a, b, (((0,), (0,)), ((), ())), preferred_element_type=F32)


def col_sum(v):
    return jnp.sum(v, axis=0, keepdims=True)


def layer_norm(v):
    centre = v - jnp.mean(v, axis=1, keepdims=True)
    factor = lax.rsqrt(jnp.mean(centre * centre, axis=1, keepdims=True) + norm_eps)
    return centre * factor, factor


def norm_back(upstream, unit_part, factor, gain):
    scaled = upstream * gain
    return factor * (
        scaled
        - jnp.mean(scaled, axis=1, keepdims=True)
        - unit_part * jnp.mean(scaled * unit_part, axis=1, keepdims=True)
    )


def full_spec(shape):
    zeros = (0,) * len(shape)
    return pl.BlockSpec(shape, lambda i: zeros)


MESH = pl.DeviceIdType.MESH


def device_of(index, parts):
    return (index // parts, lax.rem(index, parts))


def greet_all(count, parts, me):
    barrier = pltpu.get_barrier_semaphore()

    def greet(j, carry):
        pl.semaphore_signal(
            barrier, inc=1, device_id=device_of(lax.rem(me + j, count), parts), device_id_type=MESH
        )
        return carry

    lax.fori_loop(1, count, greet, 0)


def await_all(count):
    pl.semaphore_wait(pltpu.get_barrier_semaphore(), count - 1)


def swap_copy(source, landing, send_sem, recv_sem, device):
    return pltpu.make_async_remote_copy(
        src_ref=source, dst_ref=landing, send_sem=send_sem, recv_sem=recv_sem,
        device_id=device, device_id_type=MESH,
    )


def send_to_all(source_of, landing, send_sem, recv_sem, count, parts, me):
    def send(j, carry):
        other = lax.rem(me + j, count)
        swap_copy(
            source_of(other), landing.at[count - j], send_sem.at[j], recv_sem.at[count - j],
            device_of(other, parts),
        ).start()
        return carry

    lax.fori_loop(1, count, send, 0)


def await_from_all(source, landing, send_sem, recv_sem, count, parts, me):
    def wait(j, carry):
        swap_copy(
            source, landing.at[count - j], send_sem.at[j], recv_sem.at[count - j],
            device_of(lax.rem(me + j, count), parts),
        ).wait()
        return carry

    lax.fori_loop(1, count, wait, 0)


def add_landed(own, landing, count):
    return lax.fori_loop(1, count, lambda j, total: total + landing[j], own)


def to_tile(tile_ref, rows):
    tile_ref[...] = jnp.zeros_like(tile_ref)
    groups = rows[0].shape[1] // LANES
    for r, row in enumerate(rows):
        for g in range(groups):
            at = r * groups + g
            tile_ref[at : at + 1, :] = row[:, g * LANES : (g + 1) * LANES]


def from_tile(tile, row, groups):
    at = row * groups
    return jnp.concatenate([tile[at + g : at + g + 1, :] for g in range(groups)], axis=1)


def filter_kernel(
    lengths_ref, tokens_ref, near_ref, taps_ref, qkv_ref, proj_ref, fc1_ref, fc2_ref,
    filt_ref, stat_ref, near_t_ref, ext_ref, stack_ref,
    place_ref, tile, landed, local_sem, side_sem, weight_sem, send_sem, recv_sem,
    *, block, row_count, parts, scenes
):
    row_rank = lax.axis_index("rows")
    part_rank = lax.axis_index("heads")
    count = row_count * parts
    me = row_rank * parts + part_rank
    rows_here, width = tokens_ref.shape
    rows = rows_here // parts
    part = width // parts
    first = part_rank * rows
    node_total = rows_here * row_count
    greet_all(count, parts, me)

    own_copy = pltpu.make_async_copy(
        tokens_ref.at[pl.ds(first, rows)], ext_ref.at[pl.ds(HALO, rows)], local_sem.at[0]
    )
    near_copy = pltpu.make_async_copy(near_ref.at[pl.ds(first, rows)], place_ref, local_sem.at[1])
    own_copy.start()
    near_copy.start()
    low_side = ext_ref.at[pl.ds(0, HALO)]
    high_side = ext_ref.at[pl.ds(rows + HALO, HALO)]

    @pl.when(part_rank == 0)
    def _():
        pltpu.make_async_copy(tokens_ref.at[pl.ds(rows, HALO)], high_side, local_sem.at[2]).start()

    @pl.when(part_rank == 1)
    def _():
        pltpu.make_async_copy(
            tokens_ref.at[pl.ds(rows - HALO, HALO)], low_side, local_sem.at[2]
        ).start()

    @pl.when(me == 0)
    def _():
        ext_ref[0:HALO, :] = jnp.zeros((HALO, width), BF16)

    @pl.when(me == count - 1)
    def _():
        ext_ref[rows + HALO :, :] = jnp.zeros((HALO, width), BF16)

    pieces = []
    low = 0
    for j in range(3):
        pieces.append((qkv_ref.at[j], low, part))
        low += part
    for ref in (proj_ref, fc1_ref, fc2_ref):
        pieces.append((ref, low, ref.shape[0]))
        low += ref.shape[0]
    other_core = (row_rank, 1 - part_rank)

    def own_weight(i):
        ref, at, size = pieces[i]
        return pltpu.make_async_copy(
            ref, stack_ref.at[part_rank, pl.ds(at, size)], weight_sem.at[0, i]
        )

    def sent_weight(i):
        ref, at, size = pieces[i]
        return swap_copy(
            ref, stack_ref.at[part_rank, pl.ds(at, size)], weight_sem.at[1, i],
            weight_sem.at[2, i], other_core,
        )

    for i in range(len(pieces)):
        own_weight(i).start()

    def side_up():
        return swap_copy(
            tokens_ref.at[pl.ds(rows_here - HALO, HALO)], low_side, side_sem.at[0], side_sem.at[1],
            (jnp.minimum(row_rank + 1, row_count - 1), part_rank),
        )

    def side_down():
        return swap_copy(
            tokens_ref.at[pl.ds(0, HALO)], high_side, side_sem.at[0], side_sem.at[1],
            (jnp.maximum(row_rank - 1, 0), part_rank),
        )

    stat_ref[...] = jnp.zeros_like(stat_ref)
    near_copy.wait()
    own_copy.wait()

    ends = []
    reached = 0
    for s in range(scenes):
        reached = reached + lengths_ref[s]
        ends.append(reached * WIN)

    blocks = rows // block
    span = block + 2 * HALO

    def step(it, carry):
        @pl.when(it == 2)
        def _():
            await_all(count)

            @pl.when((part_rank == 0) & (row_rank < row_count - 1))
            def _():
                side_up().start()

            @pl.when((part_rank == 1) & (row_rank > 0))
            def _():
                side_down().start()

            for i in range(len(pieces)):
                sent_weight(i).start()

        @pl.when(it == blocks - 2)
        def _():
            pltpu.make_async_copy(
                tokens_ref.at[pl.ds(0, HALO)], low_side, local_sem.at[2]
            ).wait()

            @pl.when((part_rank == 0) & (row_rank < row_count - 1))
            def _():
                side_up().wait_send()

            @pl.when((part_rank == 0) & (row_rank > 0))
            def _():
                side_up().wait_recv()

            @pl.when((part_rank == 1) & (row_rank > 0))
            def _():
                side_down().wait_send()

            @pl.when((part_rank == 1) & (row_rank < row_count - 1))
            def _():
                side_down().wait_recv()

        b = lax.rem(it + 1, blocks)
        base = pl.multiple_of(b * block, block)
        window = ext_ref[pl.ds(base, span), :]
        near = place_ref[pl.ds(base, block), :]
        own_row = row_rank * rows_here + first + base + lax.broadcasted_iota(
            jnp.int32, (block, 1), 0
        )
        scene_low = jnp.zeros_like(own_row)
        scene_high = jnp.full_like(own_row, node_total)
        for end in reversed(ends):
            passed = own_row >= end
            scene_low = jnp.maximum(scene_low, jnp.where(passed, end, 0))
            scene_high = jnp.minimum(scene_high, jnp.where(passed, node_total, end))
        target = own_row + near
        usable = (near >= -HALO) & (target >= scene_low) & (target < scene_high)
        near = jnp.where(usable, near, -8 * HALO)
        padded = jnp.concatenate(
            [near, jnp.zeros((block, LANES - TAPS), jnp.int32)], axis=1
        )
        near_t_ref[:, pl.ds(base, block)] = jnp.transpose(padded)[: near_t_ref.shape[0]]
        place = lax.broadcasted_iota(jnp.int32, (block, TAPS), 0) + near + HALO
        column = lax.broadcasted_iota(jnp.int32, (block, span), 1)
        total = jnp.zeros((block, width), F32)
        group = 3
        for k0 in range(0, TAPS, group):
            hot = jnp.concatenate(
                [
                    (place[:, k : k + 1] == column).astype(F32).astype(BF16)
                    for k in range(k0, k0 + group)
                ],
                axis=0,
            )
            picked = dot_plain(hot, window)
            for j in range(group):
                total += picked[j * block : (j + 1) * block] * taps_ref[k0 + j : k0 + j + 1, :]
        filt_ref[pl.ds(base, block), :] = total
        stat_ref[0:1, :] += col_sum(total)
        stat_ref[1:2, :] += col_sum(total * total)
        return carry

    lax.fori_loop(0, blocks, step, 0)

    to_tile(tile, [stat_ref[0:1], stat_ref[1:2]])
    send_to_all(lambda other: tile, landed, send_sem, recv_sem, count, parts, me)
    for i in range(len(pieces)):
        own_weight(i).wait()
        sent_weight(i).wait()
    await_from_all(tile, landed, send_sem, recv_sem, count, parts, me)
    total = add_landed(tile[...], landed, count)
    groups = width // LANES
    stat_ref[0:1, :] = from_tile(total, 0, groups)
    stat_ref[1:2, :] = from_tile(total, 1, groups)


def filter_forward(lengths, tokens, near, params, qkv, proj, fc1, fc2, row_count, parts, block=128):
    rows_here, width = tokens.shape
    rows = rows_here // parts
    stack_rows = qkv.shape[0] * qkv.shape[1] + proj.shape[0] + fc1.shape[0] + fc2.shape[0]
    count = row_count * parts
    anywhere = pl.BlockSpec(memory_space=pl.ANY)
    vmem = pl.BlockSpec(memory_space=pltpu.VMEM)
    return pl.pallas_call(
        functools.partial(
            filter_kernel, block=block, row_count=row_count, parts=parts, scenes=lengths.shape[0]
        ),
        in_specs=[pl.BlockSpec(memory_space=pltpu.SMEM), anywhere, anywhere, vmem] + [anywhere] * 4,
        out_specs=[vmem, vmem, vmem, vmem, anywhere],
        out_shape=[
            jax.ShapeDtypeStruct((rows, width), F32),
            jax.ShapeDtypeStruct((8, width), F32),
            jax.ShapeDtypeStruct((32, rows), jnp.int32),
            jax.ShapeDtypeStruct((rows + 2 * HALO, width), BF16),
            jax.ShapeDtypeStruct((parts, stack_rows, width), BF16),
        ],
        scratch_shapes=[
            pltpu.VMEM((rows, TAPS), jnp.int32),
            pltpu.VMEM((8, LANES), F32),
            pltpu.VMEM((count, 8, LANES), F32),
            pltpu.SemaphoreType.DMA((3,)),
            pltpu.SemaphoreType.DMA((2,)),
            pltpu.SemaphoreType.DMA((3, 6)),
            pltpu.SemaphoreType.DMA((count,)),
            pltpu.SemaphoreType.DMA((count,)),
        ],
        compiler_params=pltpu.CompilerParams(
            collective_id=0, has_side_effects=True, vmem_limit_bytes=40 << 20
        ),
    )(lengths, tokens, near, params, qkv, proj, fc1, fc2)


def streams_of(cap, pieces):
    halves = []
    middle = (cap + 1) // 2
    for order, low, high in ((0, 0, middle), (1, middle, cap)):
        cuts = min(pieces, high - low)
        edges = [low + (high - low) * i // cuts for i in range(cuts + 1)] if cuts else []
        halves.append([(order, a, b - a) for a, b in zip(edges[:-1], edges[1:])])
    return [s for pair in zip(*halves) for s in pair] + halves[0][len(halves[1]) :]


def bits_of(row_count, order):
    bits = list(range(row_count.bit_length() - 1))
    if order and len(bits) > 1:
        bits[0], bits[1] = bits[1], bits[0]
    return bits


def flip(rank, bit):
    weight = 1 << bit
    return rank + weight - 2 * weight * lax.rem(rank // weight, 2)


def filter_back_kernel(
    slot_ref, ext_ref, filt_ref, dres_ref, near_t_ref, params_ref, stat_ref, small_ref, bias_ref,
    own_ref, peer_ref,
    back_ref, small_out_ref, tile_out_ref, *scratch,
    block, row_count, parts, cap, streams, node_total
):
    wide = len(streams)
    sums, staged, arrived = scratch[:wide], scratch[wide : 2 * wide], scratch[2 * wide : 3 * wide]
    (
        total_ref, grad_ref, rim_ref, rim_in, pair_in, tile, landed, flat, flat_in, part_sum,
        flat_all, pair_sem, sum_send, sum_recv, tree_send, tree_recv, rim_sem, flat_send, flat_recv,
        all_send, all_recv, out_sem,
    ) = scratch[3 * wide :]
    row_rank = lax.axis_index("rows")
    part_rank = lax.axis_index("heads")
    count = row_count * parts
    me = row_rank * parts + part_rank
    rows, width = filt_ref.shape
    groups = width // LANES
    first = part_rank * rows
    depth = row_count.bit_length() - 1
    other_core = (row_rank, 1 - part_rank)
    small_rows = params_ref.shape[0]
    bias_rows = bias_ref.shape[1] // width

    greet_all(count, parts, me)
    to_tile(tile, [small_ref[27:28], small_ref[28:29]])
    total_ref[...] = jnp.zeros_like(total_ref)
    small_out_ref[...] = jnp.zeros_like(small_out_ref)
    await_all(count)
    send_to_all(lambda other: tile, landed, sum_send, sum_recv, count, parts, me)
    pair_copy = swap_copy(peer_ref, pair_in, pair_sem.at[0], pair_sem.at[1], other_core)
    pair_copy.start()

    keep_at = {}
    for i, (order, _, size) in enumerate(streams):
        keep_at[i, 0] = 0
        for t, bit in enumerate(bits_of(row_count, order)):
            half = (row_count >> (t + 1)) * size
            keep_at[i, t + 1] = keep_at[i, t] + lax.rem(row_rank // (1 << bit), 2) * half

    def pack(i):
        order, low, size = streams[i]
        bits = bits_of(row_count, order)

        def body(p, carry):
            owner = 0
            for t, bit in enumerate(bits):
                owner = owner + lax.rem(p // (1 << (depth - 1 - t)), 2) * (1 << bit)
            for c in range(size):
                tile_id = slot_ref[owner * cap + low + c]
                at = jnp.maximum(tile_id, 0)
                value = own_ref[at] + pair_in[at].astype(F32)
                sums[i][p * size + c] = jnp.where(tile_id >= 0, value, 0.0)
            return carry

        lax.fori_loop(0, row_count, body, 0)

    def tree_copy(i, t):
        order, _, size = streams[i]
        half = (row_count >> (t + 1)) * size
        at = (row_count - (row_count >> t)) * size
        return swap_copy(
            staged[i].at[pl.ds(at, half)], arrived[i].at[pl.ds(at, half)], tree_send.at[i, t],
            tree_recv.at[i, t], (flip(row_rank, bits_of(row_count, order)[t]), part_rank),
        )

    def tree_start(i, t):
        order, _, size = streams[i]
        half = row_count >> (t + 1)
        at = (row_count - (row_count >> t)) * size
        give = keep_at[i, t] * 2 + half * size - keep_at[i, t + 1]

        def body(p, carry):
            for c in range(size):
                staged[i][at + p * size + c] = sums[i][give + p * size + c].astype(BF16)
            return carry

        lax.fori_loop(0, half, body, 0)
        tree_copy(i, t).start()

    def tree_end(i, t):
        _, _, size = streams[i]
        half = row_count >> (t + 1)
        at = (row_count - (row_count >> t)) * size
        tree_copy(i, t).wait()

        def body(p, carry):
            for c in range(size):
                k = keep_at[i, t + 1] + p * size + c
                sums[i][k] = sums[i][k] + arrived[i][at + p * size + c].astype(F32)
            return carry

        lax.fori_loop(0, half, body, 0)

    def tree_step(i, t):
        tree_end(i, t)
        if t + 1 < depth:
            tree_start(i, t + 1)

    pair_copy.wait()
    for i in range(wide):
        pack(i)
        tree_start(i, 0)

    await_from_all(tile, landed, sum_send, sum_recv, count, parts, me)
    back = add_landed(tile[...], landed, count)
    gain_mean = from_tile(back, 0, groups) * (1.0 / node_total)
    shift_mean = from_tile(back, 1, groups) * (1.0 / node_total)
    centre = stat_ref[0:1] / node_total
    inv_std = lax.rsqrt(stat_ref[1:2] / node_total - centre * centre + norm_eps)
    factor = params_ref[27:28] * inv_std
    grad_ref[...] = (
        factor * (dres_ref[...] - shift_mean - (filt_ref[...] - centre) * inv_std * gain_mean)
    ).astype(BF16)

    blocks = rows // block
    span = block + 2 * HALO
    has_before = me > 0
    has_after = me < count - 1

    def rim_low():
        return swap_copy(
            rim_ref.at[0], rim_in.at[1], rim_sem.at[0, 0], rim_sem.at[1, 1],
            device_of(jnp.maximum(me - 1, 0), parts),
        )

    def rim_high():
        return swap_copy(
            rim_ref.at[1], rim_in.at[0], rim_sem.at[0, 1], rim_sem.at[1, 0],
            device_of(jnp.minimum(me + 1, count - 1), parts),
        )

    def finish_rows(low, size):
        back_ref[pl.ds(first + low, size), :] = total_ref[HALO + low : HALO + low + size].astype(BF16)

    late = rows - 384

    def out_copy(i):
        low, size = ((late, rows - late), (0, late))[i]
        here = back_ref.at[pl.ds(first + low, size)]
        return swap_copy(here, here, out_sem.at[0, i], out_sem.at[1, i], other_core)

    schedule = [[] for _ in range(blocks)]
    for i in range(wide):
        for t in range(depth):
            schedule[min(i // 2 + t, blocks - 1)].append((t, i))

    def step(it, carry):
        b = lax.rem(it * (blocks - 1), blocks)
        base = pl.multiple_of(b * block, block)
        window = pl.ds(base, span)
        place = lax.broadcasted_iota(jnp.int32, (TAPS, block), 1) + HALO + (
            near_t_ref[:, pl.ds(base, block)][:TAPS]
        )
        row = lax.broadcasted_iota(jnp.int32, (span, block), 0)
        tokens = ext_ref[window, :].astype(F32)
        grad = grad_ref[pl.ds(base, block), :]
        total = jnp.zeros((span, width), F32)
        for k in range(TAPS):
            hot = (place[k : k + 1, :] == row).astype(F32).astype(BF16)
            spread = dot_plain(hot, grad)
            total += spread * params_ref[k : k + 1, :]
            small_out_ref[k : k + 1, :] += col_sum(spread * tokens)
        total_ref[window, :] += total

        @pl.when(it == 1)
        def _():
            rim_ref[0] = total_ref[0:HALO].astype(BF16)
            rim_ref[1] = total_ref[rows + HALO : rows + 2 * HALO].astype(BF16)

            @pl.when(has_before)
            def _():
                rim_low().start()

            @pl.when(has_after)
            def _():
                rim_high().start()

        @pl.when(it == 2)
        def _():
            @pl.when(has_before)
            def _():
                rim_low().wait_send()
                rim_high().wait_recv()
                total_ref[HALO : 2 * HALO] += rim_in[0].astype(F32)

            @pl.when(has_after)
            def _():
                rim_high().wait_send()
                rim_low().wait_recv()
                total_ref[rows : rows + HALO] += rim_in[1].astype(F32)

            finish_rows(late, rows - late)
            out_copy(0).start()

        for s in range(blocks - 1):

            @pl.when(it == s)
            def _(s=s):
                for t, i in sorted(schedule[s]):
                    tree_step(i, t)

        return carry

    lax.fori_loop(0, blocks, step, 0)

    flat[...] = jnp.zeros_like(flat)
    for r in range(small_rows):
        if r < TAPS:
            row = small_out_ref[r : r + 1, :]
        elif r < small_rows - bias_rows:
            row = small_ref[r : r + 1, :]
        else:
            at = (r - small_rows + bias_rows) * width
            row = bias_ref[0:1, at : at + width]
        for g in range(groups):
            at = r * groups + g
            flat[at // 8, at % 8 : at % 8 + 1, :] = row[:, g * LANES : (g + 1) * LANES]
    send_to_all(lambda other: flat.at[other], flat_in, flat_send, flat_recv, count, parts, me)
    finish_rows(0, late)
    out_copy(1).start()
    await_from_all(flat.at[0], flat_in, flat_send, flat_recv, count, parts, me)
    part_sum[...] = add_landed(flat[me], flat_in, count)
    send_to_all(lambda other: part_sum, flat_all, all_send, all_recv, count, parts, me)
    for t, i in sorted(schedule[blocks - 1]):
        tree_step(i, t)
    for i, (_, low, size) in enumerate(streams):
        for c in range(size):
            tile_out_ref[low + c] = sums[i][keep_at[i, depth] + c]
    await_from_all(part_sum, flat_all, all_send, all_recv, count, parts, me)
    flat_all[0] = part_sum[...]
    for r in range(small_rows):
        for g in range(groups):
            at = r * groups + g
            tile_at = lax.rem(at // 8 - me + count, count)
            small_out_ref[r : r + 1, g * LANES : (g + 1) * LANES] = flat_all[
                tile_at, at % 8 : at % 8 + 1, :
            ]
    out_copy(0).wait()
    out_copy(1).wait()


def filter_backward(
    slots, extended, filtered, dres, near_t, params, stat, small, bias, own_grad, peer_grad, cap,
    row_count, parts, block=256, pieces=3
):
    rows, width = filtered.shape
    count = row_count * parts
    depth = row_count.bit_length() - 1
    streams = streams_of(cap, pieces)
    wide = len(streams)
    vmem = pl.BlockSpec(memory_space=pltpu.VMEM)
    by_owner = [row_count * size for _, _, size in streams]
    dma = pltpu.SemaphoreType.DMA
    return pl.pallas_call(
        functools.partial(
            filter_back_kernel, block=block, row_count=row_count, parts=parts, cap=cap,
            streams=streams, node_total=rows * count,
        ),
        in_specs=[pl.BlockSpec(memory_space=pltpu.SMEM)] + [vmem] * 10,
        out_specs=[vmem] * 3,
        out_shape=[
            jax.ShapeDtypeStruct((rows * parts, width), BF16),
            jax.ShapeDtypeStruct(params.shape, F32),
            jax.ShapeDtypeStruct((cap, BR, width), F32),
        ],
        scratch_shapes=[pltpu.VMEM((n, BR, width), F32) for n in by_owner]
        + [pltpu.VMEM((n, BR, width), BF16) for n in by_owner] * 2
        + [
            pltpu.VMEM((rows + 2 * HALO, width), F32),
            pltpu.VMEM((rows, width), BF16),
            pltpu.VMEM((2, HALO, width), BF16),
            pltpu.VMEM((2, HALO, width), BF16),
            pltpu.VMEM(peer_grad.shape, BF16),
            pltpu.VMEM((8, LANES), F32),
            pltpu.VMEM((count, 8, LANES), F32),
            pltpu.VMEM((count, 8, LANES), F32),
            pltpu.VMEM((count, 8, LANES), F32),
            pltpu.VMEM((8, LANES), F32),
            pltpu.VMEM((count, 8, LANES), F32),
            dma((2,)),
            dma((count,)),
            dma((count,)),
            dma((wide, depth)),
            dma((wide, depth)),
            dma((2, 2)),
            dma((count,)),
            dma((count,)),
            dma((count,)),
            dma((count,)),
            dma((2, 2)),
        ],
        compiler_params=pltpu.CompilerParams(
            collective_id=1, has_side_effects=True, vmem_limit_bytes=58 << 20
        ),
    )(slots, extended, filtered, dres, near_t, params, stat, small, bias, own_grad, peer_grad)


def block_kernel(
    filt_ref, tok_ref, mask_ref, cot_ref, stat_ref, params_ref, bias_ref, weight_ref,
    out_ref, dres_ref, own_ref, peer_ref, small_ref, bias_grad_ref, grad_ref, *, node_total, parts, width, units, block
):
    i = pl.program_id(0)

    @pl.when(i == 0)
    def _():
        grad_ref[...] = jnp.zeros_like(grad_ref)
        small_ref[...] = jnp.zeros_like(small_ref)
        bias_grad_ref[...] = jnp.zeros_like(bias_grad_ref)

    part = width // parts
    unit_part = units // parts
    scale = HEAD_DIM**-0.5

    def weight_rows(low, count):
        return jnp.concatenate([weight_ref[h, low : low + count] for h in range(parts)], axis=0)

    def qkv_rows(j):
        return weight_rows(j * part, part)

    def proj_rows():
        return weight_rows(3 * part, part)

    def add_grad(low, value):
        for h in range(parts):
            grad_ref[h, low : low + part] += value[h * part : (h + 1) * part]

    def param(row):
        return params_ref[row : row + 1, :]

    def add_small(row, value):
        small_ref[row : row + 1, :] += value

    centre = stat_ref[0:1] / node_total
    inv_std = lax.rsqrt(stat_ref[1:2] / node_total - centre * centre + norm_eps)
    bn_norm = (filt_ref[...] - centre) * inv_std
    resid = tok_ref[...].astype(F32) + (bn_norm * param(27) + param(28))
    unit_one, factor_one = layer_norm(resid)
    normed_one = (unit_one * param(29) + param(30)).astype(BF16)
    query = ((dot_last(normed_one, qkv_rows(0)) + param(35)) * scale).astype(BF16)
    key = (dot_last(normed_one, qkv_rows(1)) * scale).astype(BF16)
    value = ((dot_last(normed_one, qkv_rows(2)) + param(36)) * scale).astype(BF16)

    side = LANES
    heads = LANES // HEAD_DIM
    groups = width // LANES
    lane_head = lax.broadcasted_iota(jnp.int32, (side, LANES), 1) // HEAD_DIM
    window_q = lax.broadcasted_iota(jnp.int32, (side, side), 0) // WIN
    window_k = lax.broadcasted_iota(jnp.int32, (side, side), 1) // WIN

    def stack_heads(a):
        return jnp.concatenate(
            [jnp.where(lane_head == j, a, jnp.zeros_like(a)) for j in range(heads)], axis=0
        )

    def pick_heads(a):
        picked = a[:side]
        for j in range(1, heads):
            picked = jnp.where(lane_head == j, a[j * side : (j + 1) * side], picked)
        return picked

    def cut(a, s, g):
        return a[s * side : (s + 1) * side, g * LANES : (g + 1) * LANES]

    kept = {}
    mixture = []
    for s in range(block // side):
        keep = (window_q == window_k) & (mask_ref[0:1, s * side : (s + 1) * side] > 0)
        mixed = []
        for g in range(groups):
            query_g = cut(query, s, g)
            keys = stack_heads(cut(key, s, g))
            values = stack_heads(cut(value, s, g))
            scores = dot_last(query_g, keys)
            probs = []
            for j in range(heads):
                score = jnp.where(keep, scores[:, j * side : (j + 1) * side], masked_score)
                power = jnp.exp(score - jnp.max(score, axis=1, keepdims=True))
                probs.append(power / jnp.sum(power, axis=1, keepdims=True))
            probs = jnp.concatenate(probs, axis=1)
            probs_low = probs.astype(BF16)
            mixed.append(dot_plain(probs_low, values))
            kept[s, g] = (query_g, keys, values, probs, probs_low)
        mixture.append(jnp.concatenate(mixed, axis=1))
    mixture = jnp.concatenate(mixture, axis=0).astype(BF16)
    after = resid + (dot_plain(mixture, proj_rows()) + param(33))
    unit_two, factor_two = layer_norm(after)
    normed_two = (unit_two * param(31) + param(32)).astype(BF16)

    cotangent = cot_ref[...]
    grad_ffn = cotangent.astype(BF16)
    ffn = jnp.zeros_like(after)
    grad_normed_two = jnp.zeros_like(after)
    chunk = unit_part // 2
    for h in range(parts):
        for c in range(2):
            low = 4 * part + c * chunk
            unit = h * unit_part + c * chunk
            fc1 = weight_ref[h, low : low + chunk]
            fc2 = weight_ref[h, low + unit_part : low + unit_part + chunk]
            hidden = dot_last(normed_two, fc1) + bias_ref[0:1, unit : unit + chunk]
            cumulative = 0.5 * (1.0 + lax.erf(hidden * 0.5**0.5))
            activation = (hidden * cumulative).astype(BF16)
            density = jnp.exp(-0.5 * hidden * hidden) * (2.0 * jnp.pi) ** (-0.5)
            ffn += dot_plain(activation, fc2)
            grad_hidden = (
                dot_last(grad_ffn, fc2) * (cumulative + hidden * density)
            ).astype(BF16)
            grad_normed_two += dot_plain(grad_hidden, fc1)
            grad_ref[h, low : low + chunk] += dot_first(grad_hidden, normed_two)
            grad_ref[h, low + unit_part : low + unit_part + chunk] += dot_first(activation, grad_ffn)
            bias_grad_ref[0:1, unit : unit + chunk] += col_sum(grad_hidden.astype(F32))
    out_ref[...] = after + (ffn + param(34))
    add_small(34, col_sum(grad_ffn.astype(F32)))

    grad_after = cotangent + norm_back(grad_normed_two, unit_two, factor_two, param(31))
    add_small(31, col_sum(grad_normed_two * unit_two))
    add_small(32, col_sum(grad_normed_two))
    grad_branch = grad_after.astype(BF16)
    add_grad(3 * part, dot_first(mixture, grad_branch))
    add_small(33, col_sum(grad_branch.astype(F32)))
    grad_mixture = dot_last(grad_branch, proj_rows()).astype(BF16)

    grads = ([], [], [])
    for s in range(block // side):
        here = ([], [], [])
        for g in range(groups):
            query_g, keys, values, probs, probs_low = kept[s, g]
            grad_mix = cut(grad_mixture, s, g)
            grad_probs = dot_last(grad_mix, values)
            grad_scores = []
            for j in range(heads):
                prob = probs[:, j * side : (j + 1) * side]
                term = prob * grad_probs[:, j * side : (j + 1) * side]
                grad_scores.append(
                    (term - prob * jnp.sum(term, axis=1, keepdims=True)).astype(BF16)
                )
            grad_scores = jnp.concatenate(grad_scores, axis=1)
            here[0].append(dot_plain(grad_scores, keys))
            here[1].append(pick_heads(dot_first(grad_scores, query_g)))
            here[2].append(pick_heads(dot_first(probs_low, grad_mix)))
        for kind in range(3):
            grads[kind].append(jnp.concatenate(here[kind], axis=1))
    grad_qkv = [jnp.concatenate(kind, axis=0).astype(BF16) for kind in grads]
    grad_normed_one = jnp.zeros_like(resid)
    for j in range(3):
        grad_normed_one += dot_plain(grad_qkv[j], qkv_rows(j))
        add_grad(j * part, scale * dot_first(grad_qkv[j], normed_one))
    grad_normed_one = scale * grad_normed_one
    add_small(35, scale * col_sum(grad_qkv[0].astype(F32)))
    add_small(36, scale * col_sum(grad_qkv[2].astype(F32)))
    dres = grad_after + norm_back(grad_normed_one, unit_one, factor_one, param(29))
    add_small(29, col_sum(grad_normed_one * unit_one))
    add_small(30, col_sum(grad_normed_one))
    add_small(27, col_sum(dres * bn_norm))
    add_small(28, col_sum(dres))
    dres_ref[...] = dres

    @pl.when(i == pl.num_programs(0) - 1)
    def _():
        mine = lax.axis_index("heads")
        own_ref[...] = grad_ref[mine]
        peer_ref[...] = grad_ref[1 - mine].astype(BF16)


def block_step(filtered, tokens, mask, cotangent, stat, params, bias, weights, node_total, block=256):
    rows, width = filtered.shape
    parts, units = weights.shape[0], bias.shape[1]
    outs = [
        jax.ShapeDtypeStruct((rows, width), F32),
        jax.ShapeDtypeStruct((rows, width), F32),
        jax.ShapeDtypeStruct(weights.shape[1:], F32),
        jax.ShapeDtypeStruct(weights.shape[1:], BF16),
        jax.ShapeDtypeStruct(params.shape, F32),
        jax.ShapeDtypeStruct(bias.shape, F32),
    ]
    by_rows = pl.BlockSpec((block, width), lambda i: (i, 0))
    return pl.pallas_call(
        functools.partial(
            block_kernel, node_total=node_total, parts=parts, width=width, units=units, block=block
        ),
        grid=(rows // block,),
        in_specs=[
            by_rows,
            by_rows,
            pl.BlockSpec((1, block), lambda i: (0, i)),
            by_rows,
            full_spec(stat.shape),
            full_spec(params.shape),
            full_spec(bias.shape),
            full_spec(weights.shape),
        ],
        out_specs=[by_rows, by_rows] + [full_spec(o.shape) for o in outs[2:]],
        out_shape=outs,
        scratch_shapes=[pltpu.VMEM(weights.shape, F32)],
        compiler_params=pltpu.CompilerParams(vmem_limit_bytes=58 << 20),
    )(filtered, tokens, mask, cotangent, stat, params, bias, weights)


def local(
    tokens_in, neighbours, scene_lengths, window_mask, small_params, qkv_weight, proj_weight,
    fc1_weight, fc2_weight, cotangent, owners, small_first, small_second, tile_first, tile_second
):
    rows_here, width = tokens_in.shape
    row_count = lax.axis_size("rows")
    parts = lax.axis_size("heads")
    row_rank = lax.axis_index("rows")
    part_rank = lax.axis_index("heads")
    rows = rows_here // parts
    node_total = rows_here * row_count
    first = part_rank * rows
    tile_count = owners.shape[0]
    slot_cap = tile_first.shape[1]

    def own(a):
        return lax.dynamic_slice_in_dim(a, first, rows, 0)

    filtered, stat, near_t, extended, weights = filter_forward(
        scene_lengths, tokens_in, neighbours, small_params, qkv_weight, proj_weight, fc1_weight,
        fc2_weight, row_count, parts
    )
    bias = small_params[37:].reshape(1, -1)
    output, dres, own_grad, peer_grad, small_grad, bias_grad = block_step(
        filtered, own(tokens_in), own(window_mask)[None], own(cotangent), stat, small_params, bias,
        weights, node_total
    )
    output = lax.all_gather(output, "heads", axis=0, tiled=True)
    dres_all = lax.all_gather(dres, "heads", axis=0, tiled=True)

    tile_order = jnp.arange(tile_count, dtype=jnp.int32)
    same_owner = (owners[:, None] == owners[None, :]) & (tile_order[None, :] < tile_order[:, None])
    slot_of = owners * slot_cap + jnp.sum(same_owner.astype(jnp.int32), axis=1)
    slot_ids = jnp.arange(row_count * slot_cap, dtype=jnp.int32)
    found = slot_of[None, :] == slot_ids[:, None]
    slot_tile = jnp.max(jnp.where(found, tile_order[None, :], -1), axis=1)

    conv_back, small_sum, tile_grad = filter_backward(
        slot_tile, extended, filtered, dres, near_t, small_params, stat, small_grad, bias_grad,
        own_grad.reshape(tile_count, BR, width), peer_grad.reshape(tile_count, BR, width), slot_cap,
        row_count, parts
    )
    input_grad = dres_all + conv_back.astype(F32)
    small_new, small_first_new, small_second_new = adam_step(
        small_params, small_sum, small_first, small_second, 0.0
    )
    own_slots = lax.dynamic_slice_in_dim(slot_tile, row_rank * slot_cap, slot_cap)
    live = (own_slots >= 0).astype(F32)[:, None, None]
    weight_tiles = lax.dynamic_index_in_dim(weights, part_rank, 0, keepdims=False)
    tile_old = jnp.take(
        weight_tiles.reshape(tile_count, BR, width), jnp.maximum(own_slots, 0), axis=0
    ).astype(F32)
    new_weight, new_first, new_second = adam_step(
        tile_old, tile_grad, tile_first[0], tile_second[0], decay_rate
    )
    new_weight = new_weight * live
    new_first = new_first * live
    new_second = new_second * live
    return (
        output,
        input_grad,
        new_weight[None],
        new_first[None],
        new_second[None],
        new_weight.astype(BF16)[None],
        small_new,
        small_first_new,
        small_second_new,
    )


def solution(mesh):
    return jax.shard_map(
        local,
        mesh=mesh,
        in_specs=(
            P("rows", None),
            P("rows", None),
            P(),
            P("rows"),
            P(),
            P(None, "heads", None),
            P("heads", None),
            P("heads", None),
            P("heads", None),
            P("rows", None),
            P(),
            P(),
            P(),
            P("heads", "rows", None, None),
            P("heads", "rows", None, None),
        ),
        out_specs=(
            P("rows", None),
            P("rows", None),
            P("heads", "rows", None, None),
            P("heads", "rows", None, None),
            P("heads", "rows", None, None),
            P("heads", "rows", None, None),
            P(),
            P(),
            P(),
        ),
        check_vma=False,
    )
```

```python
import functools

import jax
import jax.numpy as jnp
from jax import lax
from jax.experimental import pallas as pl
from jax.experimental.pallas import tpu as pltpu
from jax.sharding import PartitionSpec as P

HEAD_DIM = 32
WIN = 32
HALO = 128
BR = 16
STEP = 3
TAPS = 27
LANES = 128

norm_eps = 1e-05
adam_rate = 0.05
beta_one = 0.5
beta_two = 0.5
adam_eps = 1e-08
decay_rate = 0.05
masked_score = -1e30

F32 = jnp.float32
BF16 = jnp.bfloat16


def adam_step(weight, gradient, first_moment, second_moment, decay_factor):
    first_new = beta_one * first_moment + (1.0 - beta_one) * gradient
    second_new = beta_two * second_moment + (1.0 - beta_two) * gradient * gradient
    first_hat = first_new / (1.0 - beta_one**STEP)
    second_hat = second_new / (1.0 - beta_two**STEP)
    weight_new = weight - adam_rate * (
        first_hat / (jnp.sqrt(second_hat) + adam_eps) + decay_factor * weight
    )
    return (weight_new, first_new, second_new)


def dot_plain(a, b):
    return jnp.dot(a, b, preferred_element_type=F32)


def dot_last(a, b):
    return lax.dot_general(a, b, (((1,), (1,)), ((), ())), preferred_element_type=F32)


def dot_first(a, b):
    return lax.dot_general(a, b, (((0,), (0,)), ((), ())), preferred_element_type=F32)


def col_sum(v):
    return jnp.sum(v, axis=0, keepdims=True)


def layer_norm(v):
    centre = v - jnp.mean(v, axis=1, keepdims=True)
    factor = lax.rsqrt(jnp.mean(centre * centre, axis=1, keepdims=True) + norm_eps)
    return centre * factor, factor


def norm_back(upstream, unit_part, factor, gain):
    scaled = upstream * gain
    return factor * (
        scaled
        - jnp.mean(scaled, axis=1, keepdims=True)
        - unit_part * jnp.mean(scaled * unit_part, axis=1, keepdims=True)
    )


def full_spec(shape):
    zeros = (0,) * len(shape)
    return pl.BlockSpec(shape, lambda i: zeros)


MESH = pl.DeviceIdType.MESH


def device_of(index, parts):
    return (index // parts, lax.rem(index, parts))


def greet_all(count, parts, me):
    barrier = pltpu.get_barrier_semaphore()

    def greet(j, carry):
        pl.semaphore_signal(
            barrier, inc=1, device_id=device_of(lax.rem(me + j, count), parts), device_id_type=MESH
        )
        return carry

    lax.fori_loop(1, count, greet, 0)


def await_all(count):
    pl.semaphore_wait(pltpu.get_barrier_semaphore(), count - 1)


def swap_copy(source, landing, send_sem, recv_sem, device):
    return pltpu.make_async_remote_copy(
        src_ref=source, dst_ref=landing, send_sem=send_sem, recv_sem=recv_sem,
        device_id=device, device_id_type=MESH,
    )


def send_to_all(source_of, landing, send_sem, recv_sem, count, parts, me):
    def send(j, carry):
        other = lax.rem(me + j, count)
        swap_copy(
            source_of(other), landing.at[count - j], send_sem.at[j], recv_sem.at[count - j],
            device_of(other, parts),
        ).start()
        return carry

    lax.fori_loop(1, count, send, 0)


def await_from_all(source, landing, send_sem, recv_sem, count, parts, me):
    def wait(j, carry):
        swap_copy(
            source, landing.at[count - j], send_sem.at[j], recv_sem.at[count - j],
            device_of(lax.rem(me + j, count), parts),
        ).wait()
        return carry

    lax.fori_loop(1, count, wait, 0)


def add_landed(own, landing, count):
    return lax.fori_loop(1, count, lambda j, total: total + landing[j], own)


def to_tile(tile_ref, rows):
    tile_ref[...] = jnp.zeros_like(tile_ref)
    groups = rows[0].shape[1] // LANES
    for r, row in enumerate(rows):
        for g in range(groups):
            at = r * groups + g
            tile_ref[at : at + 1, :] = row[:, g * LANES : (g + 1) * LANES]


def from_tile(tile, row, groups):
    at = row * groups
    return jnp.concatenate([tile[at + g : at + g + 1, :] for g in range(groups)], axis=1)


def filter_kernel(
    lengths_ref, tokens_ref, near_ref, taps_ref, qkv_ref, proj_ref, fc1_ref, fc2_ref,
    filt_ref, stat_ref, near_t_ref, ext_ref, stack_ref,
    near_in, tile, landed, local_sem, side_sem, weight_sem, send_sem, recv_sem,
    *, block, row_count, parts, scenes
):
    row_rank = lax.axis_index("rows")
    part_rank = lax.axis_index("heads")
    count = row_count * parts
    me = row_rank * parts + part_rank
    rows_here, width = tokens_ref.shape
    rows = rows_here // parts
    part = width // parts
    first = part_rank * rows
    node_total = rows_here * row_count
    greet_all(count, parts, me)

    own_copy = pltpu.make_async_copy(
        tokens_ref.at[pl.ds(first, rows)], ext_ref.at[pl.ds(HALO, rows)], local_sem.at[0]
    )
    near_copy = pltpu.make_async_copy(
        near_ref.at[:, pl.ds(pl.multiple_of(first, LANES), rows)], near_in, local_sem.at[1]
    )
    own_copy.start()
    near_copy.start()
    low_side = ext_ref.at[pl.ds(0, HALO)]
    high_side = ext_ref.at[pl.ds(rows + HALO, HALO)]

    @pl.when(part_rank == 0)
    def _():
        pltpu.make_async_copy(tokens_ref.at[pl.ds(rows, HALO)], high_side, local_sem.at[2]).start()

    @pl.when(part_rank == 1)
    def _():
        pltpu.make_async_copy(
            tokens_ref.at[pl.ds(rows - HALO, HALO)], low_side, local_sem.at[2]
        ).start()

    @pl.when(me == 0)
    def _():
        ext_ref[0:HALO, :] = jnp.zeros((HALO, width), BF16)

    @pl.when(me == count - 1)
    def _():
        ext_ref[rows + HALO :, :] = jnp.zeros((HALO, width), BF16)

    pieces = []
    low = 0
    for j in range(3):
        pieces.append((qkv_ref.at[j], low, part))
        low += part
    for ref in (proj_ref, fc1_ref, fc2_ref):
        pieces.append((ref, low, ref.shape[0]))
        low += ref.shape[0]
    other_core = (row_rank, 1 - part_rank)

    def own_weight(i):
        ref, at, size = pieces[i]
        return pltpu.make_async_copy(
            ref, stack_ref.at[part_rank, pl.ds(at, size)], weight_sem.at[0, i]
        )

    def sent_weight(i):
        ref, at, size = pieces[i]
        here = stack_ref.at[part_rank, pl.ds(at, size)]
        return swap_copy(here, here, weight_sem.at[1, i], weight_sem.at[2, i], other_core)

    for i in range(len(pieces)):
        own_weight(i).start()

    def side_up():
        return swap_copy(
            tokens_ref.at[pl.ds(rows_here - HALO, HALO)], low_side, side_sem.at[0], side_sem.at[1],
            (jnp.minimum(row_rank + 1, row_count - 1), part_rank),
        )

    def side_down():
        return swap_copy(
            tokens_ref.at[pl.ds(0, HALO)], high_side, side_sem.at[0], side_sem.at[1],
            (jnp.maximum(row_rank - 1, 0), part_rank),
        )

    stat_ref[...] = jnp.zeros_like(stat_ref)
    near_copy.wait()
    own_copy.wait()

    ends = []
    reached = 0
    for s in range(scenes):
        reached = reached + lengths_ref[s]
        ends.append(reached * WIN)

    blocks = rows // block
    span = block + 2 * HALO

    def step(it, carry):
        @pl.when(it == 2)
        def _():
            await_all(count)

            @pl.when((part_rank == 0) & (row_rank < row_count - 1))
            def _():
                side_up().start()

            @pl.when((part_rank == 1) & (row_rank > 0))
            def _():
                side_down().start()

            for i in range(len(pieces)):
                own_weight(i).wait()
                sent_weight(i).start()

        @pl.when(it == blocks - 2)
        def _():
            pltpu.make_async_copy(
                tokens_ref.at[pl.ds(0, HALO)], low_side, local_sem.at[2]
            ).wait()

            @pl.when((part_rank == 0) & (row_rank < row_count - 1))
            def _():
                side_up().wait_send()

            @pl.when((part_rank == 0) & (row_rank > 0))
            def _():
                side_up().wait_recv()

            @pl.when((part_rank == 1) & (row_rank > 0))
            def _():
                side_down().wait_send()

            @pl.when((part_rank == 1) & (row_rank < row_count - 1))
            def _():
                side_down().wait_recv()

        b = lax.rem(it + 1, blocks)
        base = pl.multiple_of(b * block, block)
        window = ext_ref[pl.ds(base, span), :]
        near = near_in[:, pl.ds(base, block)]
        lane = lax.broadcasted_iota(jnp.int32, (1, block), 1)
        own_row = row_rank * rows_here + first + base + lane
        scene_low = jnp.zeros_like(own_row)
        scene_high = jnp.full_like(own_row, node_total)
        for end in ends:
            passed = own_row >= end
            scene_low = jnp.maximum(scene_low, jnp.where(passed, end, 0))
            scene_high = jnp.minimum(scene_high, jnp.where(passed, node_total, end))
        target = own_row + near
        usable = (near >= -HALO) & (target >= scene_low) & (target < scene_high)
        place_t = jnp.where(usable, near + lane + HALO, -8 * HALO)
        near_t_ref[0:TAPS, pl.ds(base, block)] = place_t
        place = jnp.transpose(
            jnp.concatenate([place_t, jnp.zeros((LANES - TAPS, block), jnp.int32)], axis=0)
        )
        column = lax.broadcasted_iota(jnp.int32, (block, span), 1)
        total = jnp.zeros((block, width), F32)
        group = 3
        for k0 in range(0, TAPS, group):
            hot = jnp.concatenate(
                [
                    (place[:, k : k + 1] == column).astype(F32).astype(BF16)
                    for k in range(k0, k0 + group)
                ],
                axis=0,
            )
            picked = dot_plain(hot, window)
            for j in range(group):
                total += picked[j * block : (j + 1) * block] * taps_ref[k0 + j : k0 + j + 1, :]
        filt_ref[pl.ds(base, block), :] = total
        stat_ref[0:1, :] += col_sum(total)
        stat_ref[1:2, :] += col_sum(total * total)
        return carry

    lax.fori_loop(0, blocks, step, 0)

    to_tile(tile, [stat_ref[0:1], stat_ref[1:2]])
    send_to_all(lambda other: tile, landed, send_sem, recv_sem, count, parts, me)
    for i in range(len(pieces)):
        sent_weight(i).wait()
    await_from_all(tile, landed, send_sem, recv_sem, count, parts, me)
    total = add_landed(tile[...], landed, count)
    groups = width // LANES
    stat_ref[0:1, :] = from_tile(total, 0, groups)
    stat_ref[1:2, :] = from_tile(total, 1, groups)


def filter_forward(lengths, tokens, near, params, qkv, proj, fc1, fc2, row_count, parts, block=128):
    rows_here, width = tokens.shape
    rows = rows_here // parts
    stack_rows = qkv.shape[0] * qkv.shape[1] + proj.shape[0] + fc1.shape[0] + fc2.shape[0]
    count = row_count * parts
    anywhere = pl.BlockSpec(memory_space=pl.ANY)
    vmem = pl.BlockSpec(memory_space=pltpu.VMEM)
    return pl.pallas_call(
        functools.partial(
            filter_kernel, block=block, row_count=row_count, parts=parts, scenes=lengths.shape[0]
        ),
        in_specs=[pl.BlockSpec(memory_space=pltpu.SMEM), anywhere, anywhere, vmem] + [anywhere] * 4,
        out_specs=[vmem] * 5,
        out_shape=[
            jax.ShapeDtypeStruct((rows, width), F32),
            jax.ShapeDtypeStruct((8, width), F32),
            jax.ShapeDtypeStruct((32, rows), jnp.int32),
            jax.ShapeDtypeStruct((rows + 2 * HALO, width), BF16),
            jax.ShapeDtypeStruct((parts, stack_rows, width), BF16),
        ],
        scratch_shapes=[
            pltpu.VMEM((TAPS, rows), jnp.int32),
            pltpu.VMEM((8, LANES), F32),
            pltpu.VMEM((count, 8, LANES), F32),
            pltpu.SemaphoreType.DMA((3,)),
            pltpu.SemaphoreType.DMA((2,)),
            pltpu.SemaphoreType.DMA((3, 6)),
            pltpu.SemaphoreType.DMA((count,)),
            pltpu.SemaphoreType.DMA((count,)),
        ],
        compiler_params=pltpu.CompilerParams(
            collective_id=0, has_side_effects=True, vmem_limit_bytes=60 << 20
        ),
    )(lengths, tokens, near, params, qkv, proj, fc1, fc2)


def streams_of(cap, depth):
    third = cap // 7 if depth > 2 else 0
    counts = [(cap - 2 * third + 1) // 2, (cap - 2 * third) // 2, third, third]
    found = []
    slot = 0
    for order, count in enumerate(counts):
        for j in range(count):
            place = j if order < 2 else 2 * j + order - 2
            found.append((place, order, slot))
            slot += 1
    return [(order, slot, place) for place, order, slot in sorted(found)]


def bits_of(depth, order):
    bits = list(range(depth))
    if order == 1 and depth > 1:
        bits[:2] = [1, 0]
    if order == 2:
        bits[:3] = [2, 0, 1]
    if order == 3:
        bits[:3] = [2, 1, 0]
    return bits


def flip(rank, bit):
    weight = 1 << bit
    return rank + weight - 2 * weight * lax.rem(rank // weight, 2)


def filter_back_kernel(
    slot_ref, ext_hbm, filt_hbm, dres_hbm, near_ref, params_ref, stat_ref, small_ref, own_hbm,
    peer_hbm, output_hbm,
    input_grad_ref, output_in, small_out_ref, tile_out_ref,
    ext_ref, filt_ref, dres_ref, own_ref, peer_ref, output_ref, pair_out, pair_in, sums, staged, arrived,
    total_ref, grad_ref, rim_ref, rim_in, tile, landed, flat, flat_in, part_sum, flat_all,
    local_sem, output_sem, pair_send, pair_recv, sum_send, sum_recv, tree_send, tree_recv, rim_sem,
    flat_send, flat_recv, all_send, all_recv, out_sem,
    *, block, row_count, parts, cap, node_total
):
    row_rank = lax.axis_index("rows")
    part_rank = lax.axis_index("heads")
    count = row_count * parts
    me = row_rank * parts + part_rank
    rows, width = filt_ref.shape
    groups = width // LANES
    first = part_rank * rows
    depth = row_count.bit_length() - 1
    streams = streams_of(cap, depth)
    wide = len(streams)
    other_core = (row_rank, 1 - part_rank)
    small_rows = params_ref.shape[0]

    loads = [
        pltpu.make_async_copy(source, landing, local_sem.at[i])
        for i, (source, landing) in enumerate(
            (
                (peer_hbm, peer_ref),
                (own_hbm, own_ref),
                (filt_hbm, filt_ref),
                (dres_hbm, dres_ref),
                (ext_hbm, ext_ref),
                (output_hbm, output_ref),
            )
        )
    ]
    greet_all(count, parts, me)
    for load in loads:
        load.start()
    to_tile(tile, [small_ref[27:28], small_ref[28:29]])
    total_ref[...] = jnp.zeros_like(total_ref)
    small_out_ref[...] = jnp.zeros_like(small_out_ref)
    await_all(count)
    send_to_all(lambda other: tile, landed, sum_send, sum_recv, count, parts, me)

    keep_at = {}
    for i, (order, _, _) in enumerate(streams):
        keep_at[i, 0] = 0
        for t, bit in enumerate(bits_of(depth, order)):
            half = row_count >> (t + 1)
            keep_at[i, t + 1] = keep_at[i, t] + lax.rem(row_rank // (1 << bit), 2) * half

    in_flight = 2
    follower = {}
    for i, (order, _, place) in enumerate(streams):
        for j, (other_order, _, other_place) in enumerate(streams):
            if min(order, 2) == min(other_order, 2) and other_place == place + in_flight:
                follower[i] = j

    def give_at(i, t):
        return 2 * keep_at[i, t] + (row_count >> (t + 1)) - keep_at[i, t + 1]

    def tile_at(i, p):
        order, slot, _ = streams[i]
        owner = 0
        for t, bit in enumerate(bits_of(depth, order)):
            owner = owner + lax.rem(p // (1 << (depth - 1 - t)), 2) * (1 << bit)
        return slot_ref[owner * cap + slot]

    def pair_copy(i):
        return swap_copy(
            pair_out.at[i], pair_in.at[i], pair_send.at[i], pair_recv.at[i], other_core
        )

    def pair_start(i):
        def body(p, carry):
            index = tile_at(i, p)
            value = peer_ref[jnp.maximum(index, 0)]
            pair_out[i, p] = jnp.where(index >= 0, value, jnp.zeros_like(value))
            return carry

        lax.fori_loop(0, row_count, body, 0, unroll=8)
        pair_copy(i).start()

    def tree_copy(i, t):
        order, _, _ = streams[i]
        half = row_count >> (t + 1)
        part = pl.ds(row_count - (row_count >> t), half)
        return swap_copy(
            staged.at[i, part], arrived.at[i, part], tree_send.at[i, t], tree_recv.at[i, t],
            (flip(row_rank, bits_of(depth, order)[t]), part_rank),
        )

    def pair_end(i):
        pair_copy(i).wait()

        def value_at(p):
            index = tile_at(i, p)
            value = own_ref[jnp.maximum(index, 0)]
            return jnp.where(index >= 0, value, 0.0) + pair_in[i, p].astype(F32)

        def give(p, carry):
            staged[i, p] = value_at(give_at(i, 0) + p).astype(BF16)
            return carry

        def keep(p, carry):
            sums[i, keep_at[i, 1] + p] = value_at(keep_at[i, 1] + p)
            return carry

        lax.fori_loop(0, row_count // 2, give, 0, unroll=8)
        if streams[i][2] < in_flight:
            tree_copy(i, 0).start()
        lax.fori_loop(0, row_count // 2, keep, 0, unroll=8)

    def tree_step(i, t):
        came = row_count - (row_count >> t)
        tree_copy(i, t).wait()
        if t == 0 and i in follower:
            tree_copy(follower[i], 0).start()
        low = keep_at[i, t + 1]

        def values(k, size):
            return sums[i, pl.ds(k, size)] + arrived[i, pl.ds(came + k - low, size)].astype(F32)

        if t + 1 < depth:
            half = row_count >> (t + 2)
            at = row_count - (row_count >> (t + 1))
            staged[i, at : at + half] = values(give_at(i, t + 1), half).astype(BF16)
            tree_copy(i, t + 1).start()
            k = keep_at[i, t + 2]
            sums[i, pl.ds(k, half)] = values(k, half)
        else:
            tile_out_ref[streams[i][1]] = values(low, 1)[0]

    loads[0].wait()
    for i in range(wide):
        pair_start(i)
    output_copy = swap_copy(output_ref, output_in, output_sem.at[0], output_sem.at[1], other_core)
    loads[1].wait()
    for i in range(wide):
        pair_end(i)

    for load in loads[2:]:
        load.wait()
    output_copy.start()
    await_from_all(tile, landed, sum_send, sum_recv, count, parts, me)
    back = add_landed(tile[...], landed, count)
    gain_mean = from_tile(back, 0, groups) * (1.0 / node_total)
    shift_mean = from_tile(back, 1, groups) * (1.0 / node_total)
    centre = stat_ref[0:1] / node_total
    inv_std = lax.rsqrt(stat_ref[1:2] / node_total - centre * centre + norm_eps)
    factor = params_ref[27:28] * inv_std
    grad_ref[...] = (
        factor * (dres_ref[...] - shift_mean - (filt_ref[...] - centre) * inv_std * gain_mean)
    ).astype(BF16)

    blocks = rows // block
    span = block + 2 * HALO
    has_before = me > 0
    has_after = me < count - 1

    def rim_low():
        return swap_copy(
            rim_ref.at[0], rim_in.at[1], rim_sem.at[0, 0], rim_sem.at[1, 1],
            device_of(jnp.maximum(me - 1, 0), parts),
        )

    def rim_high():
        return swap_copy(
            rim_ref.at[1], rim_in.at[0], rim_sem.at[0, 1], rim_sem.at[1, 0],
            device_of(jnp.minimum(me + 1, count - 1), parts),
        )

    def finish_rows(low, size):
        input_grad_ref[pl.ds(first + low, size), :] = (
            dres_ref[low : low + size] + total_ref[HALO + low : HALO + low + size]
        )

    late = rows - block - HALO

    def out_copy(i):
        low, size = ((late, rows - late), (0, late))[i]
        here = input_grad_ref.at[pl.ds(first + low, size)]
        return swap_copy(here, here, out_sem.at[0, i], out_sem.at[1, i], other_core)

    group = 3
    points = TAPS // group
    schedule = {}
    for i, (_, _, place) in enumerate(streams):
        for t in range(depth):
            due = 2 * place + 9 * t + 8
            schedule.setdefault(min(due, blocks * points), []).append((due, t, i))

    def step(it, carry):
        b = lax.rem(it * (blocks - 1), blocks)
        base = pl.multiple_of(b * block, block)
        window = pl.ds(base, span)
        place = near_ref[0:TAPS, pl.ds(base, block)]
        place = place + lax.broadcasted_iota(jnp.int32, place.shape, 1) // LANES * LANES
        row = lax.broadcasted_iota(jnp.int32, (span, block), 0)
        grad = grad_ref[pl.ds(base, block), :]
        for point in range(points):
            total = total_ref[window, :]
            tokens = ext_ref[window, :].astype(F32)
            for k in range(point * group, (point + 1) * group):
                hot = (place[k : k + 1, :] == row).astype(F32).astype(BF16)
                spread = dot_plain(hot, grad)
                total += spread * params_ref[k : k + 1, :]
                small_out_ref[k : k + 1, :] += col_sum(spread * tokens)
            total_ref[window, :] = total
            for s in range(blocks):
                if s * points + point in schedule:

                    @pl.when(it == s)
                    def _(s=s, point=point):
                        for _, t, i in sorted(schedule[s * points + point]):
                            tree_step(i, t)

        @pl.when(it == 1)
        def _():
            rim_ref[0] = total_ref[0:HALO].astype(BF16)
            rim_ref[1] = total_ref[rows + HALO : rows + 2 * HALO].astype(BF16)

            @pl.when(has_before)
            def _():
                rim_low().start()

            @pl.when(has_after)
            def _():
                rim_high().start()

        @pl.when(it == 2)
        def _():
            @pl.when(has_before)
            def _():
                rim_low().wait_send()
                rim_high().wait_recv()
                total_ref[HALO : 2 * HALO] += rim_in[0].astype(F32)

            @pl.when(has_after)
            def _():
                rim_high().wait_send()
                rim_low().wait_recv()
                total_ref[rows : rows + HALO] += rim_in[1].astype(F32)

            finish_rows(late, rows - late)
            out_copy(0).start()

        return carry

    lax.fori_loop(0, blocks, step, 0)

    flat[...] = jnp.zeros_like(flat)
    for r in range(small_rows):
        row = small_out_ref[r : r + 1, :] if r < TAPS else small_ref[r : r + 1, :]
        for g in range(groups):
            at = r * groups + g
            flat[at // 8, at % 8 : at % 8 + 1, :] = row[:, g * LANES : (g + 1) * LANES]
    send_to_all(lambda other: flat.at[other], flat_in, flat_send, flat_recv, count, parts, me)
    finish_rows(0, late)
    out_copy(1).start()
    await_from_all(flat.at[0], flat_in, flat_send, flat_recv, count, parts, me)
    part_sum[...] = add_landed(flat[me], flat_in, count)
    send_to_all(lambda other: part_sum, flat_all, all_send, all_recv, count, parts, me)
    for _, t, i in sorted(schedule.get(blocks * points, [])):
        tree_step(i, t)
    await_from_all(part_sum, flat_all, all_send, all_recv, count, parts, me)
    flat_all[0] = part_sum[...]
    for r in range(small_rows):
        for g in range(groups):
            at = r * groups + g
            tile_from = lax.rem(at // 8 - me + count, count)
            small_out_ref[r : r + 1, g * LANES : (g + 1) * LANES] = flat_all[
                tile_from, at % 8 : at % 8 + 1, :
            ]
    output_copy.wait()
    out_copy(0).wait()
    out_copy(1).wait()


def filter_backward(
    slots, extended, filtered, dres, near_t, params, stat, small, own_grad, peer_grad, output, cap,
    row_count, parts, block=256
):
    rows, width = filtered.shape
    count = row_count * parts
    depth = row_count.bit_length() - 1
    wide = len(streams_of(cap, depth))
    vmem = pl.BlockSpec(memory_space=pltpu.VMEM)
    anywhere = pl.BlockSpec(memory_space=pl.ANY)
    dma = pltpu.SemaphoreType.DMA
    of_streams = (wide, row_count, BR, width)
    return pl.pallas_call(
        functools.partial(
            filter_back_kernel, block=block, row_count=row_count, parts=parts, cap=cap,
            node_total=rows * count,
        ),
        in_specs=[pl.BlockSpec(memory_space=pltpu.SMEM)]
        + [anywhere] * 3
        + [vmem] * 4
        + [anywhere] * 3,
        out_specs=[vmem] * 4,
        out_shape=[
            jax.ShapeDtypeStruct((rows * parts, width), F32),
            jax.ShapeDtypeStruct((rows, width), F32),
            jax.ShapeDtypeStruct(params.shape, F32),
            jax.ShapeDtypeStruct((cap, BR, width), F32),
        ],
        scratch_shapes=[
            pltpu.VMEM(extended.shape, BF16),
            pltpu.VMEM(filtered.shape, F32),
            pltpu.VMEM(dres.shape, F32),
            pltpu.VMEM(own_grad.shape, F32),
            pltpu.VMEM(peer_grad.shape, BF16),
            pltpu.VMEM(output.shape, F32),
            pltpu.VMEM(of_streams, BF16),
            pltpu.VMEM(of_streams, BF16),
            pltpu.VMEM(of_streams, F32),
            pltpu.VMEM(of_streams, BF16),
            pltpu.VMEM(of_streams, BF16),
            pltpu.VMEM((rows + 2 * HALO, width), F32),
            pltpu.VMEM((rows, width), BF16),
            pltpu.VMEM((2, HALO, width), BF16),
            pltpu.VMEM((2, HALO, width), BF16),
            pltpu.VMEM((8, LANES), F32),
            pltpu.VMEM((count, 8, LANES), F32),
            pltpu.VMEM((count, 8, LANES), F32),
            pltpu.VMEM((count, 8, LANES), F32),
            pltpu.VMEM((8, LANES), F32),
            pltpu.VMEM((count, 8, LANES), F32),
            dma((6,)),
            dma((2,)),
            dma((wide,)),
            dma((wide,)),
            dma((count,)),
            dma((count,)),
            dma((wide, depth)),
            dma((wide, depth)),
            dma((2, 2)),
            dma((count,)),
            dma((count,)),
            dma((count,)),
            dma((count,)),
            dma((2, 2)),
        ],
        compiler_params=pltpu.CompilerParams(
            collective_id=1, has_side_effects=True, vmem_limit_bytes=60 << 20
        ),
    )(
        slots, extended, filtered, dres, near_t, params, stat, small, own_grad, peer_grad, output
    )


def last_kernel(
    slot_ref, rank_ref, output_own, output_in, grad_in, weight_ref, params_ref, first_ref,
    second_ref, small_ref, tile_grad_ref, tile_first_ref, tile_second_ref,
    output_ref, input_grad_ref, weight_out, first_out, second_out, low_out, params_out,
    small_first_out, small_second_out,
    stage_ref, old_ref, copy_sem, tile_sem
):
    row_rank, part_rank = rank_ref[0], rank_ref[1]
    rows = output_own.shape[0]
    cap = tile_grad_ref.shape[0]
    cuts = 4
    copies = []
    size = rows // cuts
    for j in range(cuts):
        own_rows = pl.ds(part_rank * rows + j * size, size)
        other_rows = pl.ds((1 - part_rank) * rows + j * size, size)
        part = pl.ds(j * size, size)
        copies.append((output_own.at[part], output_ref.at[own_rows]))
        copies.append((output_in.at[part], output_ref.at[other_rows]))
        copies.append((grad_in.at[own_rows], input_grad_ref.at[own_rows]))
        copies.append((grad_in.at[other_rows], input_grad_ref.at[other_rows]))
    reads = [
        pltpu.make_async_copy(source, stage_ref.at[i], copy_sem.at[0, i])
        for i, (source, _) in enumerate(copies)
    ]
    writes = [
        pltpu.make_async_copy(stage_ref.at[i], landing, copy_sem.at[1, i])
        for i, (_, landing) in enumerate(copies)
    ]
    tiles = [slot_ref[row_rank * cap + c] for c in range(cap)]
    olds = [
        pltpu.make_async_copy(
            weight_ref.at[part_rank, pl.ds(pl.multiple_of(jnp.maximum(t, 0) * BR, BR), BR)],
            old_ref.at[c],
            tile_sem.at[c],
        )
        for c, t in enumerate(tiles)
    ]
    for copy in olds:
        copy.start()
    for copy in reads:
        copy.start()
    params_out[...], small_first_out[...], small_second_out[...] = adam_step(
        params_ref[...], small_ref[...], first_ref[...], second_ref[...], 0.0
    )
    for read, write in zip(reads, writes):
        read.wait()
        write.start()
    for c, t in enumerate(tiles):
        olds[c].wait()
        new = adam_step(
            old_ref[c].astype(F32), tile_grad_ref[c], tile_first_ref[0, c], tile_second_ref[0, c],
            decay_rate,
        )
        live = [jnp.where(t >= 0, a, 0.0) for a in new]
        weight_out[0, c] = live[0]
        first_out[0, c] = live[1]
        second_out[0, c] = live[2]
        low_out[0, c] = live[0].astype(BF16)
    for copy in writes:
        copy.wait()


def last_step(
    slots, ranks, output_own, output_in, input_grad, weights, params, small_first, small_second,
    small_sum, tile_grad, tile_first, tile_second
):
    vmem = pl.BlockSpec(memory_space=pltpu.VMEM)
    anywhere = pl.BlockSpec(memory_space=pl.ANY)
    smem = pl.BlockSpec(memory_space=pltpu.SMEM)
    full = jax.ShapeDtypeStruct(input_grad.shape, F32)
    tile = jax.ShapeDtypeStruct(tile_first.shape, F32)
    small = jax.ShapeDtypeStruct(params.shape, F32)
    return pl.pallas_call(
        last_kernel,
        in_specs=[smem, smem] + [anywhere] * 4 + [vmem] * 7,
        out_specs=[anywhere] * 2 + [vmem] * 7,
        out_shape=[
            full, full, tile, tile, tile, jax.ShapeDtypeStruct(tile_first.shape, BF16), small,
            small, small,
        ],
        scratch_shapes=[
            pltpu.VMEM((16, output_own.shape[0] // 4, output_own.shape[1]), F32),
            pltpu.VMEM(tile_grad.shape, BF16),
            pltpu.SemaphoreType.DMA((2, 16)),
            pltpu.SemaphoreType.DMA((tile_grad.shape[0],)),
        ],
        compiler_params=pltpu.CompilerParams(vmem_limit_bytes=60 << 20),
    )(
        slots, ranks, output_own, output_in, input_grad, weights, params, small_first, small_second,
        small_sum, tile_grad, tile_first, tile_second
    )


def block_kernel(
    rank_ref, filt_ref, tok_ref, mask_ref, cot_ref, stat_ref, params_ref, weight_ref,
    out_ref, dres_ref, own_ref, peer_ref, small_ref, grad_ref, *, node_total, parts, width, units, block
):
    i = pl.program_id(0)

    @pl.when(i == 0)
    def _():
        grad_ref[...] = jnp.zeros_like(grad_ref)
        small_ref[...] = jnp.zeros_like(small_ref)

    part = width // parts
    unit_part = units // parts
    scale = HEAD_DIM**-0.5

    def weight_rows(low, count):
        return jnp.concatenate([weight_ref[h, low : low + count] for h in range(parts)], axis=0)

    def qkv_rows(j):
        return weight_rows(j * part, part)

    def proj_rows():
        return weight_rows(3 * part, part)

    def add_grad(low, value):
        for h in range(parts):
            grad_ref[h, low : low + part] += value[h * part : (h + 1) * part]

    def param(row):
        return params_ref[row : row + 1, :]

    def add_small(row, value):
        small_ref[row : row + 1, :] += value

    centre = stat_ref[0:1] / node_total
    inv_std = lax.rsqrt(stat_ref[1:2] / node_total - centre * centre + norm_eps)
    bn_norm = (filt_ref[...] - centre) * inv_std
    resid = tok_ref[...].astype(F32) + (bn_norm * param(27) + param(28))
    unit_one, factor_one = layer_norm(resid)
    normed_one = (unit_one * param(29) + param(30)).astype(BF16)
    query = ((dot_last(normed_one, qkv_rows(0)) + param(35)) * scale).astype(BF16)
    key = (dot_last(normed_one, qkv_rows(1)) * scale).astype(BF16)
    value = ((dot_last(normed_one, qkv_rows(2)) + param(36)) * scale).astype(BF16)

    side = LANES
    heads = LANES // HEAD_DIM
    groups = width // LANES
    lane_head = lax.broadcasted_iota(jnp.int32, (side, LANES), 1) // HEAD_DIM
    window_q = lax.broadcasted_iota(jnp.int32, (side, side), 0) // WIN
    window_k = lax.broadcasted_iota(jnp.int32, (side, side), 1) // WIN

    def stack_heads(a):
        return jnp.concatenate(
            [jnp.where(lane_head == j, a, jnp.zeros_like(a)) for j in range(heads)], axis=0
        )

    def pick_heads(a):
        picked = a[:side]
        for j in range(1, heads):
            picked = jnp.where(lane_head == j, a[j * side : (j + 1) * side], picked)
        return picked

    def cut(a, s, g):
        return a[s * side : (s + 1) * side, g * LANES : (g + 1) * LANES]

    kept = {}
    mixture = []
    for s in range(block // side):
        keep = (window_q == window_k) & (mask_ref[0:1, s * side : (s + 1) * side] > 0)
        mixed = []
        for g in range(groups):
            query_g = cut(query, s, g)
            keys = stack_heads(cut(key, s, g))
            values = stack_heads(cut(value, s, g))
            scores = dot_last(query_g, keys)
            probs = []
            for j in range(heads):
                score = jnp.where(keep, scores[:, j * side : (j + 1) * side], masked_score)
                power = jnp.exp(score - jnp.max(score, axis=1, keepdims=True))
                probs.append(power / jnp.sum(power, axis=1, keepdims=True))
            probs = jnp.concatenate(probs, axis=1)
            probs_low = probs.astype(BF16)
            mixed.append(dot_plain(probs_low, values))
            kept[s, g] = (query_g, keys, values, probs, probs_low)
        mixture.append(jnp.concatenate(mixed, axis=1))
    mixture = jnp.concatenate(mixture, axis=0).astype(BF16)
    after = resid + (dot_plain(mixture, proj_rows()) + param(33))
    unit_two, factor_two = layer_norm(after)
    normed_two = (unit_two * param(31) + param(32)).astype(BF16)

    cotangent = cot_ref[...]
    grad_ffn = cotangent.astype(BF16)
    ffn = jnp.zeros_like(after)
    grad_normed_two = jnp.zeros_like(after)
    chunk = width
    for h in range(parts):
        for c in range(unit_part // chunk):
            low = 4 * part + c * chunk
            unit = 37 + (h * unit_part) // chunk + c
            fc1 = weight_ref[h, low : low + chunk]
            fc2 = weight_ref[h, low + unit_part : low + unit_part + chunk]
            hidden = dot_last(normed_two, fc1) + param(unit)
            cumulative = 0.5 * (1.0 + lax.erf(hidden * 0.5**0.5))
            activation = (hidden * cumulative).astype(BF16)
            density = jnp.exp(-0.5 * hidden * hidden) * (2.0 * jnp.pi) ** (-0.5)
            ffn += dot_plain(activation, fc2)
            grad_hidden = (
                dot_last(grad_ffn, fc2) * (cumulative + hidden * density)
            ).astype(BF16)
            grad_normed_two += dot_plain(grad_hidden, fc1)
            grad_ref[h, low : low + chunk] += dot_first(grad_hidden, normed_two)
            grad_ref[h, low + unit_part : low + unit_part + chunk] += dot_first(activation, grad_ffn)
            add_small(unit, col_sum(grad_hidden.astype(F32)))
    out_ref[...] = after + (ffn + param(34))
    add_small(34, col_sum(grad_ffn.astype(F32)))

    grad_after = cotangent + norm_back(grad_normed_two, unit_two, factor_two, param(31))
    add_small(31, col_sum(grad_normed_two * unit_two))
    add_small(32, col_sum(grad_normed_two))
    grad_branch = grad_after.astype(BF16)
    add_grad(3 * part, dot_first(mixture, grad_branch))
    add_small(33, col_sum(grad_branch.astype(F32)))
    grad_mixture = dot_last(grad_branch, proj_rows()).astype(BF16)

    grads = ([], [], [])
    for s in range(block // side):
        here = ([], [], [])
        for g in range(groups):
            query_g, keys, values, probs, probs_low = kept[s, g]
            grad_mix = cut(grad_mixture, s, g)
            grad_probs = dot_last(grad_mix, values)
            grad_scores = []
            for j in range(heads):
                prob = probs[:, j * side : (j + 1) * side]
                term = prob * grad_probs[:, j * side : (j + 1) * side]
                grad_scores.append(
                    (term - prob * jnp.sum(term, axis=1, keepdims=True)).astype(BF16)
                )
            grad_scores = jnp.concatenate(grad_scores, axis=1)
            here[0].append(dot_plain(grad_scores, keys))
            here[1].append(pick_heads(dot_first(grad_scores, query_g)))
            here[2].append(pick_heads(dot_first(probs_low, grad_mix)))
        for kind in range(3):
            grads[kind].append(jnp.concatenate(here[kind], axis=1))
    grad_qkv = [jnp.concatenate(kind, axis=0).astype(BF16) for kind in grads]
    grad_normed_one = jnp.zeros_like(resid)
    for j in range(3):
        grad_normed_one += dot_plain(grad_qkv[j], qkv_rows(j))
        add_grad(j * part, scale * dot_first(grad_qkv[j], normed_one))
    grad_normed_one = scale * grad_normed_one
    add_small(35, scale * col_sum(grad_qkv[0].astype(F32)))
    add_small(36, scale * col_sum(grad_qkv[2].astype(F32)))
    dres = grad_after + norm_back(grad_normed_one, unit_one, factor_one, param(29))
    add_small(29, col_sum(grad_normed_one * unit_one))
    add_small(30, col_sum(grad_normed_one))
    add_small(27, col_sum(dres * bn_norm))
    add_small(28, col_sum(dres))
    dres_ref[...] = dres

    @pl.when(i == pl.num_programs(0) - 1)
    def _():
        mine = lax.axis_index("heads")
        own_ref[...] = grad_ref[mine]
        peer_ref[...] = grad_ref[1 - mine].astype(BF16)


def block_step(filtered, tokens, mask, cotangent, stat, params, weights, node_total, block=256):
    rows, width = filtered.shape
    parts = weights.shape[0]
    units = (weights.shape[1] - 4 * (width // parts)) // 2 * parts
    blocks = rows // block
    outs = [
        jax.ShapeDtypeStruct((rows, width), F32),
        jax.ShapeDtypeStruct((rows, width), F32),
        jax.ShapeDtypeStruct(weights.shape[1:], F32),
        jax.ShapeDtypeStruct(weights.shape[1:], BF16),
        jax.ShapeDtypeStruct(params.shape, F32),
    ]

    def whole(shape):
        zeros = (0,) * len(shape)
        return pl.BlockSpec(shape, lambda i, rank: zeros)

    here = pl.BlockSpec((block, width), lambda i, rank: (i, 0))
    chip = pl.BlockSpec((block, width), lambda i, rank: (rank[0] * blocks + i, 0))
    return pl.pallas_call(
        functools.partial(
            block_kernel, node_total=node_total, parts=parts, width=width, units=units, block=block
        ),
        grid_spec=pltpu.PrefetchScalarGridSpec(
            num_scalar_prefetch=1,
            grid=(blocks,),
            in_specs=[
                here,
                chip,
                pl.BlockSpec((1, block), lambda i, rank: (0, rank[0] * blocks + i)),
                chip,
                whole(stat.shape),
                whole(params.shape),
                whole(weights.shape),
            ],
            out_specs=[here, here] + [whole(o.shape) for o in outs[2:]],
            scratch_shapes=[pltpu.VMEM(weights.shape, F32)],
        ),
        out_shape=outs,
        compiler_params=pltpu.CompilerParams(vmem_limit_bytes=60 << 20),
    )(lax.axis_index("heads").reshape(1), filtered, tokens, mask, cotangent, stat, params, weights)


def local(
    tokens_in, neighbours, scene_lengths, window_mask, small_params, qkv_weight, proj_weight,
    fc1_weight, fc2_weight, cotangent, owners, small_first, small_second, tile_first, tile_second
):
    rows_here, width = tokens_in.shape
    row_count = lax.axis_size("rows")
    parts = lax.axis_size("heads")
    row_rank = lax.axis_index("rows")
    part_rank = lax.axis_index("heads")
    rows = rows_here // parts
    node_total = rows_here * row_count
    tile_count = owners.shape[0]
    slot_cap = tile_first.shape[1]

    filtered, stat, near_t, extended, weights = filter_forward(
        scene_lengths, tokens_in, neighbours.T, small_params, qkv_weight, proj_weight, fc1_weight,
        fc2_weight, row_count, parts
    )
    output, dres, own_grad, peer_grad, small_grad = block_step(
        filtered, tokens_in, window_mask[None], cotangent, stat, small_params, weights, node_total
    )

    tile_order = jnp.arange(tile_count, dtype=jnp.int32)
    same_owner = (owners[:, None] == owners[None, :]) & (tile_order[None, :] < tile_order[:, None])
    slot_of = owners * slot_cap + jnp.sum(same_owner.astype(jnp.int32), axis=1)
    slot_ids = jnp.arange(row_count * slot_cap, dtype=jnp.int32)
    found = slot_of[None, :] == slot_ids[:, None]
    slot_tile = jnp.max(jnp.where(found, tile_order[None, :], -1), axis=1)

    input_grad, output_in, small_sum, tile_grad = filter_backward(
        slot_tile, extended, filtered, dres, near_t, small_params, stat, small_grad,
        own_grad.reshape(tile_count, BR, width), peer_grad.reshape(tile_count, BR, width), output,
        slot_cap, row_count, parts
    )
    return last_step(
        slot_tile, jnp.stack([row_rank, part_rank]), output, output_in, input_grad, weights,
        small_params, small_first, small_second, small_sum, tile_grad, tile_first, tile_second
    )


def solution(mesh):
    return jax.shard_map(
        local,
        mesh=mesh,
        in_specs=(
            P("rows", None),
            P("rows", None),
            P(),
            P("rows"),
            P(),
            P(None, "heads", None),
            P("heads", None),
            P("heads", None),
            P("heads", None),
            P("rows", None),
            P(),
            P(),
            P(),
            P("heads", "rows", None, None),
            P("heads", "rows", None, None),
        ),
        out_specs=(
            P("rows", None),
            P("rows", None),
            P("heads", "rows", None, None),
            P("heads", "rows", None, None),
            P("heads", "rows", None, None),
            P("heads", "rows", None, None),
            P(),
            P(),
            P(),
        ),
        check_vma=False,
    )
```

```python
import functools

import jax
import jax.numpy as jnp
from jax import lax
from jax.experimental import pallas as pl
from jax.experimental.pallas import tpu as pltpu
from jax.sharding import PartitionSpec as P

HEAD_DIM = 32
WIN = 32
HALO = 128
BR = 16
STEP = 3
TAPS = 27
LANES = 128

norm_eps = 1e-05
adam_rate = 0.05
beta_one = 0.5
beta_two = 0.5
adam_eps = 1e-08
decay_rate = 0.05
masked_score = -1e30

F32 = jnp.float32
BF16 = jnp.bfloat16


def adam_step(weight, gradient, first_moment, second_moment, decay_factor):
    first_new = beta_one * first_moment + (1.0 - beta_one) * gradient
    second_new = beta_two * second_moment + (1.0 - beta_two) * gradient * gradient
    first_hat = first_new / (1.0 - beta_one**STEP)
    second_hat = second_new / (1.0 - beta_two**STEP)
    weight_new = weight - adam_rate * (
        first_hat / (jnp.sqrt(second_hat) + adam_eps) + decay_factor * weight
    )
    return (weight_new, first_new, second_new)


def dot_plain(a, b):
    return jnp.dot(a, b, preferred_element_type=F32)


def dot_last(a, b):
    return lax.dot_general(a, b, (((1,), (1,)), ((), ())), preferred_element_type=F32)


def dot_first(a, b):
    return lax.dot_general(a, b, (((0,), (0,)), ((), ())), preferred_element_type=F32)


def col_sum(v):
    return jnp.sum(v, axis=0, keepdims=True)


def layer_norm(v):
    centre = v - jnp.mean(v, axis=1, keepdims=True)
    factor = lax.rsqrt(jnp.mean(centre * centre, axis=1, keepdims=True) + norm_eps)
    return centre * factor, factor


def norm_back(upstream, unit_part, factor, gain):
    scaled = upstream * gain
    return factor * (
        scaled
        - jnp.mean(scaled, axis=1, keepdims=True)
        - unit_part * jnp.mean(scaled * unit_part, axis=1, keepdims=True)
    )


def full_spec(shape):
    zeros = (0,) * len(shape)
    return pl.BlockSpec(shape, lambda i: zeros)


MESH = pl.DeviceIdType.MESH


def device_of(index, parts):
    return (index // parts, lax.rem(index, parts))


def greet_all(count, parts, me):
    barrier = pltpu.get_barrier_semaphore()

    def greet(j, carry):
        pl.semaphore_signal(
            barrier, inc=1, device_id=device_of(lax.rem(me + j, count), parts), device_id_type=MESH
        )
        return carry

    lax.fori_loop(1, count, greet, 0)


def await_all(count):
    pl.semaphore_wait(pltpu.get_barrier_semaphore(), count - 1)


def swap_copy(source, landing, send_sem, recv_sem, device):
    return pltpu.make_async_remote_copy(
        src_ref=source, dst_ref=landing, send_sem=send_sem, recv_sem=recv_sem,
        device_id=device, device_id_type=MESH,
    )


def send_to_all(source_of, landing, send_sem, recv_sem, count, parts, me):
    def send(j, carry):
        other = lax.rem(me + j, count)
        swap_copy(
            source_of(other), landing.at[count - j], send_sem.at[j], recv_sem.at[count - j],
            device_of(other, parts),
        ).start()
        return carry

    lax.fori_loop(1, count, send, 0)


def await_from_all(source, landing, send_sem, recv_sem, count, parts, me):
    def wait(j, carry):
        swap_copy(
            source, landing.at[count - j], send_sem.at[j], recv_sem.at[count - j],
            device_of(lax.rem(me + j, count), parts),
        ).wait()
        return carry

    lax.fori_loop(1, count, wait, 0)


def add_landed(own, landing, count):
    return lax.fori_loop(1, count, lambda j, total: total + landing[j], own)


def to_tile(tile_ref, rows):
    tile_ref[...] = jnp.zeros_like(tile_ref)
    groups = rows[0].shape[1] // LANES
    for r, row in enumerate(rows):
        for g in range(groups):
            at = r * groups + g
            tile_ref[at : at + 1, :] = row[:, g * LANES : (g + 1) * LANES]


def from_tile(tile, row, groups):
    at = row * groups
    return jnp.concatenate([tile[at + g : at + g + 1, :] for g in range(groups)], axis=1)


def filter_kernel(
    lengths_ref, tokens_ref, near_ref, taps_ref, qkv_ref, proj_ref, fc1_ref, fc2_ref,
    filt_ref, stat_ref, near_t_ref, ext_ref, stack_ref,
    near_in, tile, landed, local_sem, side_sem, weight_sem, send_sem, recv_sem,
    *, block, row_count, parts, scenes
):
    row_rank = lax.axis_index("rows")
    part_rank = lax.axis_index("heads")
    count = row_count * parts
    me = row_rank * parts + part_rank
    rows_here, width = tokens_ref.shape
    rows = rows_here // parts
    part = width // parts
    first = part_rank * rows
    node_total = rows_here * row_count
    greet_all(count, parts, me)

    own_copy = pltpu.make_async_copy(
        tokens_ref.at[pl.ds(first, rows)], ext_ref.at[pl.ds(HALO, rows)], local_sem.at[0]
    )
    near_copy = pltpu.make_async_copy(
        near_ref.at[:, pl.ds(pl.multiple_of(first, LANES), rows)], near_in, local_sem.at[1]
    )
    own_copy.start()
    near_copy.start()
    low_side = ext_ref.at[pl.ds(0, HALO)]
    high_side = ext_ref.at[pl.ds(rows + HALO, HALO)]

    @pl.when(part_rank == 0)
    def _():
        pltpu.make_async_copy(tokens_ref.at[pl.ds(rows, HALO)], high_side, local_sem.at[2]).start()

    @pl.when(part_rank == 1)
    def _():
        pltpu.make_async_copy(
            tokens_ref.at[pl.ds(rows - HALO, HALO)], low_side, local_sem.at[2]
        ).start()

    @pl.when(me == 0)
    def _():
        ext_ref[0:HALO, :] = jnp.zeros((HALO, width), BF16)

    @pl.when(me == count - 1)
    def _():
        ext_ref[rows + HALO :, :] = jnp.zeros((HALO, width), BF16)

    pieces = []
    low = 0
    for j in range(3):
        pieces.append((qkv_ref.at[j], low, part))
        low += part
    for ref in (proj_ref, fc1_ref, fc2_ref):
        pieces.append((ref, low, ref.shape[0]))
        low += ref.shape[0]
    other_core = (row_rank, 1 - part_rank)

    def own_weight(i):
        ref, at, size = pieces[i]
        return pltpu.make_async_copy(
            ref, stack_ref.at[part_rank, pl.ds(at, size)], weight_sem.at[0, i]
        )

    def sent_weight(i):
        ref, at, size = pieces[i]
        here = stack_ref.at[part_rank, pl.ds(at, size)]
        return swap_copy(here, here, weight_sem.at[1, i], weight_sem.at[2, i], other_core)

    for i in range(len(pieces)):
        own_weight(i).start()

    def side_up():
        return swap_copy(
            tokens_ref.at[pl.ds(rows_here - HALO, HALO)], low_side, side_sem.at[0], side_sem.at[1],
            (jnp.minimum(row_rank + 1, row_count - 1), part_rank),
        )

    def side_down():
        return swap_copy(
            tokens_ref.at[pl.ds(0, HALO)], high_side, side_sem.at[0], side_sem.at[1],
            (jnp.maximum(row_rank - 1, 0), part_rank),
        )

    stat_ref[...] = jnp.zeros_like(stat_ref)
    near_copy.wait()
    own_copy.wait()

    ends = []
    reached = 0
    for s in range(scenes):
        reached = reached + lengths_ref[s]
        ends.append(reached * WIN)

    blocks = rows // block
    span = block + 2 * HALO

    def step(it, carry):
        @pl.when(it == 2)
        def _():
            await_all(count)

            @pl.when((part_rank == 0) & (row_rank < row_count - 1))
            def _():
                side_up().start()

            @pl.when((part_rank == 1) & (row_rank > 0))
            def _():
                side_down().start()

            for i in range(len(pieces)):
                own_weight(i).wait()
                sent_weight(i).start()

        @pl.when(it == blocks - 2)
        def _():
            pltpu.make_async_copy(
                tokens_ref.at[pl.ds(0, HALO)], low_side, local_sem.at[2]
            ).wait()

            @pl.when((part_rank == 0) & (row_rank < row_count - 1))
            def _():
                side_up().wait_send()

            @pl.when((part_rank == 0) & (row_rank > 0))
            def _():
                side_up().wait_recv()

            @pl.when((part_rank == 1) & (row_rank > 0))
            def _():
                side_down().wait_send()

            @pl.when((part_rank == 1) & (row_rank < row_count - 1))
            def _():
                side_down().wait_recv()

        b = lax.rem(it + 1, blocks)
        base = pl.multiple_of(b * block, block)
        window = ext_ref[pl.ds(base, span), :]
        near = near_in[:, pl.ds(base, block)]
        lane = lax.broadcasted_iota(jnp.int32, (1, block), 1)
        own_row = row_rank * rows_here + first + base + lane
        scene_low = jnp.zeros_like(own_row)
        scene_high = jnp.full_like(own_row, node_total)
        for end in ends:
            passed = own_row >= end
            scene_low = jnp.maximum(scene_low, jnp.where(passed, end, 0))
            scene_high = jnp.minimum(scene_high, jnp.where(passed, node_total, end))
        target = own_row + near
        usable = (near >= -HALO) & (target >= scene_low) & (target < scene_high)
        place_t = jnp.where(usable, near + lane + HALO, -8 * HALO)
        near_t_ref[0:TAPS, pl.ds(base, block)] = place_t
        place = jnp.transpose(
            jnp.concatenate([place_t, jnp.zeros((LANES - TAPS, block), jnp.int32)], axis=0)
        )
        column = lax.broadcasted_iota(jnp.int32, (block, span), 1)
        total = jnp.zeros((block, width), F32)
        group = 3
        for k0 in range(0, TAPS, group):
            hot = jnp.concatenate(
                [
                    (place[:, k : k + 1] == column).astype(F32).astype(BF16)
                    for k in range(k0, k0 + group)
                ],
                axis=0,
            )
            picked = dot_plain(hot, window)
            for j in range(group):
                total += picked[j * block : (j + 1) * block] * taps_ref[k0 + j : k0 + j + 1, :]
        filt_ref[pl.ds(base, block), :] = total
        stat_ref[0:1, :] += col_sum(total)
        stat_ref[1:2, :] += col_sum(total * total)
        return carry

    lax.fori_loop(0, blocks, step, 0)

    to_tile(tile, [stat_ref[0:1], stat_ref[1:2]])
    send_to_all(lambda other: tile, landed, send_sem, recv_sem, count, parts, me)
    for i in range(len(pieces)):
        sent_weight(i).wait()
    await_from_all(tile, landed, send_sem, recv_sem, count, parts, me)
    total = add_landed(tile[...], landed, count)
    groups = width // LANES
    stat_ref[0:1, :] = from_tile(total, 0, groups)
    stat_ref[1:2, :] = from_tile(total, 1, groups)


def filter_forward(lengths, tokens, near, params, qkv, proj, fc1, fc2, row_count, parts, block=128):
    rows_here, width = tokens.shape
    rows = rows_here // parts
    stack_rows = qkv.shape[0] * qkv.shape[1] + proj.shape[0] + fc1.shape[0] + fc2.shape[0]
    count = row_count * parts
    anywhere = pl.BlockSpec(memory_space=pl.ANY)
    vmem = pl.BlockSpec(memory_space=pltpu.VMEM)
    return pl.pallas_call(
        functools.partial(
            filter_kernel, block=block, row_count=row_count, parts=parts, scenes=lengths.shape[0]
        ),
        in_specs=[pl.BlockSpec(memory_space=pltpu.SMEM), anywhere, anywhere, vmem] + [anywhere] * 4,
        out_specs=[vmem] * 5,
        out_shape=[
            jax.ShapeDtypeStruct((rows, width), F32),
            jax.ShapeDtypeStruct((8, width), F32),
            jax.ShapeDtypeStruct((32, rows), jnp.int32),
            jax.ShapeDtypeStruct((rows + 2 * HALO, width), BF16),
            jax.ShapeDtypeStruct((parts, stack_rows, width), BF16),
        ],
        scratch_shapes=[
            pltpu.VMEM((TAPS, rows), jnp.int32),
            pltpu.VMEM((8, LANES), F32),
            pltpu.VMEM((count, 8, LANES), F32),
            pltpu.SemaphoreType.DMA((3,)),
            pltpu.SemaphoreType.DMA((2,)),
            pltpu.SemaphoreType.DMA((3, 6)),
            pltpu.SemaphoreType.DMA((count,)),
            pltpu.SemaphoreType.DMA((count,)),
        ],
        compiler_params=pltpu.CompilerParams(
            collective_id=0, has_side_effects=True, vmem_limit_bytes=60 << 20
        ),
    )(lengths, tokens, near, params, qkv, proj, fc1, fc2)


def streams_of(cap, depth):
    seventh = cap // 7 if depth > 2 else 0
    rest = cap - 2 * seventh
    sizes = [
        (0, 0, rest // 2 // 2), (1, 0, (rest - rest // 2) // 2), (2, 0, seventh),
        (0, 1, rest // 2 - rest // 2 // 2), (1, 1, (rest - rest // 2) - (rest - rest // 2) // 2),
        (3, 0, seventh),
    ]
    streams = []
    slot = 0
    for order, place, size in sizes:
        if size:
            streams.append((order, slot, size, place))
            slot += size
    return streams


def bits_of(depth, order):
    bits = list(range(depth))
    if order == 1 and depth > 1:
        bits[:2] = [1, 0]
    if order == 2:
        bits[:3] = [2, 0, 1]
    if order == 3:
        bits[:3] = [2, 1, 0]
    return bits


def flip(rank, bit):
    weight = 1 << bit
    return rank + weight - 2 * weight * lax.rem(rank // weight, 2)


def filter_back_kernel(
    slot_ref, ext_hbm, filt_hbm, dres_hbm, near_ref, params_ref, stat_ref, small_ref, own_hbm,
    peer_hbm, output_hbm,
    input_grad_ref, output_in, small_out_ref, tile_out_ref,
    ext_ref, filt_ref, dres_ref, own_ref, peer_ref, output_ref, pair_out, pair_in, sums, staged, arrived,
    total_ref, grad_ref, rim_ref, rim_in, tile, landed, flat, flat_in, part_sum, flat_all,
    local_sem, output_sem, pair_send, pair_recv, sum_send, sum_recv, tree_send, tree_recv, rim_sem,
    flat_send, flat_recv, all_send, all_recv, out_sem,
    *, block, row_count, parts, cap, node_total
):
    row_rank = lax.axis_index("rows")
    part_rank = lax.axis_index("heads")
    count = row_count * parts
    me = row_rank * parts + part_rank
    rows, width = filt_ref.shape
    groups = width // LANES
    first = part_rank * rows
    depth = row_count.bit_length() - 1
    streams = streams_of(cap, depth)
    wide = len(streams)
    other_core = (row_rank, 1 - part_rank)
    small_rows = params_ref.shape[0]

    loads = [
        pltpu.make_async_copy(source, landing, local_sem.at[i])
        for i, (source, landing) in enumerate(
            (
                (peer_hbm, peer_ref),
                (own_hbm, own_ref),
                (filt_hbm, filt_ref),
                (dres_hbm, dres_ref),
                (ext_hbm, ext_ref),
                (output_hbm, output_ref),
            )
        )
    ]
    greet_all(count, parts, me)
    for load in loads:
        load.start()
    to_tile(tile, [small_ref[27:28], small_ref[28:29]])
    total_ref[...] = jnp.zeros_like(total_ref)
    small_out_ref[...] = jnp.zeros_like(small_out_ref)
    await_all(count)
    send_to_all(lambda other: tile, landed, sum_send, sum_recv, count, parts, me)

    keep_at = {}
    for i, (order, _, _, _) in enumerate(streams):
        keep_at[i, 0] = 0
        for t, bit in enumerate(bits_of(depth, order)):
            half = row_count >> (t + 1)
            keep_at[i, t + 1] = keep_at[i, t] + lax.rem(row_rank // (1 << bit), 2) * half

    def give_at(i, t):
        return 2 * keep_at[i, t] + (row_count >> (t + 1)) - keep_at[i, t + 1]

    def slots_of(i):
        return pl.ds(streams[i][1], streams[i][2])

    def tile_at(i, c, p):
        order, slot, _, _ = streams[i]
        owner = 0
        for t, bit in enumerate(bits_of(depth, order)):
            owner = owner + lax.rem(p // (1 << (depth - 1 - t)), 2) * (1 << bit)
        return slot_ref[owner * cap + slot + c]

    def pair_copy(i):
        part = slots_of(i)
        return swap_copy(
            pair_out.at[part], pair_in.at[part], pair_send.at[i], pair_recv.at[i], other_core
        )

    def pair_start(i):
        for c in range(streams[i][2]):

            def body(p, carry, c=c):
                index = tile_at(i, c, p)
                value = peer_ref[jnp.maximum(index, 0)]
                pair_out[streams[i][1] + c, p] = jnp.where(index >= 0, value, jnp.zeros_like(value))
                return carry

            lax.fori_loop(0, row_count, body, 0, unroll=8)
        pair_copy(i).start()

    def tree_copy(i, t):
        order = streams[i][0]
        half = row_count >> (t + 1)
        part = pl.ds(row_count - (row_count >> t), half)
        here = slots_of(i)
        return swap_copy(
            staged.at[here, part], arrived.at[here, part], tree_send.at[i, t], tree_recv.at[i, t],
            (flip(row_rank, bits_of(depth, order)[t]), part_rank),
        )

    def pair_end(i):
        pair_copy(i).wait()
        _, slot, size, _ = streams[i]

        def value_at(c, p):
            index = tile_at(i, c, p)
            value = own_ref[jnp.maximum(index, 0)]
            return jnp.where(index >= 0, value, 0.0) + pair_in[slot + c, p].astype(F32)

        for c in range(size):

            def give(p, carry, c=c):
                staged[slot + c, p] = value_at(c, give_at(i, 0) + p).astype(BF16)
                return carry

            lax.fori_loop(0, row_count // 2, give, 0, unroll=8)
        tree_copy(i, 0).start()
        for c in range(size):

            def keep(p, carry, c=c):
                sums[slot + c, keep_at[i, 1] + p] = value_at(c, keep_at[i, 1] + p)
                return carry

            lax.fori_loop(0, row_count // 2, keep, 0, unroll=8)

    def tree_step(i, t):
        came = row_count - (row_count >> t)
        tree_copy(i, t).wait()
        low = keep_at[i, t + 1]
        here = slots_of(i)

        def values(k, size):
            return sums[here, pl.ds(k, size)] + arrived[here, pl.ds(came + k - low, size)].astype(F32)

        if t + 1 < depth:
            half = row_count >> (t + 2)
            at = row_count - (row_count >> (t + 1))
            staged[here, at : at + half] = values(give_at(i, t + 1), half).astype(BF16)
            tree_copy(i, t + 1).start()
            k = keep_at[i, t + 2]
            sums[here, pl.ds(k, half)] = values(k, half)
        else:
            tile_out_ref[here] = values(low, 1)[:, 0]

    loads[0].wait()
    for i in range(wide):
        pair_start(i)
    output_copy = swap_copy(output_ref, output_in, output_sem.at[0], output_sem.at[1], other_core)
    loads[1].wait()
    for i in range(wide):
        pair_end(i)

    for load in loads[2:]:
        load.wait()
    output_copy.start()
    await_from_all(tile, landed, sum_send, sum_recv, count, parts, me)
    back = add_landed(tile[...], landed, count)
    gain_mean = from_tile(back, 0, groups) * (1.0 / node_total)
    shift_mean = from_tile(back, 1, groups) * (1.0 / node_total)
    centre = stat_ref[0:1] / node_total
    inv_std = lax.rsqrt(stat_ref[1:2] / node_total - centre * centre + norm_eps)
    factor = params_ref[27:28] * inv_std
    grad_ref[...] = (
        factor * (dres_ref[...] - shift_mean - (filt_ref[...] - centre) * inv_std * gain_mean)
    ).astype(BF16)

    blocks = rows // block
    span = block + 2 * HALO
    has_before = me > 0
    has_after = me < count - 1

    def rim_low():
        return swap_copy(
            rim_ref.at[0], rim_in.at[1], rim_sem.at[0, 0], rim_sem.at[1, 1],
            device_of(jnp.maximum(me - 1, 0), parts),
        )

    def rim_high():
        return swap_copy(
            rim_ref.at[1], rim_in.at[0], rim_sem.at[0, 1], rim_sem.at[1, 0],
            device_of(jnp.minimum(me + 1, count - 1), parts),
        )

    def finish_rows(low, size):
        input_grad_ref[pl.ds(first + low, size), :] = (
            dres_ref[low : low + size] + total_ref[HALO + low : HALO + low + size]
        )

    late = rows - block - HALO

    def out_copy(i):
        low, size = ((late, rows - late), (0, late))[i]
        here = input_grad_ref.at[pl.ds(first + low, size)]
        return swap_copy(here, here, out_sem.at[0, i], out_sem.at[1, i], other_core)

    group = 3
    points = TAPS // group
    schedule = {}
    for i, (_, _, _, place) in enumerate(streams):
        for t in range(depth):
            due = 10 + 8 * place + 9 * t
            schedule.setdefault(min(due, blocks * points), []).append((due, t, i))

    def step(it, carry):
        b = lax.rem(it * (blocks - 1), blocks)
        base = pl.multiple_of(b * block, block)
        window = pl.ds(base, span)
        place = near_ref[0:TAPS, pl.ds(base, block)]
        place = place + lax.broadcasted_iota(jnp.int32, place.shape, 1) // LANES * LANES
        row = lax.broadcasted_iota(jnp.int32, (span, block), 0)
        grad = grad_ref[pl.ds(base, block), :]
        for point in range(points):
            total = total_ref[window, :]
            tokens = ext_ref[window, :].astype(F32)
            for k in range(point * group, (point + 1) * group):
                hot = (place[k : k + 1, :] == row).astype(F32).astype(BF16)
                spread = dot_plain(hot, grad)
                total += spread * params_ref[k : k + 1, :]
                small_out_ref[k : k + 1, :] += col_sum(spread * tokens)
            total_ref[window, :] = total
            for s in range(blocks):
                if s * points + point in schedule:

                    @pl.when(it == s)
                    def _(s=s, point=point):
                        for _, t, i in sorted(schedule[s * points + point]):
                            tree_step(i, t)

        @pl.when(it == 1)
        def _():
            rim_ref[0] = total_ref[0:HALO].astype(BF16)
            rim_ref[1] = total_ref[rows + HALO : rows + 2 * HALO].astype(BF16)

            @pl.when(has_before)
            def _():
                rim_low().start()

            @pl.when(has_after)
            def _():
                rim_high().start()

        @pl.when(it == 2)
        def _():
            @pl.when(has_before)
            def _():
                rim_low().wait_send()
                rim_high().wait_recv()
                total_ref[HALO : 2 * HALO] += rim_in[0].astype(F32)

            @pl.when(has_after)
            def _():
                rim_high().wait_send()
                rim_low().wait_recv()
                total_ref[rows : rows + HALO] += rim_in[1].astype(F32)

            finish_rows(late, rows - late)
            out_copy(0).start()

        return carry

    lax.fori_loop(0, blocks, step, 0)

    flat[...] = jnp.zeros_like(flat)
    for r in range(small_rows):
        row = small_out_ref[r : r + 1, :] if r < TAPS else small_ref[r : r + 1, :]
        for g in range(groups):
            at = r * groups + g
            flat[at // 8, at % 8 : at % 8 + 1, :] = row[:, g * LANES : (g + 1) * LANES]
    send_to_all(lambda other: flat.at[other], flat_in, flat_send, flat_recv, count, parts, me)
    finish_rows(0, late)
    out_copy(1).start()
    await_from_all(flat.at[0], flat_in, flat_send, flat_recv, count, parts, me)
    part_sum[...] = add_landed(flat[me], flat_in, count)
    send_to_all(lambda other: part_sum, flat_all, all_send, all_recv, count, parts, me)
    for _, t, i in sorted(schedule.get(blocks * points, [])):
        tree_step(i, t)
    await_from_all(part_sum, flat_all, all_send, all_recv, count, parts, me)
    flat_all[0] = part_sum[...]
    for r in range(small_rows):
        for g in range(groups):
            at = r * groups + g
            tile_from = lax.rem(at // 8 - me + count, count)
            small_out_ref[r : r + 1, g * LANES : (g + 1) * LANES] = flat_all[
                tile_from, at % 8 : at % 8 + 1, :
            ]
    output_copy.wait()
    out_copy(0).wait()
    out_copy(1).wait()


def filter_backward(
    slots, extended, filtered, dres, near_t, params, stat, small, own_grad, peer_grad, output, cap,
    row_count, parts, block=256
):
    rows, width = filtered.shape
    count = row_count * parts
    depth = row_count.bit_length() - 1
    wide = len(streams_of(cap, depth))
    vmem = pl.BlockSpec(memory_space=pltpu.VMEM)
    anywhere = pl.BlockSpec(memory_space=pl.ANY)
    dma = pltpu.SemaphoreType.DMA
    of_streams = (cap, row_count, BR, width)
    return pl.pallas_call(
        functools.partial(
            filter_back_kernel, block=block, row_count=row_count, parts=parts, cap=cap,
            node_total=rows * count,
        ),
        in_specs=[pl.BlockSpec(memory_space=pltpu.SMEM)]
        + [anywhere] * 3
        + [vmem] * 4
        + [anywhere] * 3,
        out_specs=[vmem] * 4,
        out_shape=[
            jax.ShapeDtypeStruct((rows * parts, width), F32),
            jax.ShapeDtypeStruct((rows, width), F32),
            jax.ShapeDtypeStruct(params.shape, F32),
            jax.ShapeDtypeStruct((cap, BR, width), F32),
        ],
        scratch_shapes=[
            pltpu.VMEM(extended.shape, BF16),
            pltpu.VMEM(filtered.shape, F32),
            pltpu.VMEM(dres.shape, F32),
            pltpu.VMEM(own_grad.shape, F32),
            pltpu.VMEM(peer_grad.shape, BF16),
            pltpu.VMEM(output.shape, F32),
            pltpu.VMEM(of_streams, BF16),
            pltpu.VMEM(of_streams, BF16),
            pltpu.VMEM(of_streams, F32),
            pltpu.VMEM(of_streams, BF16),
            pltpu.VMEM(of_streams, BF16),
            pltpu.VMEM((rows + 2 * HALO, width), F32),
            pltpu.VMEM((rows, width), BF16),
            pltpu.VMEM((2, HALO, width), BF16),
            pltpu.VMEM((2, HALO, width), BF16),
            pltpu.VMEM((8, LANES), F32),
            pltpu.VMEM((count, 8, LANES), F32),
            pltpu.VMEM((count, 8, LANES), F32),
            pltpu.VMEM((count, 8, LANES), F32),
            pltpu.VMEM((8, LANES), F32),
            pltpu.VMEM((count, 8, LANES), F32),
            dma((6,)),
            dma((2,)),
            dma((wide,)),
            dma((wide,)),
            dma((count,)),
            dma((count,)),
            dma((wide, depth)),
            dma((wide, depth)),
            dma((2, 2)),
            dma((count,)),
            dma((count,)),
            dma((count,)),
            dma((count,)),
            dma((2, 2)),
        ],
        compiler_params=pltpu.CompilerParams(
            collective_id=1, has_side_effects=True, vmem_limit_bytes=60 << 20
        ),
    )(
        slots, extended, filtered, dres, near_t, params, stat, small, own_grad, peer_grad, output
    )


def last_kernel(
    slot_ref, rank_ref, output_own, output_in, grad_in, weight_ref, params_ref, first_ref,
    second_ref, small_ref, tile_grad_ref, tile_first_ref, tile_second_ref,
    output_ref, input_grad_ref, weight_out, first_out, second_out, low_out, params_out,
    small_first_out, small_second_out,
    stage_ref, old_ref, copy_sem, tile_sem
):
    row_rank, part_rank = rank_ref[0], rank_ref[1]
    rows = output_own.shape[0]
    cap = tile_grad_ref.shape[0]
    cuts = 4
    copies = []
    size = rows // cuts
    for j in range(cuts):
        own_rows = pl.ds(part_rank * rows + j * size, size)
        other_rows = pl.ds((1 - part_rank) * rows + j * size, size)
        part = pl.ds(j * size, size)
        copies.append((output_own.at[part], output_ref.at[own_rows]))
        copies.append((output_in.at[part], output_ref.at[other_rows]))
        copies.append((grad_in.at[own_rows], input_grad_ref.at[own_rows]))
        copies.append((grad_in.at[other_rows], input_grad_ref.at[other_rows]))
    reads = [
        pltpu.make_async_copy(source, stage_ref.at[i], copy_sem.at[0, i])
        for i, (source, _) in enumerate(copies)
    ]
    writes = [
        pltpu.make_async_copy(stage_ref.at[i], landing, copy_sem.at[1, i])
        for i, (_, landing) in enumerate(copies)
    ]
    tiles = [slot_ref[row_rank * cap + c] for c in range(cap)]
    olds = [
        pltpu.make_async_copy(
            weight_ref.at[part_rank, pl.ds(pl.multiple_of(jnp.maximum(t, 0) * BR, BR), BR)],
            old_ref.at[c],
            tile_sem.at[c],
        )
        for c, t in enumerate(tiles)
    ]
    for copy in olds:
        copy.start()
    for copy in reads:
        copy.start()
    params_out[...], small_first_out[...], small_second_out[...] = adam_step(
        params_ref[...], small_ref[...], first_ref[...], second_ref[...], 0.0
    )
    for read, write in zip(reads, writes):
        read.wait()
        write.start()
    for c, t in enumerate(tiles):
        olds[c].wait()
        new = adam_step(
            old_ref[c].astype(F32), tile_grad_ref[c], tile_first_ref[0, c], tile_second_ref[0, c],
            decay_rate,
        )
        live = [jnp.where(t >= 0, a, 0.0) for a in new]
        weight_out[0, c] = live[0]
        first_out[0, c] = live[1]
        second_out[0, c] = live[2]
        low_out[0, c] = live[0].astype(BF16)
    for copy in writes:
        copy.wait()


def last_step(
    slots, ranks, output_own, output_in, input_grad, weights, params, small_first, small_second,
    small_sum, tile_grad, tile_first, tile_second
):
    vmem = pl.BlockSpec(memory_space=pltpu.VMEM)
    anywhere = pl.BlockSpec(memory_space=pl.ANY)
    smem = pl.BlockSpec(memory_space=pltpu.SMEM)
    full = jax.ShapeDtypeStruct(input_grad.shape, F32)
    tile = jax.ShapeDtypeStruct(tile_first.shape, F32)
    small = jax.ShapeDtypeStruct(params.shape, F32)
    return pl.pallas_call(
        last_kernel,
        in_specs=[smem, smem] + [anywhere] * 4 + [vmem] * 7,
        out_specs=[anywhere] * 2 + [vmem] * 7,
        out_shape=[
            full, full, tile, tile, tile, jax.ShapeDtypeStruct(tile_first.shape, BF16), small,
            small, small,
        ],
        scratch_shapes=[
            pltpu.VMEM((16, output_own.shape[0] // 4, output_own.shape[1]), F32),
            pltpu.VMEM(tile_grad.shape, BF16),
            pltpu.SemaphoreType.DMA((2, 16)),
            pltpu.SemaphoreType.DMA((tile_grad.shape[0],)),
        ],
        compiler_params=pltpu.CompilerParams(vmem_limit_bytes=60 << 20),
    )(
        slots, ranks, output_own, output_in, input_grad, weights, params, small_first, small_second,
        small_sum, tile_grad, tile_first, tile_second
    )


def block_kernel(
    rank_ref, filt_ref, tok_ref, mask_ref, cot_ref, stat_ref, params_ref, weight_ref,
    out_ref, dres_ref, own_ref, peer_ref, small_ref, grad_ref, *, node_total, parts, width, units, block
):
    i = pl.program_id(0)

    @pl.when(i == 0)
    def _():
        grad_ref[...] = jnp.zeros_like(grad_ref)
        small_ref[...] = jnp.zeros_like(small_ref)

    part = width // parts
    unit_part = units // parts
    scale = HEAD_DIM**-0.5

    def weight_rows(low, count):
        return jnp.concatenate([weight_ref[h, low : low + count] for h in range(parts)], axis=0)

    def qkv_rows(j):
        return weight_rows(j * part, part)

    def proj_rows():
        return weight_rows(3 * part, part)

    def add_grad(low, value):
        for h in range(parts):
            grad_ref[h, low : low + part] += value[h * part : (h + 1) * part]

    def param(row):
        return params_ref[row : row + 1, :]

    def add_small(row, value):
        small_ref[row : row + 1, :] += value

    centre = stat_ref[0:1] / node_total
    inv_std = lax.rsqrt(stat_ref[1:2] / node_total - centre * centre + norm_eps)
    bn_norm = (filt_ref[...] - centre) * inv_std
    resid = tok_ref[...].astype(F32) + (bn_norm * param(27) + param(28))
    unit_one, factor_one = layer_norm(resid)
    normed_one = (unit_one * param(29) + param(30)).astype(BF16)
    query = ((dot_last(normed_one, qkv_rows(0)) + param(35)) * scale).astype(BF16)
    key = (dot_last(normed_one, qkv_rows(1)) * scale).astype(BF16)
    value = ((dot_last(normed_one, qkv_rows(2)) + param(36)) * scale).astype(BF16)

    side = LANES
    heads = LANES // HEAD_DIM
    groups = width // LANES
    lane_head = lax.broadcasted_iota(jnp.int32, (side, LANES), 1) // HEAD_DIM
    window_q = lax.broadcasted_iota(jnp.int32, (side, side), 0) // WIN
    window_k = lax.broadcasted_iota(jnp.int32, (side, side), 1) // WIN

    def stack_heads(a):
        return jnp.concatenate(
            [jnp.where(lane_head == j, a, jnp.zeros_like(a)) for j in range(heads)], axis=0
        )

    def pick_heads(a):
        picked = a[:side]
        for j in range(1, heads):
            picked = jnp.where(lane_head == j, a[j * side : (j + 1) * side], picked)
        return picked

    def cut(a, s, g):
        return a[s * side : (s + 1) * side, g * LANES : (g + 1) * LANES]

    sides = block // side
    pairs = [(s, g) for s in range(sides) for g in range(groups)]

    def join(pieces):
        return jnp.concatenate(
            [
                jnp.concatenate(pieces[s * groups : (s + 1) * groups], axis=1)
                for s in range(sides)
            ],
            axis=0,
        )

    keeps = [
        (window_q == window_k) & (mask_ref[0:1, s * side : (s + 1) * side] > 0)
        for s in range(sides)
    ]
    queries = [cut(query, s, g) for s, g in pairs]
    keys = [stack_heads(cut(key, s, g)) for s, g in pairs]
    values = [stack_heads(cut(value, s, g)) for s, g in pairs]
    scores = [dot_last(a, b) for a, b in zip(queries, keys)]
    probs = []
    for (s, _), score_all in zip(pairs, scores):
        here = []
        for j in range(heads):
            score = jnp.where(keeps[s], score_all[:, j * side : (j + 1) * side], masked_score)
            power = jnp.exp(score - jnp.max(score, axis=1, keepdims=True))
            here.append(power * (1.0 / jnp.sum(power, axis=1, keepdims=True)))
        probs.append(jnp.concatenate(here, axis=1))
    probs_low = [p.astype(BF16) for p in probs]
    mixture = join([dot_plain(p, v) for p, v in zip(probs_low, values)]).astype(BF16)
    after = resid + (dot_plain(mixture, proj_rows()) + param(33))
    unit_two, factor_two = layer_norm(after)
    normed_two = (unit_two * param(31) + param(32)).astype(BF16)

    cotangent = cot_ref[...]
    grad_ffn = cotangent.astype(BF16)
    ffn = jnp.zeros_like(after)
    grad_normed_two = jnp.zeros_like(after)
    chunk = unit_part
    for h in range(parts):
        for c in range(unit_part // chunk):
            low = 4 * part + c * chunk
            unit = 37 + (h * unit_part + c * chunk) // width
            bias_rows = range(unit, unit + chunk // width)
            fc1 = weight_ref[h, low : low + chunk]
            fc2 = weight_ref[h, low + unit_part : low + unit_part + chunk]
            hidden = dot_last(normed_two, fc1) + jnp.concatenate(
                [param(r) for r in bias_rows], axis=1
            )
            cumulative = 0.5 * (1.0 + lax.erf(hidden * 0.5**0.5))
            activation = (hidden * cumulative).astype(BF16)
            density = jnp.exp(-0.5 * hidden * hidden) * (2.0 * jnp.pi) ** (-0.5)
            ffn += dot_plain(activation, fc2)
            grad_hidden = (
                dot_last(grad_ffn, fc2) * (cumulative + hidden * density)
            ).astype(BF16)
            grad_normed_two += dot_plain(grad_hidden, fc1)
            grad_ref[h, low : low + chunk] += dot_first(grad_hidden, normed_two)
            grad_ref[h, low + unit_part : low + unit_part + chunk] += dot_first(activation, grad_ffn)
            bias_sum = col_sum(grad_hidden.astype(F32))
            for j, r in enumerate(bias_rows):
                add_small(r, bias_sum[:, j * width : (j + 1) * width])
    out_ref[...] = after + (ffn + param(34))
    add_small(34, col_sum(grad_ffn.astype(F32)))

    grad_after = cotangent + norm_back(grad_normed_two, unit_two, factor_two, param(31))
    add_small(31, col_sum(grad_normed_two * unit_two))
    add_small(32, col_sum(grad_normed_two))
    grad_branch = grad_after.astype(BF16)
    add_grad(3 * part, dot_first(mixture, grad_branch))
    add_small(33, col_sum(grad_branch.astype(F32)))
    grad_mixture = dot_last(grad_branch, proj_rows()).astype(BF16)

    grad_mix = [cut(grad_mixture, s, g) for s, g in pairs]
    grad_probs = [dot_last(a, v) for a, v in zip(grad_mix, values)]
    grad_values = [pick_heads(dot_first(p, a)) for p, a in zip(probs_low, grad_mix)]
    grad_scores = []
    for prob_all, grad_all in zip(probs, grad_probs):
        here = []
        for j in range(heads):
            prob = prob_all[:, j * side : (j + 1) * side]
            term = prob * grad_all[:, j * side : (j + 1) * side]
            here.append((term - prob * jnp.sum(term, axis=1, keepdims=True)).astype(BF16))
        grad_scores.append(jnp.concatenate(here, axis=1))
    grad_queries = [dot_plain(a, k) for a, k in zip(grad_scores, keys)]
    grad_keys = [pick_heads(dot_first(a, q)) for a, q in zip(grad_scores, queries)]
    grad_qkv = [join(kind).astype(BF16) for kind in (grad_queries, grad_keys, grad_values)]
    grad_normed_one = jnp.zeros_like(resid)
    for j in range(3):
        grad_normed_one += dot_plain(grad_qkv[j], qkv_rows(j))
        add_grad(j * part, scale * dot_first(grad_qkv[j], normed_one))
    grad_normed_one = scale * grad_normed_one
    add_small(35, scale * col_sum(grad_qkv[0].astype(F32)))
    add_small(36, scale * col_sum(grad_qkv[2].astype(F32)))
    dres = grad_after + norm_back(grad_normed_one, unit_one, factor_one, param(29))
    add_small(29, col_sum(grad_normed_one * unit_one))
    add_small(30, col_sum(grad_normed_one))
    add_small(27, col_sum(dres * bn_norm))
    add_small(28, col_sum(dres))
    dres_ref[...] = dres

    @pl.when(i == pl.num_programs(0) - 1)
    def _():
        mine = lax.axis_index("heads")
        own_ref[...] = grad_ref[mine]
        peer_ref[...] = grad_ref[1 - mine].astype(BF16)


def block_step(filtered, tokens, mask, cotangent, stat, params, weights, node_total, block=512):
    rows, width = filtered.shape
    parts = weights.shape[0]
    units = (weights.shape[1] - 4 * (width // parts)) // 2 * parts
    blocks = rows // block
    outs = [
        jax.ShapeDtypeStruct((rows, width), F32),
        jax.ShapeDtypeStruct((rows, width), F32),
        jax.ShapeDtypeStruct(weights.shape[1:], F32),
        jax.ShapeDtypeStruct(weights.shape[1:], BF16),
        jax.ShapeDtypeStruct(params.shape, F32),
    ]

    def whole(shape):
        zeros = (0,) * len(shape)
        return pl.BlockSpec(shape, lambda i, rank: zeros)

    here = pl.BlockSpec((block, width), lambda i, rank: (i, 0))
    chip = pl.BlockSpec((block, width), lambda i, rank: (rank[0] * blocks + i, 0))
    return pl.pallas_call(
        functools.partial(
            block_kernel, node_total=node_total, parts=parts, width=width, units=units, block=block
        ),
        grid_spec=pltpu.PrefetchScalarGridSpec(
            num_scalar_prefetch=1,
            grid=(blocks,),
            in_specs=[
                here,
                chip,
                pl.BlockSpec((1, block), lambda i, rank: (0, rank[0] * blocks + i)),
                chip,
                whole(stat.shape),
                whole(params.shape),
                whole(weights.shape),
            ],
            out_specs=[here, here] + [whole(o.shape) for o in outs[2:]],
            scratch_shapes=[pltpu.VMEM(weights.shape, F32)],
        ),
        out_shape=outs,
        compiler_params=pltpu.CompilerParams(vmem_limit_bytes=60 << 20),
    )(lax.axis_index("heads").reshape(1), filtered, tokens, mask, cotangent, stat, params, weights)


def local(
    tokens_in, neighbours, scene_lengths, window_mask, small_params, qkv_weight, proj_weight,
    fc1_weight, fc2_weight, cotangent, owners, small_first, small_second, tile_first, tile_second
):
    rows_here, width = tokens_in.shape
    row_count = lax.axis_size("rows")
    parts = lax.axis_size("heads")
    row_rank = lax.axis_index("rows")
    part_rank = lax.axis_index("heads")
    rows = rows_here // parts
    node_total = rows_here * row_count
    tile_count = owners.shape[0]
    slot_cap = tile_first.shape[1]

    filtered, stat, near_t, extended, weights = filter_forward(
        scene_lengths, tokens_in, neighbours.T, small_params, qkv_weight, proj_weight, fc1_weight,
        fc2_weight, row_count, parts
    )
    output, dres, own_grad, peer_grad, small_grad = block_step(
        filtered, tokens_in, window_mask[None], cotangent, stat, small_params, weights, node_total
    )

    tile_order = jnp.arange(tile_count, dtype=jnp.int32)
    same_owner = (owners[:, None] == owners[None, :]) & (tile_order[None, :] < tile_order[:, None])
    slot_of = owners * slot_cap + jnp.sum(same_owner.astype(jnp.int32), axis=1)
    slot_ids = jnp.arange(row_count * slot_cap, dtype=jnp.int32)
    found = slot_of[None, :] == slot_ids[:, None]
    slot_tile = jnp.max(jnp.where(found, tile_order[None, :], -1), axis=1)

    input_grad, output_in, small_sum, tile_grad = filter_backward(
        slot_tile, extended, filtered, dres, near_t, small_params, stat, small_grad,
        own_grad.reshape(tile_count, BR, width), peer_grad.reshape(tile_count, BR, width), output,
        slot_cap, row_count, parts
    )
    return last_step(
        slot_tile, jnp.stack([row_rank, part_rank]), output, output_in, input_grad, weights,
        small_params, small_first, small_second, small_sum, tile_grad, tile_first, tile_second
    )


def solution(mesh):
    return jax.shard_map(
        local,
        mesh=mesh,
        in_specs=(
            P("rows", None),
            P("rows", None),
            P(),
            P("rows"),
            P(),
            P(None, "heads", None),
            P("heads", None),
            P("heads", None),
            P("heads", None),
            P("rows", None),
            P(),
            P(),
            P(),
            P("heads", "rows", None, None),
            P("heads", "rows", None, None),
        ),
        out_specs=(
            P("rows", None),
            P("rows", None),
            P("heads", "rows", None, None),
            P("heads", "rows", None, None),
            P("heads", "rows", None, None),
            P("heads", "rows", None, None),
            P(),
            P(),
            P(),
        ),
        check_vma=False,
    )
```

```python
import functools

import jax
import jax.numpy as jnp
from jax import lax
from jax.experimental import pallas as pl
from jax.experimental.pallas import tpu as pltpu
from jax.sharding import PartitionSpec as P

HEAD_DIM = 32
WIN = 32
HALO = 128
BR = 16
STEP = 3
TAPS = 27
LANES = 128

norm_eps = 1e-05
adam_rate = 0.05
beta_one = 0.5
beta_two = 0.5
adam_eps = 1e-08
decay_rate = 0.05
masked_score = -1e30

F32 = jnp.float32
BF16 = jnp.bfloat16


def adam_step(weight, gradient, first_moment, second_moment, decay_factor):
    first_new = beta_one * first_moment + (1.0 - beta_one) * gradient
    second_new = beta_two * second_moment + (1.0 - beta_two) * gradient * gradient
    first_hat = first_new / (1.0 - beta_one**STEP)
    second_hat = second_new / (1.0 - beta_two**STEP)
    weight_new = weight - adam_rate * (
        first_hat / (jnp.sqrt(second_hat) + adam_eps) + decay_factor * weight
    )
    return (weight_new, first_new, second_new)


def dot_plain(a, b):
    return jnp.dot(a, b, preferred_element_type=F32)


def dot_last(a, b):
    return lax.dot_general(a, b, (((1,), (1,)), ((), ())), preferred_element_type=F32)


def dot_first(a, b):
    return lax.dot_general(a, b, (((0,), (0,)), ((), ())), preferred_element_type=F32)


def col_sum(v):
    return jnp.sum(v, axis=0, keepdims=True)


def layer_norm(v):
    centre = v - jnp.mean(v, axis=1, keepdims=True)
    factor = lax.rsqrt(jnp.mean(centre * centre, axis=1, keepdims=True) + norm_eps)
    return centre * factor, factor


def norm_back(upstream, unit_part, factor, gain):
    scaled = upstream * gain
    return factor * (
        scaled
        - jnp.mean(scaled, axis=1, keepdims=True)
        - unit_part * jnp.mean(scaled * unit_part, axis=1, keepdims=True)
    )


def full_spec(shape):
    zeros = (0,) * len(shape)
    return pl.BlockSpec(shape, lambda i: zeros)


MESH = pl.DeviceIdType.MESH


def device_of(index, parts):
    return (index // parts, lax.rem(index, parts))


def greet_all(count, parts, me):
    barrier = pltpu.get_barrier_semaphore()

    def greet(j, carry):
        pl.semaphore_signal(
            barrier, inc=1, device_id=device_of(lax.rem(me + j, count), parts), device_id_type=MESH
        )
        return carry

    lax.fori_loop(1, count, greet, 0)


def await_all(count):
    pl.semaphore_wait(pltpu.get_barrier_semaphore(), count - 1)


def swap_copy(source, landing, send_sem, recv_sem, device):
    return pltpu.make_async_remote_copy(
        src_ref=source, dst_ref=landing, send_sem=send_sem, recv_sem=recv_sem,
        device_id=device, device_id_type=MESH,
    )


def send_to_all(source_of, landing, send_sem, recv_sem, count, parts, me):
    def send(j, carry):
        other = lax.rem(me + j, count)
        swap_copy(
            source_of(other), landing.at[count - j], send_sem.at[j], recv_sem.at[count - j],
            device_of(other, parts),
        ).start()
        return carry

    lax.fori_loop(1, count, send, 0)


def await_from_all(source, landing, send_sem, recv_sem, count, parts, me):
    def wait(j, carry):
        swap_copy(
            source, landing.at[count - j], send_sem.at[j], recv_sem.at[count - j],
            device_of(lax.rem(me + j, count), parts),
        ).wait()
        return carry

    lax.fori_loop(1, count, wait, 0)


def add_landed(own, landing, count):
    return lax.fori_loop(1, count, lambda j, total: total + landing[j], own)


def to_tile(tile_ref, rows):
    tile_ref[...] = jnp.zeros_like(tile_ref)
    groups = rows[0].shape[1] // LANES
    for r, row in enumerate(rows):
        for g in range(groups):
            at = r * groups + g
            tile_ref[at : at + 1, :] = row[:, g * LANES : (g + 1) * LANES]


def from_tile(tile, row, groups):
    at = row * groups
    return jnp.concatenate([tile[at + g : at + g + 1, :] for g in range(groups)], axis=1)


def streams_of(cap, depth):
    seventh = cap // 7 if depth > 2 else 0
    rest = cap - 2 * seventh
    sizes = [
        (0, 0, rest // 2 // 2), (1, 0, (rest - rest // 2) // 2), (2, 0, seventh),
        (0, 1, rest // 2 - rest // 2 // 2), (1, 1, (rest - rest // 2) - (rest - rest // 2) // 2),
        (3, 0, seventh),
    ]
    streams = []
    slot = 0
    for order, place, size in sizes:
        if size:
            streams.append((order, slot, size, place))
            slot += size
    return streams


def bits_of(depth, order):
    bits = list(range(depth))
    if order == 1 and depth > 1:
        bits[:2] = [1, 0]
    if order == 2:
        bits[:3] = [2, 0, 1]
    if order == 3:
        bits[:3] = [2, 1, 0]
    return bits


def flip(rank, bit):
    weight = 1 << bit
    return rank + weight - 2 * weight * lax.rem(rank // weight, 2)


def step_kernel(
    lengths_ref, slot_ref, tokens_hbm, near_hbm, cot_hbm, qkv_hbm, proj_hbm, fc1_hbm, fc2_hbm,
    tile_first_hbm, tile_second_hbm, mask_ref, params_ref, small_first_ref, small_second_ref,
    output_ref, input_grad_ref, weight_out, first_out, second_out, low_out, params_out,
    small_first_out, small_second_out,
    near_in, near_t, ext_ref, filt_ref, stat_ref, stack_ref, cot_ref, stack_grad, small_ref,
    total_ref, grad_ref, rim_ref, rim_in, pair_in, staged, arrived, sums, tile_sum, tile_first_ref,
    tile_second_ref, tile, landed, back_tile, back_landed, flat, flat_in, part_sum, flat_all,
    local_sem, side_sem, weight_sem, stat_send, stat_recv, back_send, back_recv, pair_send,
    pair_recv, tree_send, tree_recv, rim_sem, flat_send, flat_recv, all_send, all_recv, out_sem,
    *, filter_block, row_block, back_block, row_count, parts, cap, scenes
):
    row_rank = lax.axis_index("rows")
    part_rank = lax.axis_index("heads")
    count = row_count * parts
    me = row_rank * parts + part_rank
    other_core = (row_rank, 1 - part_rank)
    rows_here, width = tokens_hbm.shape
    rows = rows_here // parts
    first = part_rank * rows
    node_total = rows_here * row_count
    groups = width // LANES
    part = width // parts
    unit_part = fc1_hbm.shape[0] * BR
    depth = row_count.bit_length() - 1
    streams = streams_of(cap, depth)
    wide = len(streams)
    small_rows = params_ref.shape[0]
    scale = HEAD_DIM**-0.5
    greet_all(count, parts, me)

    own_copy = pltpu.make_async_copy(
        tokens_hbm.at[pl.ds(first, rows)], ext_ref.at[pl.ds(HALO, rows)], local_sem.at[0]
    )
    near_copy = pltpu.make_async_copy(
        near_hbm.at[:, pl.ds(pl.multiple_of(first, LANES), rows)], near_in, local_sem.at[1]
    )
    late_copies = [
        pltpu.make_async_copy(cot_hbm.at[pl.ds(first, rows)], cot_ref, local_sem.at[3]),
        pltpu.make_async_copy(tile_first_hbm, tile_first_ref, local_sem.at[4]),
        pltpu.make_async_copy(tile_second_hbm, tile_second_ref, local_sem.at[5]),
    ]
    own_copy.start()
    near_copy.start()
    low_side = ext_ref.at[pl.ds(0, HALO)]
    high_side = ext_ref.at[pl.ds(rows + HALO, HALO)]

    @pl.when(part_rank == 0)
    def _():
        pltpu.make_async_copy(tokens_hbm.at[pl.ds(rows, HALO)], high_side, local_sem.at[2]).start()

    @pl.when(part_rank == 1)
    def _():
        pltpu.make_async_copy(
            tokens_hbm.at[pl.ds(rows - HALO, HALO)], low_side, local_sem.at[2]
        ).start()

    @pl.when(me == 0)
    def _():
        ext_ref[0:HALO, :] = jnp.zeros((HALO, width), BF16)

    @pl.when(me == count - 1)
    def _():
        ext_ref[rows + HALO :, :] = jnp.zeros((HALO, width), BF16)

    pieces = []
    low = 0
    for ref in (qkv_hbm, proj_hbm, fc1_hbm, fc2_hbm):
        pieces.append((ref, low, ref.shape[0]))
        low += ref.shape[0]

    def own_weight(i):
        ref, at, size = pieces[i]
        return pltpu.make_async_copy(
            ref, stack_ref.at[part_rank, pl.ds(at, size)], weight_sem.at[0, i]
        )

    def sent_weight(i):
        _, at, size = pieces[i]
        here = stack_ref.at[part_rank, pl.ds(at, size)]
        return swap_copy(here, here, weight_sem.at[1, i], weight_sem.at[2, i], other_core)

    for i in range(len(pieces)):
        own_weight(i).start()
    for copy in late_copies:
        copy.start()

    def side_up():
        return swap_copy(
            tokens_hbm.at[pl.ds(rows_here - HALO, HALO)], low_side, side_sem.at[0], side_sem.at[1],
            (jnp.minimum(row_rank + 1, row_count - 1), part_rank),
        )

    def side_down():
        return swap_copy(
            tokens_hbm.at[pl.ds(0, HALO)], high_side, side_sem.at[0], side_sem.at[1],
            (jnp.maximum(row_rank - 1, 0), part_rank),
        )

    stat_ref[...] = jnp.zeros_like(stat_ref)
    stack_grad[...] = jnp.zeros_like(stack_grad)
    small_ref[...] = jnp.zeros_like(small_ref)
    total_ref[...] = jnp.zeros_like(total_ref)
    ends = []
    reached = 0
    for s in range(scenes):
        reached = reached + lengths_ref[s]
        ends.append(reached * WIN)
    near_copy.wait()
    own_copy.wait()

    block = filter_block
    blocks = rows // block
    span = block + 2 * HALO

    def filter_step(it, carry):
        @pl.when(it == 2)
        def _():
            await_all(count)

            @pl.when((part_rank == 0) & (row_rank < row_count - 1))
            def _():
                side_up().start()

            @pl.when((part_rank == 1) & (row_rank > 0))
            def _():
                side_down().start()

            for i in range(len(pieces)):
                own_weight(i).wait()
                sent_weight(i).start()

        @pl.when(it == blocks - 2)
        def _():
            pltpu.make_async_copy(
                tokens_hbm.at[pl.ds(0, HALO)], low_side, local_sem.at[2]
            ).wait()

            @pl.when((part_rank == 0) & (row_rank < row_count - 1))
            def _():
                side_up().wait_send()

            @pl.when((part_rank == 0) & (row_rank > 0))
            def _():
                side_up().wait_recv()

            @pl.when((part_rank == 1) & (row_rank > 0))
            def _():
                side_down().wait_send()

            @pl.when((part_rank == 1) & (row_rank < row_count - 1))
            def _():
                side_down().wait_recv()

        b = lax.rem(it + 1, blocks)
        base = pl.multiple_of(b * block, block)
        window = ext_ref[pl.ds(base, span), :]
        near = near_in[:, pl.ds(base, block)]
        lane = lax.broadcasted_iota(jnp.int32, (1, block), 1)
        own_row = row_rank * rows_here + first + base + lane
        scene_low = jnp.zeros_like(own_row)
        scene_high = jnp.full_like(own_row, node_total)
        for end in ends:
            passed = own_row >= end
            scene_low = jnp.maximum(scene_low, jnp.where(passed, end, 0))
            scene_high = jnp.minimum(scene_high, jnp.where(passed, node_total, end))
        target = own_row + near
        usable = (near >= -HALO) & (target >= scene_low) & (target < scene_high)
        place_t = jnp.where(usable, near + lane + HALO, -8 * HALO)
        near_t[0:TAPS, pl.ds(base, block)] = place_t
        place = jnp.transpose(
            jnp.concatenate([place_t, jnp.zeros((LANES - TAPS, block), jnp.int32)], axis=0)
        )
        column = lax.broadcasted_iota(jnp.int32, (block, span), 1)
        total = jnp.zeros((block, width), F32)
        group = 3
        for k0 in range(0, TAPS, group):
            hot = jnp.concatenate(
                [
                    (place[:, k : k + 1] == column).astype(F32).astype(BF16)
                    for k in range(k0, k0 + group)
                ],
                axis=0,
            )
            picked = dot_plain(hot, window)
            for j in range(group):
                total += picked[j * block : (j + 1) * block] * params_ref[k0 + j : k0 + j + 1, :]
        filt_ref[pl.ds(base, block), :] = total
        stat_ref[0:1, :] += col_sum(total)
        stat_ref[1:2, :] += col_sum(total * total)
        return carry

    lax.fori_loop(0, blocks, filter_step, 0)

    to_tile(tile, [stat_ref[0:1], stat_ref[1:2]])
    send_to_all(lambda other: tile, landed, stat_send, stat_recv, count, parts, me)
    for i in range(len(pieces)):
        sent_weight(i).wait()
    late_copies[0].wait()
    await_from_all(tile, landed, stat_send, stat_recv, count, parts, me)
    stat = add_landed(tile[...], landed, count)
    centre = from_tile(stat, 0, groups) / node_total
    inv_std = lax.rsqrt(from_tile(stat, 1, groups) / node_total - centre * centre + norm_eps)
    stat_ref[0:1, :] = centre
    stat_ref[1:2, :] = inv_std

    def weight_part(h, low, size):
        return stack_ref[h, low // BR : (low + size) // BR].reshape(size, width)

    def weight_rows(low, size):
        return jnp.concatenate([weight_part(h, low, size) for h in range(parts)], axis=0)

    def qkv_rows(j):
        return weight_rows(j * part, part)

    def proj_rows():
        return weight_rows(3 * part, part)

    def add_part(h, low, value):
        size = value.shape[0]
        stack_grad[h, low // BR : (low + size) // BR] += value.reshape(size // BR, BR, width)

    def add_grad(low, value):
        for h in range(parts):
            add_part(h, low, value[h * part : (h + 1) * part])

    def param(row):
        return params_ref[row : row + 1, :]

    def add_small(row, value):
        small_ref[row : row + 1, :] += value

    def out_copy(ref, sem, low, size):
        here = ref.at[pl.ds(pl.multiple_of(first + low, LANES), size)]
        return swap_copy(here, here, out_sem.at[0, sem], out_sem.at[1, sem], other_core)

    def row_step(it, carry):
        block = row_block
        base = pl.multiple_of(it * block, block)
        block_rows = pl.ds(base, block)
        there = pl.ds(pl.multiple_of(first + base, LANES), block)
        mask_at = (first + base) // LANES
        bn_norm = (filt_ref[block_rows, :] - stat_ref[0:1]) * stat_ref[1:2]
        resid = ext_ref[pl.ds(pl.multiple_of(base + HALO, HALO), block), :].astype(F32) + (
            bn_norm * param(27) + param(28)
        )
        unit_one, factor_one = layer_norm(resid)
        normed_one = (unit_one * param(29) + param(30)).astype(BF16)
        query = ((dot_last(normed_one, qkv_rows(0)) + param(35)) * scale).astype(BF16)
        key = (dot_last(normed_one, qkv_rows(1)) * scale).astype(BF16)
        value = ((dot_last(normed_one, qkv_rows(2)) + param(36)) * scale).astype(BF16)

        side = LANES
        heads = LANES // HEAD_DIM
        lane_head = lax.broadcasted_iota(jnp.int32, (side, LANES), 1) // HEAD_DIM
        window_q = lax.broadcasted_iota(jnp.int32, (side, side), 0) // WIN
        window_k = lax.broadcasted_iota(jnp.int32, (side, side), 1) // WIN

        def stack_heads(a):
            return jnp.concatenate(
                [jnp.where(lane_head == j, a, jnp.zeros_like(a)) for j in range(heads)], axis=0
            )

        def pick_heads(a):
            picked = a[:side]
            for j in range(1, heads):
                picked = jnp.where(lane_head == j, a[j * side : (j + 1) * side], picked)
            return picked

        def cut(a, s, g):
            return a[s * side : (s + 1) * side, g * LANES : (g + 1) * LANES]

        sides = block // side
        pairs = [(s, g) for s in range(sides) for g in range(groups)]

        def join(pieces):
            return jnp.concatenate(
                [
                    jnp.concatenate(pieces[s * groups : (s + 1) * groups], axis=1)
                    for s in range(sides)
                ],
                axis=0,
            )

        keeps = [
            (window_q == window_k) & (mask_ref[pl.ds(mask_at + s, 1), :] > 0)
            for s in range(sides)
        ]
        queries = [cut(query, s, g) for s, g in pairs]
        keys = [stack_heads(cut(key, s, g)) for s, g in pairs]
        values = [stack_heads(cut(value, s, g)) for s, g in pairs]
        scores = [dot_last(a, b) for a, b in zip(queries, keys)]
        probs = []
        for (s, _), score_all in zip(pairs, scores):
            here = []
            for j in range(heads):
                score = jnp.where(keeps[s], score_all[:, j * side : (j + 1) * side], masked_score)
                power = jnp.exp(score - jnp.max(score, axis=1, keepdims=True))
                here.append(power * (1.0 / jnp.sum(power, axis=1, keepdims=True)))
            probs.append(jnp.concatenate(here, axis=1))
        probs_low = [p.astype(BF16) for p in probs]
        mixture = join([dot_plain(p, v) for p, v in zip(probs_low, values)]).astype(BF16)
        after = resid + (dot_plain(mixture, proj_rows()) + param(33))
        unit_two, factor_two = layer_norm(after)
        normed_two = (unit_two * param(31) + param(32)).astype(BF16)

        cotangent = cot_ref[block_rows, :]
        grad_ffn = cotangent.astype(BF16)
        ffn = jnp.zeros_like(after)
        grad_normed_two = jnp.zeros_like(after)
        chunk = unit_part
        for h in range(parts):
            for c in range(unit_part // chunk):
                low = 4 * part + c * chunk
                unit = 37 + (h * unit_part + c * chunk) // width
                bias_rows = range(unit, unit + chunk // width)
                fc1 = weight_part(h, low, chunk)
                fc2 = weight_part(h, low + unit_part, chunk)
                hidden = dot_last(normed_two, fc1) + jnp.concatenate(
                    [param(r) for r in bias_rows], axis=1
                )
                cumulative = 0.5 * (1.0 + lax.erf(hidden * 0.5**0.5))
                activation = (hidden * cumulative).astype(BF16)
                density = jnp.exp(-0.5 * hidden * hidden) * (2.0 * jnp.pi) ** (-0.5)
                ffn += dot_plain(activation, fc2)
                grad_hidden = (
                    dot_last(grad_ffn, fc2) * (cumulative + hidden * density)
                ).astype(BF16)
                grad_normed_two += dot_plain(grad_hidden, fc1)
                add_part(h, low, dot_first(grad_hidden, normed_two))
                add_part(h, low + unit_part, dot_first(activation, grad_ffn))
                bias_sum = col_sum(grad_hidden.astype(F32))
                for j, r in enumerate(bias_rows):
                    add_small(r, bias_sum[:, j * width : (j + 1) * width])
        output_ref[there, :] = after + (ffn + param(34))
        add_small(34, col_sum(grad_ffn.astype(F32)))

        grad_after = cotangent + norm_back(grad_normed_two, unit_two, factor_two, param(31))
        add_small(31, col_sum(grad_normed_two * unit_two))
        add_small(32, col_sum(grad_normed_two))
        grad_branch = grad_after.astype(BF16)
        add_grad(3 * part, dot_first(mixture, grad_branch))
        add_small(33, col_sum(grad_branch.astype(F32)))
        grad_mixture = dot_last(grad_branch, proj_rows()).astype(BF16)

        grad_mix = [cut(grad_mixture, s, g) for s, g in pairs]
        grad_probs = [dot_last(a, v) for a, v in zip(grad_mix, values)]
        grad_values = [pick_heads(dot_first(p, a)) for p, a in zip(probs_low, grad_mix)]
        grad_scores = []
        for prob_all, grad_all in zip(probs, grad_probs):
            here = []
            for j in range(heads):
                prob = prob_all[:, j * side : (j + 1) * side]
                term = prob * grad_all[:, j * side : (j + 1) * side]
                here.append((term - prob * jnp.sum(term, axis=1, keepdims=True)).astype(BF16))
            grad_scores.append(jnp.concatenate(here, axis=1))
        grad_queries = [dot_plain(a, k) for a, k in zip(grad_scores, keys)]
        grad_keys = [pick_heads(dot_first(a, q)) for a, q in zip(grad_scores, queries)]
        grad_qkv = [join(kind).astype(BF16) for kind in (grad_queries, grad_keys, grad_values)]
        grad_normed_one = jnp.zeros_like(resid)
        for j in range(3):
            grad_normed_one += dot_plain(grad_qkv[j], qkv_rows(j))
            add_grad(j * part, scale * dot_first(grad_qkv[j], normed_one))
        grad_normed_one = scale * grad_normed_one
        add_small(35, scale * col_sum(grad_qkv[0].astype(F32)))
        add_small(36, scale * col_sum(grad_qkv[2].astype(F32)))
        dres = grad_after + norm_back(grad_normed_one, unit_one, factor_one, param(29))
        add_small(29, col_sum(grad_normed_one * unit_one))
        add_small(30, col_sum(grad_normed_one))
        add_small(27, col_sum(dres * bn_norm))
        add_small(28, col_sum(dres))
        input_grad_ref[there, :] = dres
        for s in range(rows // block):

            @pl.when(it == s)
            def _(s=s):
                out_copy(output_ref, s, s * block, block).start()

        return carry

    lax.fori_loop(0, rows // row_block, row_step, 0)

    to_tile(back_tile, [small_ref[27:28], small_ref[28:29]])
    send_to_all(lambda other: back_tile, back_landed, back_send, back_recv, count, parts, me)
    keep_at = {}
    for i, (order, _, _, _) in enumerate(streams):
        keep_at[i, 0] = 0
        for t, bit in enumerate(bits_of(depth, order)):
            half = row_count >> (t + 1)
            keep_at[i, t + 1] = keep_at[i, t] + lax.rem(row_rank // (1 << bit), 2) * half

    def give_at(i, t):
        return 2 * keep_at[i, t] + (row_count >> (t + 1)) - keep_at[i, t + 1]

    def slots_of(i):
        return pl.ds(streams[i][1], streams[i][2])

    def tile_at(i, c, p):
        order, slot, _, _ = streams[i]
        owner = 0
        for t, bit in enumerate(bits_of(depth, order)):
            owner = owner + lax.rem(p // (1 << (depth - 1 - t)), 2) * (1 << bit)
        return slot_ref[owner * cap + slot + c]

    def pair_copy(i):
        part = slots_of(i)
        return swap_copy(
            staged.at[part], pair_in.at[part], pair_send.at[i], pair_recv.at[i], other_core
        )

    def pair_start(i):
        for c in range(streams[i][2]):

            def body(p, carry, c=c):
                index = tile_at(i, c, p)
                value = stack_grad[1 - part_rank, jnp.maximum(index, 0)].astype(BF16)
                staged[streams[i][1] + c, p] = jnp.where(index >= 0, value, jnp.zeros_like(value))
                return carry

            lax.fori_loop(0, row_count, body, 0, unroll=8)
        pair_copy(i).start()

    def tree_copy(i, t):
        order = streams[i][0]
        half = row_count >> (t + 1)
        part = pl.ds(row_count - (row_count >> t), half)
        here = slots_of(i)
        return swap_copy(
            staged.at[here, part], arrived.at[here, part], tree_send.at[i, t], tree_recv.at[i, t],
            (flip(row_rank, bits_of(depth, order)[t]), part_rank),
        )

    def pair_end(i):
        pair_copy(i).wait()
        _, slot, size, _ = streams[i]

        def value_at(c, p):
            index = tile_at(i, c, p)
            value = stack_grad[part_rank, jnp.maximum(index, 0)]
            return jnp.where(index >= 0, value, 0.0) + pair_in[slot + c, p].astype(F32)

        for c in range(size):

            def give(p, carry, c=c):
                staged[slot + c, p] = value_at(c, give_at(i, 0) + p).astype(BF16)
                return carry

            lax.fori_loop(0, row_count // 2, give, 0, unroll=8)
        tree_copy(i, 0).start()
        for c in range(size):

            def keep(p, carry, c=c):
                sums[slot + c, keep_at[i, 1] + p] = value_at(c, keep_at[i, 1] + p)
                return carry

            lax.fori_loop(0, row_count // 2, keep, 0, unroll=8)

    def tree_step(i, t):
        came = row_count - (row_count >> t)
        tree_copy(i, t).wait()
        low = keep_at[i, t + 1]
        here = slots_of(i)

        def values(k, size):
            return sums[here, pl.ds(k, size)] + arrived[here, pl.ds(came + k - low, size)].astype(F32)

        if t + 1 < depth:
            half = row_count >> (t + 2)
            at = row_count - (row_count >> (t + 1))
            staged[here, at : at + half] = values(give_at(i, t + 1), half).astype(BF16)
            tree_copy(i, t + 1).start()
            k = keep_at[i, t + 2]
            sums[here, pl.ds(k, half)] = values(k, half)
        else:
            tile_sum[here] = values(low, 1)[:, 0]

    for i in range(wide):
        pair_start(i)
    for i in range(wide):
        pair_end(i)
    own_rows = pl.ds(pl.multiple_of(first, LANES), rows)
    await_from_all(back_tile, back_landed, back_send, back_recv, count, parts, me)
    back = add_landed(back_tile[...], back_landed, count)
    gain_mean = from_tile(back, 0, groups) * (1.0 / node_total)
    shift_mean = from_tile(back, 1, groups) * (1.0 / node_total)
    factor = params_ref[27:28] * inv_std
    grad_ref[...] = (
        factor
        * (
            input_grad_ref[own_rows, :]
            - shift_mean
            - (filt_ref[...] - centre) * inv_std * gain_mean
        )
    ).astype(BF16)

    block = back_block
    blocks = rows // block
    span = block + 2 * HALO
    has_before = me > 0
    has_after = me < count - 1

    def rim_low():
        return swap_copy(
            rim_ref.at[0], rim_in.at[1], rim_sem.at[0, 0], rim_sem.at[1, 1],
            device_of(jnp.maximum(me - 1, 0), parts),
        )

    def rim_high():
        return swap_copy(
            rim_ref.at[1], rim_in.at[0], rim_sem.at[0, 1], rim_sem.at[1, 0],
            device_of(jnp.minimum(me + 1, count - 1), parts),
        )

    def finish_rows(low, size):
        input_grad_ref[pl.ds(pl.multiple_of(first + low, LANES), size), :] += total_ref[
            HALO + low : HALO + low + size
        ]

    late = rows - block - HALO
    out_first = rows // row_block

    group = 3
    points = TAPS // group
    schedule = {}
    for i, (_, _, _, place) in enumerate(streams):
        for t in range(depth):
            due = 10 + 8 * place + 9 * t
            schedule.setdefault(min(due, blocks * points), []).append((due, t, i))

    def back_step(it, carry):
        b = lax.rem(it * (blocks - 1), blocks)
        base = pl.multiple_of(b * block, block)
        window = pl.ds(base, span)
        place = near_t[0:TAPS, pl.ds(base, block)]
        place = place + lax.broadcasted_iota(jnp.int32, place.shape, 1) // LANES * LANES
        row = lax.broadcasted_iota(jnp.int32, (span, block), 0)
        grad = grad_ref[pl.ds(base, block), :]
        for point in range(points):
            total = total_ref[window, :]
            tokens = ext_ref[window, :].astype(F32)
            for k in range(point * group, (point + 1) * group):
                hot = (place[k : k + 1, :] == row).astype(F32).astype(BF16)
                spread = dot_plain(hot, grad)
                total += spread * params_ref[k : k + 1, :]
                small_ref[k : k + 1, :] += col_sum(spread * tokens)
            total_ref[window, :] = total
            for s in range(blocks):
                if s * points + point in schedule:

                    @pl.when(it == s)
                    def _(s=s, point=point):
                        for _, t, i in sorted(schedule[s * points + point]):
                            tree_step(i, t)

        @pl.when(it == 1)
        def _():
            rim_ref[0] = total_ref[0:HALO].astype(BF16)
            rim_ref[1] = total_ref[rows + HALO : rows + 2 * HALO].astype(BF16)

            @pl.when(has_before)
            def _():
                rim_low().start()

            @pl.when(has_after)
            def _():
                rim_high().start()

        @pl.when(it == 2)
        def _():
            @pl.when(has_before)
            def _():
                rim_low().wait_send()
                rim_high().wait_recv()
                total_ref[HALO : 2 * HALO] += rim_in[0].astype(F32)

            @pl.when(has_after)
            def _():
                rim_high().wait_send()
                rim_low().wait_recv()
                total_ref[rows : rows + HALO] += rim_in[1].astype(F32)

            finish_rows(late, rows - late)
            out_copy(input_grad_ref, out_first, late, rows - late).start()

        return carry

    lax.fori_loop(0, blocks, back_step, 0)

    flat[...] = jnp.zeros_like(flat)
    for r in range(small_rows):
        row = small_ref[r : r + 1, :]
        for g in range(groups):
            at = r * groups + g
            flat[at // 8, at % 8 : at % 8 + 1, :] = row[:, g * LANES : (g + 1) * LANES]
    send_to_all(lambda other: flat.at[other], flat_in, flat_send, flat_recv, count, parts, me)
    finish_rows(0, late)
    out_copy(input_grad_ref, out_first + 1, 0, late).start()
    await_from_all(flat.at[0], flat_in, flat_send, flat_recv, count, parts, me)
    part_sum[...] = add_landed(flat[me], flat_in, count)
    send_to_all(lambda other: part_sum, flat_all, all_send, all_recv, count, parts, me)
    for _, t, i in sorted(schedule.get(blocks * points, [])):
        tree_step(i, t)
    late_copies[1].wait()
    late_copies[2].wait()
    for c in range(cap):
        index = slot_ref[row_rank * cap + c]
        new = adam_step(
            stack_ref[part_rank, jnp.maximum(index, 0)].astype(F32), tile_sum[c], tile_first_ref[0, c],
            tile_second_ref[0, c], decay_rate,
        )
        live = [jnp.where(index >= 0, a, 0.0) for a in new]
        weight_out[0, c] = live[0]
        first_out[0, c] = live[1]
        second_out[0, c] = live[2]
        low_out[0, c] = live[0].astype(BF16)
    await_from_all(part_sum, flat_all, all_send, all_recv, count, parts, me)
    flat_all[0] = part_sum[...]
    for r in range(small_rows):
        for g in range(groups):
            at = r * groups + g
            tile_from = lax.rem(at // 8 - me + count, count)
            small_ref[r : r + 1, g * LANES : (g + 1) * LANES] = flat_all[
                tile_from, at % 8 : at % 8 + 1, :
            ]
    params_out[...], small_first_out[...], small_second_out[...] = adam_step(
        params_ref[...], small_ref[...], small_first_ref[...], small_second_ref[...], 0.0
    )
    for s in range(out_first):
        out_copy(output_ref, s, s * row_block, row_block).wait()
    out_copy(input_grad_ref, out_first, late, rows - late).wait()
    out_copy(input_grad_ref, out_first + 1, 0, late).wait()


def local(
    tokens_in, neighbours, scene_lengths, window_mask, small_params, qkv_weight, proj_weight,
    fc1_weight, fc2_weight, cotangent, owners, small_first, small_second, tile_first, tile_second
):
    rows_here, width = tokens_in.shape
    row_count = lax.axis_size("rows")
    parts = lax.axis_size("heads")
    count = row_count * parts
    rows = rows_here // parts
    tile_count = owners.shape[0]
    cap = tile_first.shape[1]
    depth = row_count.bit_length() - 1
    wide = len(streams_of(cap, depth))
    filter_block, row_block, back_block = 128, 512, 256

    tile_order = jnp.arange(tile_count, dtype=jnp.int32)
    same_owner = (owners[:, None] == owners[None, :]) & (tile_order[None, :] < tile_order[:, None])
    slot_of = owners * cap + jnp.sum(same_owner.astype(jnp.int32), axis=1)
    slot_ids = jnp.arange(row_count * cap, dtype=jnp.int32)
    found = slot_of[None, :] == slot_ids[:, None]
    slot_tile = jnp.max(jnp.where(found, tile_order[None, :], -1), axis=1)

    def by_tile(weight):
        return weight.reshape(-1, BR, width)

    vmem = pl.BlockSpec(memory_space=pltpu.VMEM)
    anywhere = pl.BlockSpec(memory_space=pl.ANY)
    smem = pl.BlockSpec(memory_space=pltpu.SMEM)
    dma = pltpu.SemaphoreType.DMA
    full = jax.ShapeDtypeStruct((rows_here, width), F32)
    tiles = jax.ShapeDtypeStruct(tile_first.shape, F32)
    small = jax.ShapeDtypeStruct(small_params.shape, F32)
    by_slot = (cap, row_count, BR, width)
    exchange = [pltpu.VMEM((8, LANES), F32), pltpu.VMEM((count, 8, LANES), F32)]
    return pl.pallas_call(
        functools.partial(
            step_kernel, filter_block=filter_block, row_block=row_block, back_block=back_block,
            row_count=row_count, parts=parts, cap=cap, scenes=scene_lengths.shape[0],
        ),
        in_specs=[smem] * 2 + [anywhere] * 9 + [vmem] * 4,
        out_specs=[vmem] * 9,
        out_shape=[
            full, full, tiles, tiles, tiles, jax.ShapeDtypeStruct(tile_first.shape, BF16), small,
            small, small,
        ],
        scratch_shapes=[
            pltpu.VMEM((TAPS, rows), jnp.int32),
            pltpu.VMEM((32, rows), jnp.int32),
            pltpu.VMEM((rows + 2 * HALO, width), BF16),
            pltpu.VMEM((rows, width), F32),
            pltpu.VMEM((8, width), F32),
            pltpu.VMEM((parts, tile_count, BR, width), BF16),
            pltpu.VMEM((rows, width), F32),
            pltpu.VMEM((parts, tile_count, BR, width), F32),
            pltpu.VMEM(small_params.shape, F32),
            pltpu.VMEM((rows + 2 * HALO, width), F32),
            pltpu.VMEM((rows, width), BF16),
            pltpu.VMEM((2, HALO, width), BF16),
            pltpu.VMEM((2, HALO, width), BF16),
            pltpu.VMEM(by_slot, BF16),
            pltpu.VMEM(by_slot, BF16),
            pltpu.VMEM(by_slot, BF16),
            pltpu.VMEM(by_slot, F32),
            pltpu.VMEM((cap, BR, width), F32),
            pltpu.VMEM(tile_first.shape, F32),
            pltpu.VMEM(tile_first.shape, F32),
        ]
        + exchange
        + exchange
        + [exchange[1]] * 2
        + exchange
        + [
            dma((6,)),
            dma((2,)),
            dma((3, 4)),
            dma((count,)),
            dma((count,)),
            dma((count,)),
            dma((count,)),
            dma((wide,)),
            dma((wide,)),
            dma((wide, depth)),
            dma((wide, depth)),
            dma((2, 2)),
            dma((count,)),
            dma((count,)),
            dma((count,)),
            dma((count,)),
            dma((2, rows // row_block + 2)),
        ],
        compiler_params=pltpu.CompilerParams(
            collective_id=0, has_side_effects=True, vmem_limit_bytes=62 << 20
        ),
    )(
        scene_lengths, slot_tile, tokens_in, neighbours.T, cotangent, by_tile(qkv_weight),
        by_tile(proj_weight), by_tile(fc1_weight), by_tile(fc2_weight), tile_first, tile_second, window_mask.reshape(-1, LANES),
        small_params, small_first, small_second,
    )


def solution(mesh):
    return jax.shard_map(
        local,
        mesh=mesh,
        in_specs=(
            P("rows", None),
            P("rows", None),
            P(),
            P("rows"),
            P(),
            P(None, "heads", None),
            P("heads", None),
            P("heads", None),
            P("heads", None),
            P("rows", None),
            P(),
            P(),
            P(),
            P("heads", "rows", None, None),
            P("heads", "rows", None, None),
        ),
        out_specs=(
            P("rows", None),
            P("rows", None),
            P("heads", "rows", None, None),
            P("heads", "rows", None, None),
            P("heads", "rows", None, None),
            P("heads", "rows", None, None),
            P(),
            P(),
            P(),
        ),
        check_vma=False,
    )
```

```python
import functools

import jax
import jax.numpy as jnp
from jax import lax
from jax.experimental import pallas as pl
from jax.experimental.pallas import tpu as pltpu
from jax.sharding import PartitionSpec as P

HEAD_DIM = 32
WIN = 32
HALO = 128
BR = 16
STEP = 3
TAPS = 27
LANES = 128

norm_eps = 1e-05
adam_rate = 0.05
beta_one = 0.5
beta_two = 0.5
adam_eps = 1e-08
decay_rate = 0.05
masked_score = -1e30

F32 = jnp.float32
BF16 = jnp.bfloat16


def adam_step(weight, gradient, first_moment, second_moment, decay_factor):
    first_new = beta_one * first_moment + (1.0 - beta_one) * gradient
    second_new = beta_two * second_moment + (1.0 - beta_two) * gradient * gradient
    first_hat = first_new / (1.0 - beta_one**STEP)
    second_hat = second_new / (1.0 - beta_two**STEP)
    weight_new = weight - adam_rate * (
        first_hat / (jnp.sqrt(second_hat) + adam_eps) + decay_factor * weight
    )
    return (weight_new, first_new, second_new)


def dot_plain(a, b):
    return jnp.dot(a, b, preferred_element_type=F32)


def dot_last(a, b):
    return lax.dot_general(a, b, (((1,), (1,)), ((), ())), preferred_element_type=F32)


def dot_first(a, b):
    return lax.dot_general(a, b, (((0,), (0,)), ((), ())), preferred_element_type=F32)


def col_sum(v):
    return jnp.sum(v, axis=0, keepdims=True)


def layer_norm(v):
    centre = v - jnp.mean(v, axis=1, keepdims=True)
    factor = lax.rsqrt(jnp.mean(centre * centre, axis=1, keepdims=True) + norm_eps)
    return centre * factor, factor


def norm_back(upstream, unit_part, factor, gain):
    scaled = upstream * gain
    return factor * (
        scaled
        - jnp.mean(scaled, axis=1, keepdims=True)
        - unit_part * jnp.mean(scaled * unit_part, axis=1, keepdims=True)
    )


def full_spec(shape):
    zeros = (0,) * len(shape)
    return pl.BlockSpec(shape, lambda i: zeros)


MESH = pl.DeviceIdType.MESH


def device_of(index, parts):
    return (index // parts, lax.rem(index, parts))


def greet_all(count, parts, me):
    barrier = pltpu.get_barrier_semaphore()

    def greet(j, carry):
        pl.semaphore_signal(
            barrier, inc=1, device_id=device_of(lax.rem(me + j, count), parts), device_id_type=MESH
        )
        return carry

    lax.fori_loop(1, count, greet, 0)


def await_all(count):
    pl.semaphore_wait(pltpu.get_barrier_semaphore(), count - 1)


def swap_copy(source, landing, send_sem, recv_sem, device):
    return pltpu.make_async_remote_copy(
        src_ref=source, dst_ref=landing, send_sem=send_sem, recv_sem=recv_sem,
        device_id=device, device_id_type=MESH,
    )


def send_to_all(source_of, landing, send_sem, recv_sem, count, parts, me):
    def send(j, carry):
        other = lax.rem(me + j, count)
        swap_copy(
            source_of(other), landing.at[count - j], send_sem.at[j], recv_sem.at[count - j],
            device_of(other, parts),
        ).start()
        return carry

    lax.fori_loop(1, count, send, 0)


def await_from_all(source, landing, send_sem, recv_sem, count, parts, me):
    def wait(j, carry):
        swap_copy(
            source, landing.at[count - j], send_sem.at[j], recv_sem.at[count - j],
            device_of(lax.rem(me + j, count), parts),
        ).wait()
        return carry

    lax.fori_loop(1, count, wait, 0)


def add_landed(own, landing, count):
    return lax.fori_loop(1, count, lambda j, total: total + landing[j], own)


def to_tile(tile_ref, rows):
    tile_ref[...] = jnp.zeros_like(tile_ref)
    groups = rows[0].shape[1] // LANES
    for r, row in enumerate(rows):
        for g in range(groups):
            at = r * groups + g
            tile_ref[at : at + 1, :] = row[:, g * LANES : (g + 1) * LANES]


def from_tile(tile, row, groups):
    at = row * groups
    return jnp.concatenate([tile[at + g : at + g + 1, :] for g in range(groups)], axis=1)


def streams_of(cap, depth):
    seventh = cap // 7 if depth > 2 else 0
    rest = cap - 2 * seventh
    sizes = [
        (0, 0, rest // 2 // 2), (1, 0, (rest - rest // 2) // 2), (2, 0, seventh),
        (0, 1, rest // 2 - rest // 2 // 2), (1, 1, (rest - rest // 2) - (rest - rest // 2) // 2),
        (3, 0, seventh),
    ]
    streams = []
    slot = 0
    for order, place, size in sizes:
        if size:
            streams.append((order, slot, size, place))
            slot += size
    return streams


def bits_of(depth, order):
    bits = list(range(depth))
    if order == 1 and depth > 1:
        bits[:2] = [1, 0]
    if order == 2:
        bits[:3] = [2, 0, 1]
    if order == 3:
        bits[:3] = [2, 1, 0]
    return bits


def flip(rank, bit):
    weight = 1 << bit
    return rank + weight - 2 * weight * lax.rem(rank // weight, 2)


def step_kernel(
    lengths_ref, slot_ref, tokens_hbm, near_hbm, cot_hbm, qkv_hbm, proj_hbm, fc1_hbm, fc2_hbm,
    tile_first_hbm, tile_second_hbm, mask_ref, params_ref, small_first_ref, small_second_ref,
    output_hbm, input_grad_hbm, weight_out, first_out, second_out, low_out, params_out,
    small_first_out, small_second_out,
    output_ref, input_grad_ref, near_in, near_t, ext_ref, filt_ref, stat_ref, stack_ref, cot_ref, stack_grad, small_ref,
    total_ref, grad_ref, rim_ref, rim_in, pair_out, pair_in, staged, arrived, sums, tile_sum, tile_first_ref,
    tile_second_ref, tile, landed, back_tile, back_landed, flat, part_sum,
    local_sem, side_sem, weight_sem, stat_send, stat_recv, back_send, back_recv, pair_send,
    pair_recv, tree_send, tree_recv, rim_sem, flat_send, flat_recv, all_send, all_recv, out_sem, leave_sem,
    *, filter_block, row_block, back_block, row_count, parts, cap, scenes
):
    row_rank = lax.axis_index("rows")
    part_rank = lax.axis_index("heads")
    count = row_count * parts
    me = row_rank * parts + part_rank
    other_core = (row_rank, 1 - part_rank)
    rows_here, width = tokens_hbm.shape
    rows = rows_here // parts
    first = part_rank * rows
    node_total = rows_here * row_count
    groups = width // LANES
    part = width // parts
    unit_part = fc1_hbm.shape[0] * BR
    depth = row_count.bit_length() - 1
    streams = streams_of(cap, depth)
    wide = len(streams)
    small_rows = params_ref.shape[0]
    scale = HEAD_DIM**-0.5
    greet_all(count, parts, me)

    own_copy = pltpu.make_async_copy(
        tokens_hbm.at[pl.ds(first, rows)], ext_ref.at[pl.ds(HALO, rows)], local_sem.at[0]
    )
    near_copy = pltpu.make_async_copy(
        near_hbm.at[:, pl.ds(pl.multiple_of(first, LANES), rows)], near_in, local_sem.at[1]
    )
    late_copies = [
        pltpu.make_async_copy(cot_hbm.at[pl.ds(first, rows)], cot_ref, local_sem.at[3]),
        pltpu.make_async_copy(tile_first_hbm, tile_first_ref, local_sem.at[4]),
        pltpu.make_async_copy(tile_second_hbm, tile_second_ref, local_sem.at[5]),
    ]
    own_copy.start()
    near_copy.start()
    low_side = ext_ref.at[pl.ds(0, HALO)]
    high_side = ext_ref.at[pl.ds(rows + HALO, HALO)]

    @pl.when(part_rank == 0)
    def _():
        pltpu.make_async_copy(tokens_hbm.at[pl.ds(rows, HALO)], high_side, local_sem.at[2]).start()

    @pl.when(part_rank == 1)
    def _():
        pltpu.make_async_copy(
            tokens_hbm.at[pl.ds(rows - HALO, HALO)], low_side, local_sem.at[2]
        ).start()

    @pl.when(me == 0)
    def _():
        ext_ref[0:HALO, :] = jnp.zeros((HALO, width), BF16)

    @pl.when(me == count - 1)
    def _():
        ext_ref[rows + HALO :, :] = jnp.zeros((HALO, width), BF16)

    pieces = []
    low = 0
    for ref in (qkv_hbm, proj_hbm, fc1_hbm, fc2_hbm):
        pieces.append((ref, low, ref.shape[0]))
        low += ref.shape[0]

    def own_weight(i):
        ref, at, size = pieces[i]
        return pltpu.make_async_copy(
            ref, stack_ref.at[part_rank, pl.ds(at, size)], weight_sem.at[0, i]
        )

    def sent_weight(i):
        _, at, size = pieces[i]
        here = stack_ref.at[part_rank, pl.ds(at, size)]
        return swap_copy(here, here, weight_sem.at[1, i], weight_sem.at[2, i], other_core)

    for i in range(len(pieces)):
        own_weight(i).start()
    for copy in late_copies:
        copy.start()

    def side_up():
        return swap_copy(
            tokens_hbm.at[pl.ds(rows_here - HALO, HALO)], low_side, side_sem.at[0], side_sem.at[1],
            (jnp.minimum(row_rank + 1, row_count - 1), part_rank),
        )

    def side_down():
        return swap_copy(
            tokens_hbm.at[pl.ds(0, HALO)], high_side, side_sem.at[0], side_sem.at[1],
            (jnp.maximum(row_rank - 1, 0), part_rank),
        )

    stat_ref[...] = jnp.zeros_like(stat_ref)
    stack_grad[...] = jnp.zeros_like(stack_grad)
    small_ref[...] = jnp.zeros_like(small_ref)
    total_ref[...] = jnp.zeros_like(total_ref)
    ends = []
    reached = 0
    for s in range(scenes):
        reached = reached + lengths_ref[s]
        ends.append(reached * WIN)
    near_copy.wait()
    own_copy.wait()

    block = filter_block
    blocks = rows // block
    span = block + 2 * HALO

    def filter_step(it, carry):
        @pl.when(it == 2)
        def _():
            await_all(count)

            @pl.when((part_rank == 0) & (row_rank < row_count - 1))
            def _():
                side_up().start()

            @pl.when((part_rank == 1) & (row_rank > 0))
            def _():
                side_down().start()

            for i in range(len(pieces)):
                own_weight(i).wait()
                sent_weight(i).start()

        @pl.when(it == blocks - 2)
        def _():
            pltpu.make_async_copy(
                tokens_hbm.at[pl.ds(0, HALO)], low_side, local_sem.at[2]
            ).wait()

            @pl.when((part_rank == 0) & (row_rank < row_count - 1))
            def _():
                side_up().wait_send()

            @pl.when((part_rank == 0) & (row_rank > 0))
            def _():
                side_up().wait_recv()

            @pl.when((part_rank == 1) & (row_rank > 0))
            def _():
                side_down().wait_send()

            @pl.when((part_rank == 1) & (row_rank < row_count - 1))
            def _():
                side_down().wait_recv()

        b = lax.rem(it + 1, blocks)
        base = pl.multiple_of(b * block, block)
        window = ext_ref[pl.ds(base, span), :]
        near = near_in[:, pl.ds(base, block)]
        lane = lax.broadcasted_iota(jnp.int32, (1, block), 1)
        own_row = row_rank * rows_here + first + base + lane
        scene_low = jnp.zeros_like(own_row)
        scene_high = jnp.full_like(own_row, node_total)
        for end in ends:
            passed = own_row >= end
            scene_low = jnp.maximum(scene_low, jnp.where(passed, end, 0))
            scene_high = jnp.minimum(scene_high, jnp.where(passed, node_total, end))
        target = own_row + near
        usable = (near >= -HALO) & (target >= scene_low) & (target < scene_high)
        place_t = jnp.where(usable, near + lane + HALO, -8 * HALO)
        near_t[0:TAPS, pl.ds(base, block)] = place_t
        place = jnp.transpose(
            jnp.concatenate([place_t, jnp.zeros((LANES - TAPS, block), jnp.int32)], axis=0)
        )
        column = lax.broadcasted_iota(jnp.int32, (block, span), 1)
        total = jnp.zeros((block, width), F32)
        group = 3
        for k0 in range(0, TAPS, group):
            hot = jnp.concatenate(
                [
                    (place[:, k : k + 1] == column).astype(F32).astype(BF16)
                    for k in range(k0, k0 + group)
                ],
                axis=0,
            )
            picked = dot_plain(hot, window)
            for j in range(group):
                total += picked[j * block : (j + 1) * block] * params_ref[k0 + j : k0 + j + 1, :]
        filt_ref[pl.ds(base, block), :] = total
        stat_ref[0:1, :] += col_sum(total)
        stat_ref[1:2, :] += col_sum(total * total)
        return carry

    lax.fori_loop(0, blocks, filter_step, 0)

    to_tile(tile, [stat_ref[0:1], stat_ref[1:2]])
    send_to_all(lambda other: tile, landed, stat_send, stat_recv, count, parts, me)
    for i in range(len(pieces)):
        sent_weight(i).wait()
    late_copies[0].wait()
    await_from_all(tile, landed, stat_send, stat_recv, count, parts, me)
    stat = add_landed(tile[...], landed, count)
    centre = from_tile(stat, 0, groups) / node_total
    inv_std = lax.rsqrt(from_tile(stat, 1, groups) / node_total - centre * centre + norm_eps)
    stat_ref[0:1, :] = centre
    stat_ref[1:2, :] = inv_std

    def weight_part(h, low, size):
        return stack_ref[h, low // BR : (low + size) // BR].reshape(size, width)

    def weight_rows(low, size):
        return jnp.concatenate([weight_part(h, low, size) for h in range(parts)], axis=0)

    def qkv_rows(j):
        return weight_rows(j * part, part)

    def proj_rows():
        return weight_rows(3 * part, part)

    def add_part(h, low, value):
        size = value.shape[0]
        stack_grad[h, low // BR : (low + size) // BR] += value.reshape(size // BR, BR, width)

    def add_grad(low, value):
        for h in range(parts):
            add_part(h, low, value[h * part : (h + 1) * part])

    def param(row):
        return params_ref[row : row + 1, :]

    def add_small(row, value):
        small_ref[row : row + 1, :] += value

    def out_copy(ref, sem, low, size):
        here = ref.at[pl.ds(pl.multiple_of(first + low, LANES), size)]
        return swap_copy(here, here, out_sem.at[0, sem], out_sem.at[1, sem], other_core)

    early = 4 * part // BR
    tile_count = stack_ref.shape[1]

    def pair_copy(i):
        tiles = pl.ds(0, early) if i == 0 else pl.ds(early, tile_count - early)
        return swap_copy(
            pair_out.at[tiles], pair_in.at[tiles], pair_send.at[i], pair_recv.at[i], other_core
        )

    def pair_start(i):
        low, high = (0, early) if i == 0 else (early, tile_count)
        pair_out[low:high] = stack_grad[1 - part_rank, low:high].astype(BF16)
        pair_copy(i).start()

    def leave(ref, hbm, sem, rank, low, size):
        there = pl.ds(pl.multiple_of(rank * rows + low, LANES), size)
        return pltpu.make_async_copy(ref.at[there], hbm.at[there], leave_sem.at[sem])

    def leave_output(s, own):
        rank = part_rank if own else 1 - part_rank
        return leave(output_ref, output_hbm, 2 * s + own, rank, s * row_block, row_block)

    def row_step(it, carry):
        block = row_block
        base = pl.multiple_of(it * block, block)
        block_rows = pl.ds(base, block)
        there = pl.ds(pl.multiple_of(first + base, LANES), block)
        mask_at = (first + base) // LANES
        bn_norm = (filt_ref[block_rows, :] - stat_ref[0:1]) * stat_ref[1:2]
        resid = ext_ref[pl.ds(pl.multiple_of(base + HALO, HALO), block), :].astype(F32) + (
            bn_norm * param(27) + param(28)
        )
        unit_one, factor_one = layer_norm(resid)
        normed_one = (unit_one * param(29) + param(30)).astype(BF16)
        query = ((dot_last(normed_one, qkv_rows(0)) + param(35)) * scale).astype(BF16)
        key = (dot_last(normed_one, qkv_rows(1)) * scale).astype(BF16)
        value = ((dot_last(normed_one, qkv_rows(2)) + param(36)) * scale).astype(BF16)

        side = LANES
        heads = LANES // HEAD_DIM
        lane_head = lax.broadcasted_iota(jnp.int32, (side, LANES), 1) // HEAD_DIM
        window_q = lax.broadcasted_iota(jnp.int32, (side, side), 0) // WIN
        window_k = lax.broadcasted_iota(jnp.int32, (side, side), 1) // WIN

        def stack_heads(a):
            return jnp.concatenate(
                [jnp.where(lane_head == j, a, jnp.zeros_like(a)) for j in range(heads)], axis=0
            )

        def pick_heads(a):
            picked = a[:side]
            for j in range(1, heads):
                picked = jnp.where(lane_head == j, a[j * side : (j + 1) * side], picked)
            return picked

        def cut(a, s, g):
            return a[s * side : (s + 1) * side, g * LANES : (g + 1) * LANES]

        sides = block // side
        pairs = [(s, g) for s in range(sides) for g in range(groups)]

        def join(pieces):
            return jnp.concatenate(
                [
                    jnp.concatenate(pieces[s * groups : (s + 1) * groups], axis=1)
                    for s in range(sides)
                ],
                axis=0,
            )

        keeps = [
            (window_q == window_k) & (mask_ref[pl.ds(mask_at + s, 1), :] > 0)
            for s in range(sides)
        ]
        queries = [cut(query, s, g) for s, g in pairs]
        keys = [stack_heads(cut(key, s, g)) for s, g in pairs]
        values = [stack_heads(cut(value, s, g)) for s, g in pairs]
        scores = [dot_last(a, b) for a, b in zip(queries, keys)]
        probs = []
        for (s, _), score_all in zip(pairs, scores):
            here = []
            for j in range(heads):
                score = jnp.where(keeps[s], score_all[:, j * side : (j + 1) * side], masked_score)
                power = jnp.exp(score - jnp.max(score, axis=1, keepdims=True))
                here.append(power * (1.0 / jnp.sum(power, axis=1, keepdims=True)))
            probs.append(jnp.concatenate(here, axis=1))
        probs_low = [p.astype(BF16) for p in probs]
        mixture = join([dot_plain(p, v) for p, v in zip(probs_low, values)]).astype(BF16)
        after = resid + (dot_plain(mixture, proj_rows()) + param(33))
        unit_two, factor_two = layer_norm(after)
        normed_two = (unit_two * param(31) + param(32)).astype(BF16)

        cotangent = cot_ref[block_rows, :]
        grad_ffn = cotangent.astype(BF16)
        ffn = jnp.zeros_like(after)
        grad_normed_two = jnp.zeros_like(after)
        chunk = unit_part
        for h in range(parts):
            for c in range(unit_part // chunk):
                low = 4 * part + c * chunk
                unit = 37 + (h * unit_part + c * chunk) // width
                bias_rows = range(unit, unit + chunk // width)
                fc1 = weight_part(h, low, chunk)
                fc2 = weight_part(h, low + unit_part, chunk)
                hidden = dot_last(normed_two, fc1) + jnp.concatenate(
                    [param(r) for r in bias_rows], axis=1
                )
                cumulative = 0.5 * (1.0 + lax.erf(hidden * 0.5**0.5))
                activation = (hidden * cumulative).astype(BF16)
                density = jnp.exp(-0.5 * hidden * hidden) * (2.0 * jnp.pi) ** (-0.5)
                ffn += dot_plain(activation, fc2)
                grad_hidden = (
                    dot_last(grad_ffn, fc2) * (cumulative + hidden * density)
                ).astype(BF16)
                grad_normed_two += dot_plain(grad_hidden, fc1)
                add_part(h, low, dot_first(grad_hidden, normed_two))
                add_part(h, low + unit_part, dot_first(activation, grad_ffn))
                bias_sum = col_sum(grad_hidden.astype(F32))
                for j, r in enumerate(bias_rows):
                    add_small(r, bias_sum[:, j * width : (j + 1) * width])
        output_ref[there, :] = after + (ffn + param(34))
        add_small(34, col_sum(grad_ffn.astype(F32)))

        @pl.when(it == rows // row_block - 1)
        def _():
            pair_start(1)


        grad_after = cotangent + norm_back(grad_normed_two, unit_two, factor_two, param(31))
        add_small(31, col_sum(grad_normed_two * unit_two))
        add_small(32, col_sum(grad_normed_two))
        grad_branch = grad_after.astype(BF16)
        add_grad(3 * part, dot_first(mixture, grad_branch))
        add_small(33, col_sum(grad_branch.astype(F32)))
        grad_mixture = dot_last(grad_branch, proj_rows()).astype(BF16)

        grad_mix = [cut(grad_mixture, s, g) for s, g in pairs]
        grad_probs = [dot_last(a, v) for a, v in zip(grad_mix, values)]
        grad_values = [pick_heads(dot_first(p, a)) for p, a in zip(probs_low, grad_mix)]
        grad_scores = []
        for prob_all, grad_all in zip(probs, grad_probs):
            here = []
            for j in range(heads):
                prob = prob_all[:, j * side : (j + 1) * side]
                term = prob * grad_all[:, j * side : (j + 1) * side]
                here.append((term - prob * jnp.sum(term, axis=1, keepdims=True)).astype(BF16))
            grad_scores.append(jnp.concatenate(here, axis=1))
        grad_queries = [dot_plain(a, k) for a, k in zip(grad_scores, keys)]
        grad_keys = [pick_heads(dot_first(a, q)) for a, q in zip(grad_scores, queries)]
        grad_qkv = [join(kind).astype(BF16) for kind in (grad_queries, grad_keys, grad_values)]
        grad_normed_one = jnp.zeros_like(resid)
        for j in range(3):
            grad_normed_one += dot_plain(grad_qkv[j], qkv_rows(j))
            add_grad(j * part, scale * dot_first(grad_qkv[j], normed_one))
        grad_normed_one = scale * grad_normed_one
        add_small(35, scale * col_sum(grad_qkv[0].astype(F32)))
        add_small(36, scale * col_sum(grad_qkv[2].astype(F32)))
        dres = grad_after + norm_back(grad_normed_one, unit_one, factor_one, param(29))
        add_small(29, col_sum(grad_normed_one * unit_one))
        add_small(30, col_sum(grad_normed_one))
        add_small(27, col_sum(dres * bn_norm))
        add_small(28, col_sum(dres))
        input_grad_ref[there, :] = dres
        for s in range(rows // block):

            @pl.when(it == s)
            def _(s=s):
                out_copy(output_ref, s, s * block, block).start()
                leave_output(s, 1).start()

        return carry

    lax.fori_loop(0, rows // row_block, row_step, 0)

    pair_start(0)
    to_tile(back_tile, [small_ref[27:28], small_ref[28:29]])
    send_to_all(lambda other: back_tile, back_landed, back_send, back_recv, count, parts, me)
    keep_at = {}
    for i, (order, _, _, _) in enumerate(streams):
        keep_at[i, 0] = 0
        for t, bit in enumerate(bits_of(depth, order)):
            half = row_count >> (t + 1)
            keep_at[i, t + 1] = keep_at[i, t] + lax.rem(row_rank // (1 << bit), 2) * half

    def give_at(i, t):
        return 2 * keep_at[i, t] + (row_count >> (t + 1)) - keep_at[i, t + 1]

    def slots_of(i):
        return pl.ds(streams[i][1], streams[i][2])

    def tile_at(i, c, p):
        order, slot, _, _ = streams[i]
        owner = 0
        for t, bit in enumerate(bits_of(depth, order)):
            owner = owner + lax.rem(p // (1 << (depth - 1 - t)), 2) * (1 << bit)
        return slot_ref[owner * cap + slot + c]

    def tree_copy(i, t):
        order = streams[i][0]
        half = row_count >> (t + 1)
        part = pl.ds(row_count - (row_count >> t), half)
        here = slots_of(i)
        return swap_copy(
            staged.at[here, part], arrived.at[here, part], tree_send.at[i, t], tree_recv.at[i, t],
            (flip(row_rank, bits_of(depth, order)[t]), part_rank),
        )

    def tree_first(i):
        _, slot, size, _ = streams[i]

        def value_at(c, p):
            index = tile_at(i, c, p)
            at = jnp.maximum(index, 0)
            value = stack_grad[part_rank, at] + pair_in[at].astype(F32)
            return jnp.where(index >= 0, value, 0.0)

        for c in range(size):

            def give(p, carry, c=c):
                staged[slot + c, p] = value_at(c, give_at(i, 0) + p).astype(BF16)
                return carry

            lax.fori_loop(0, row_count // 2, give, 0, unroll=8)
        tree_copy(i, 0).start()
        for c in range(size):

            def keep(p, carry, c=c):
                sums[slot + c, keep_at[i, 1] + p] = value_at(c, keep_at[i, 1] + p)
                return carry

            lax.fori_loop(0, row_count // 2, keep, 0, unroll=8)

    def tree_step(i, t):
        came = row_count - (row_count >> t)
        tree_copy(i, t).wait()
        low = keep_at[i, t + 1]
        here = slots_of(i)

        def values(k, size):
            return sums[here, pl.ds(k, size)] + arrived[here, pl.ds(came + k - low, size)].astype(F32)

        if t + 1 < depth:
            half = row_count >> (t + 2)
            at = row_count - (row_count >> (t + 1))
            staged[here, at : at + half] = values(give_at(i, t + 1), half).astype(BF16)
            tree_copy(i, t + 1).start()
            k = keep_at[i, t + 2]
            sums[here, pl.ds(k, half)] = values(k, half)
        else:
            tile_sum[here] = values(low, 1)[:, 0]

    pair_copy(1).wait()
    pair_copy(0).wait()
    for i in range(wide):
        tree_first(i)
    own_rows = pl.ds(pl.multiple_of(first, LANES), rows)
    await_from_all(back_tile, back_landed, back_send, back_recv, count, parts, me)
    back = add_landed(back_tile[...], back_landed, count)
    gain_mean = from_tile(back, 0, groups) * (1.0 / node_total)
    shift_mean = from_tile(back, 1, groups) * (1.0 / node_total)
    factor = params_ref[27:28] * inv_std
    grad_ref[...] = (
        factor
        * (
            input_grad_ref[own_rows, :]
            - shift_mean
            - (filt_ref[...] - centre) * inv_std * gain_mean
        )
    ).astype(BF16)

    block = back_block
    blocks = rows // block
    span = block + 2 * HALO
    has_before = me > 0
    has_after = me < count - 1

    def rim_low():
        return swap_copy(
            rim_ref.at[0], rim_in.at[1], rim_sem.at[0, 0], rim_sem.at[1, 1],
            device_of(jnp.maximum(me - 1, 0), parts),
        )

    def rim_high():
        return swap_copy(
            rim_ref.at[1], rim_in.at[0], rim_sem.at[0, 1], rim_sem.at[1, 0],
            device_of(jnp.minimum(me + 1, count - 1), parts),
        )

    def finish_rows(low, size):
        input_grad_ref[pl.ds(pl.multiple_of(first + low, LANES), size), :] += total_ref[
            HALO + low : HALO + low + size
        ]

    late = rows - block - HALO
    out_first = rows // row_block

    def leave_grad(i, own):
        low, size = ((late, rows - late), (0, late))[i]
        rank = part_rank if own else 1 - part_rank
        return leave(
            input_grad_ref, input_grad_hbm, 2 * out_first + 2 * i + own, rank, low, size
        )


    group = 3
    points = TAPS // group
    schedule = {}
    for i, (_, _, _, place) in enumerate(streams):
        for t in range(depth):
            due = 10 + 8 * place + 9 * t
            schedule.setdefault(min(due, blocks * points), []).append((due, t, i))

    def back_step(it, carry):
        b = lax.rem(it * (blocks - 1), blocks)
        base = pl.multiple_of(b * block, block)
        window = pl.ds(base, span)
        place = near_t[0:TAPS, pl.ds(base, block)]
        place = place + lax.broadcasted_iota(jnp.int32, place.shape, 1) // LANES * LANES
        row = lax.broadcasted_iota(jnp.int32, (span, block), 0)
        grad = grad_ref[pl.ds(base, block), :]
        for point in range(points):
            total = total_ref[window, :]
            tokens = ext_ref[window, :].astype(F32)
            for k in range(point * group, (point + 1) * group):
                hot = (place[k : k + 1, :] == row).astype(F32).astype(BF16)
                spread = dot_plain(hot, grad)
                total += spread * params_ref[k : k + 1, :]
                small_ref[k : k + 1, :] += col_sum(spread * tokens)
            total_ref[window, :] = total
            for s in range(blocks):
                if s * points + point in schedule:

                    @pl.when(it == s)
                    def _(s=s, point=point):
                        for _, t, i in sorted(schedule[s * points + point]):
                            tree_step(i, t)

        @pl.when(it == 1)
        def _():
            rim_ref[0] = total_ref[0:HALO].astype(BF16)
            rim_ref[1] = total_ref[rows + HALO : rows + 2 * HALO].astype(BF16)

            @pl.when(has_before)
            def _():
                rim_low().start()

            @pl.when(has_after)
            def _():
                rim_high().start()

        @pl.when(it == 2)
        def _():
            @pl.when(has_before)
            def _():
                rim_low().wait_send()
                rim_high().wait_recv()
                total_ref[HALO : 2 * HALO] += rim_in[0].astype(F32)

            @pl.when(has_after)
            def _():
                rim_high().wait_send()
                rim_low().wait_recv()
                total_ref[rows : rows + HALO] += rim_in[1].astype(F32)

            finish_rows(late, rows - late)
            out_copy(input_grad_ref, out_first, late, rows - late).start()
            leave_grad(0, 1).start()

        return carry

    lax.fori_loop(0, blocks, back_step, 0)

    flat_in, flat_all = landed, back_landed
    flat[...] = jnp.zeros_like(flat)
    for r in range(small_rows):
        row = small_ref[r : r + 1, :]
        for g in range(groups):
            at = r * groups + g
            flat[at // 8, at % 8 : at % 8 + 1, :] = row[:, g * LANES : (g + 1) * LANES]
    send_to_all(lambda other: flat.at[other], flat_in, flat_send, flat_recv, count, parts, me)
    finish_rows(0, late)
    out_copy(input_grad_ref, out_first + 1, 0, late).start()
    leave_grad(1, 1).start()
    for s in range(out_first):
        out_copy(output_ref, s, s * row_block, row_block).wait()
        leave_output(s, 0).start()
    out_copy(input_grad_ref, out_first, late, rows - late).wait()
    leave_grad(0, 0).start()
    await_from_all(flat.at[0], flat_in, flat_send, flat_recv, count, parts, me)
    part_sum[...] = add_landed(flat[me], flat_in, count)
    send_to_all(lambda other: part_sum, flat_all, all_send, all_recv, count, parts, me)
    for _, t, i in sorted(schedule.get(blocks * points, [])):
        tree_step(i, t)
    late_copies[1].wait()
    late_copies[2].wait()
    for c in range(cap):
        index = slot_ref[row_rank * cap + c]
        new = adam_step(
            stack_ref[part_rank, jnp.maximum(index, 0)].astype(F32), tile_sum[c], tile_first_ref[0, c],
            tile_second_ref[0, c], decay_rate,
        )
        live = [jnp.where(index >= 0, a, 0.0) for a in new]
        weight_out[0, c] = live[0]
        first_out[0, c] = live[1]
        second_out[0, c] = live[2]
        low_out[0, c] = live[0].astype(BF16)
    await_from_all(part_sum, flat_all, all_send, all_recv, count, parts, me)
    flat_all[0] = part_sum[...]
    for r in range(small_rows):
        for g in range(groups):
            at = r * groups + g
            tile_from = lax.rem(at // 8 - me + count, count)
            small_ref[r : r + 1, g * LANES : (g + 1) * LANES] = flat_all[
                tile_from, at % 8 : at % 8 + 1, :
            ]
    out_copy(input_grad_ref, out_first + 1, 0, late).wait()
    leave_grad(1, 0).start()
    params_out[...], small_first_out[...], small_second_out[...] = adam_step(
        params_ref[...], small_ref[...], small_first_ref[...], small_second_ref[...], 0.0
    )
    for s in range(out_first):
        leave_output(s, 0).wait()
        leave_output(s, 1).wait()
    leave_grad(0, 0).wait()
    leave_grad(0, 1).wait()
    leave_grad(1, 0).wait()
    leave_grad(1, 1).wait()


def hand_on_kernel(*refs, cuts):
    count = len(cuts)
    sources, landings, stages = refs[:count], refs[count : 2 * count], refs[2 * count : 3 * count]
    sem = refs[3 * count]
    reads, writes = [], []
    for source, landing, stage, cut in zip(sources, landings, stages, cuts):
        size = source.shape[0] // cut
        for c in range(cut):
            part = pl.ds(c * size, size)
            i = len(reads)
            reads.append(pltpu.make_async_copy(source.at[part], stage.at[part], sem.at[0, i]))
            writes.append(pltpu.make_async_copy(stage.at[part], landing.at[part], sem.at[1, i]))
    for read in reads:
        read.start()
    for read, write in zip(reads, writes):
        read.wait()
        write.start()
    for write in writes:
        write.wait()


def hand_on(arrays):
    cuts = [4 if a.shape[0] % 4 == 0 and a.size > 1 << 19 else 1 for a in arrays]
    shapes = [jax.ShapeDtypeStruct(a.shape, a.dtype) for a in arrays]
    anywhere = pl.BlockSpec(memory_space=pl.ANY)
    return pl.pallas_call(
        functools.partial(hand_on_kernel, cuts=cuts),
        in_specs=[anywhere] * len(arrays),
        out_specs=[anywhere] * len(arrays),
        out_shape=shapes,
        scratch_shapes=[pltpu.VMEM(a.shape, a.dtype) for a in arrays]
        + [pltpu.SemaphoreType.DMA((2, sum(cuts)))],
        compiler_params=pltpu.CompilerParams(vmem_limit_bytes=60 << 20),
    )(*arrays)


def local(
    tokens_in, neighbours, scene_lengths, window_mask, small_params, qkv_weight, proj_weight,
    fc1_weight, fc2_weight, cotangent, owners, small_first, small_second, tile_first, tile_second
):
    rows_here, width = tokens_in.shape
    row_count = lax.axis_size("rows")
    parts = lax.axis_size("heads")
    count = row_count * parts
    rows = rows_here // parts
    tile_count = owners.shape[0]
    cap = tile_first.shape[1]
    depth = row_count.bit_length() - 1
    wide = len(streams_of(cap, depth))
    filter_block, row_block, back_block = 128, 512, 256

    tile_order = jnp.arange(tile_count, dtype=jnp.int32)
    same_owner = (owners[:, None] == owners[None, :]) & (tile_order[None, :] < tile_order[:, None])
    slot_of = owners * cap + jnp.sum(same_owner.astype(jnp.int32), axis=1)
    slot_ids = jnp.arange(row_count * cap, dtype=jnp.int32)
    found = slot_of[None, :] == slot_ids[:, None]
    slot_tile = jnp.max(jnp.where(found, tile_order[None, :], -1), axis=1)

    def by_tile(weight):
        return weight.reshape(-1, BR, width)

    vmem = pl.BlockSpec(memory_space=pltpu.VMEM)
    anywhere = pl.BlockSpec(memory_space=pl.ANY)
    smem = pl.BlockSpec(memory_space=pltpu.SMEM)
    dma = pltpu.SemaphoreType.DMA
    full = jax.ShapeDtypeStruct((rows_here, width), F32)
    tiles = jax.ShapeDtypeStruct(tile_first.shape, F32)
    small = jax.ShapeDtypeStruct(small_params.shape, F32)
    by_slot = (cap, row_count, BR, width)
    exchange = [pltpu.VMEM((8, LANES), F32), pltpu.VMEM((count, 8, LANES), F32)]
    results = pl.pallas_call(
        functools.partial(
            step_kernel, filter_block=filter_block, row_block=row_block, back_block=back_block,
            row_count=row_count, parts=parts, cap=cap, scenes=scene_lengths.shape[0],
        ),
        in_specs=[smem] * 2 + [anywhere] * 9 + [vmem] * 4,
        out_specs=[anywhere] * 2 + [vmem] * 7,
        out_shape=[
            full, full, tiles, tiles, tiles, jax.ShapeDtypeStruct(tile_first.shape, BF16), small,
            small, small,
        ],
        scratch_shapes=[
            pltpu.VMEM((rows_here, width), F32),
            pltpu.VMEM((rows_here, width), F32),
            pltpu.VMEM((TAPS, rows), jnp.int32),
            pltpu.VMEM((32, rows), jnp.int32),
            pltpu.VMEM((rows + 2 * HALO, width), BF16),
            pltpu.VMEM((rows, width), F32),
            pltpu.VMEM((8, width), F32),
            pltpu.VMEM((parts, tile_count, BR, width), BF16),
            pltpu.VMEM((rows, width), F32),
            pltpu.VMEM((parts, tile_count, BR, width), F32),
            pltpu.VMEM(small_params.shape, F32),
            pltpu.VMEM((rows + 2 * HALO, width), F32),
            pltpu.VMEM((rows, width), BF16),
            pltpu.VMEM((2, HALO, width), BF16),
            pltpu.VMEM((2, HALO, width), BF16),
            pltpu.VMEM((tile_count, BR, width), BF16),
            pltpu.VMEM((tile_count, BR, width), BF16),
            pltpu.VMEM(by_slot, BF16),
            pltpu.VMEM(by_slot, BF16),
            pltpu.VMEM(by_slot, F32),
            pltpu.VMEM((cap, BR, width), F32),
            pltpu.VMEM(tile_first.shape, F32),
            pltpu.VMEM(tile_first.shape, F32),
        ]
        + exchange
        + exchange
        + [exchange[1], exchange[0]]
        + [
            dma((6,)),
            dma((2,)),
            dma((3, 4)),
            dma((count,)),
            dma((count,)),
            dma((count,)),
            dma((count,)),
            dma((2,)),
            dma((2,)),
            dma((wide, depth)),
            dma((wide, depth)),
            dma((2, 2)),
            dma((count,)),
            dma((count,)),
            dma((count,)),
            dma((count,)),
            dma((2, rows // row_block + 2)),
            dma((2 * (rows // row_block) + 4,)),
        ],
        compiler_params=pltpu.CompilerParams(
            collective_id=0, has_side_effects=True, vmem_limit_bytes=62 << 20
        ),
    )(
        scene_lengths, slot_tile, tokens_in, neighbours.T, cotangent, by_tile(qkv_weight),
        by_tile(proj_weight), by_tile(fc1_weight), by_tile(fc2_weight), tile_first, tile_second, window_mask.reshape(-1, LANES),
        small_params, small_first, small_second,
    )
    return hand_on(results)


def solution(mesh):
    return jax.shard_map(
        local,
        mesh=mesh,
        in_specs=(
            P("rows", None),
            P("rows", None),
            P(),
            P("rows"),
            P(),
            P(None, "heads", None),
            P("heads", None),
            P("heads", None),
            P("heads", None),
            P("rows", None),
            P(),
            P(),
            P(),
            P("heads", "rows", None, None),
            P("heads", "rows", None, None),
        ),
        out_specs=(
            P("rows", None),
            P("rows", None),
            P("heads", "rows", None, None),
            P("heads", "rows", None, None),
            P("heads", "rows", None, None),
            P("heads", "rows", None, None),
            P(),
            P(),
            P(),
        ),
        check_vma=False,
    )
```

```python
import functools

import jax
import jax.numpy as jnp
from jax import lax
from jax.experimental import pallas as pl
from jax.experimental.pallas import tpu as pltpu
from jax.sharding import PartitionSpec as P

HEAD_DIM = 32
WIN = 32
HALO = 128
BR = 16
STEP = 3
TAPS = 27
LANES = 128

norm_eps = 1e-05
adam_rate = 0.05
beta_one = 0.5
beta_two = 0.5
adam_eps = 1e-08
decay_rate = 0.05
masked_score = -1e30

F32 = jnp.float32
BF16 = jnp.bfloat16


def adam_step(weight, gradient, first_moment, second_moment, decay_factor):
    first_new = beta_one * first_moment + (1.0 - beta_one) * gradient
    second_new = beta_two * second_moment + (1.0 - beta_two) * gradient * gradient
    first_hat = first_new / (1.0 - beta_one**STEP)
    second_hat = second_new / (1.0 - beta_two**STEP)
    weight_new = weight - adam_rate * (
        first_hat / (jnp.sqrt(second_hat) + adam_eps) + decay_factor * weight
    )
    return (weight_new, first_new, second_new)


def dot_plain(a, b):
    return jnp.dot(a, b, preferred_element_type=F32)


def dot_last(a, b):
    return lax.dot_general(a, b, (((1,), (1,)), ((), ())), preferred_element_type=F32)


def dot_first(a, b):
    return lax.dot_general(a, b, (((0,), (0,)), ((), ())), preferred_element_type=F32)


def col_sum(v):
    return jnp.sum(v, axis=0, keepdims=True)


def layer_norm(v):
    centre = v - jnp.mean(v, axis=1, keepdims=True)
    factor = lax.rsqrt(jnp.mean(centre * centre, axis=1, keepdims=True) + norm_eps)
    return centre * factor, factor


def norm_back(upstream, unit_part, factor, gain):
    scaled = upstream * gain
    return factor * (
        scaled
        - jnp.mean(scaled, axis=1, keepdims=True)
        - unit_part * jnp.mean(scaled * unit_part, axis=1, keepdims=True)
    )


def full_spec(shape):
    zeros = (0,) * len(shape)
    return pl.BlockSpec(shape, lambda i: zeros)


MESH = pl.DeviceIdType.MESH


def device_of(index, parts):
    return (index // parts, lax.rem(index, parts))


def greet_all(count, parts, me):
    barrier = pltpu.get_barrier_semaphore()

    def greet(j, carry):
        pl.semaphore_signal(
            barrier, inc=1, device_id=device_of(lax.rem(me + j, count), parts), device_id_type=MESH
        )
        return carry

    lax.fori_loop(1, count, greet, 0)


def await_all(count):
    pl.semaphore_wait(pltpu.get_barrier_semaphore(), count - 1)


def swap_copy(source, landing, send_sem, recv_sem, device):
    return pltpu.make_async_remote_copy(
        src_ref=source, dst_ref=landing, send_sem=send_sem, recv_sem=recv_sem,
        device_id=device, device_id_type=MESH,
    )


def send_to_all(source_of, landing, send_sem, recv_sem, count, parts, me):
    def send(j, carry):
        other = lax.rem(me + j, count)
        swap_copy(
            source_of(other), landing.at[count - j], send_sem.at[j], recv_sem.at[count - j],
            device_of(other, parts),
        ).start()
        return carry

    lax.fori_loop(1, count, send, 0)


def await_from_all(source, landing, send_sem, recv_sem, count, parts, me):
    def wait(j, carry):
        swap_copy(
            source, landing.at[count - j], send_sem.at[j], recv_sem.at[count - j],
            device_of(lax.rem(me + j, count), parts),
        ).wait()
        return carry

    lax.fori_loop(1, count, wait, 0)


def add_landed(own, landing, count):
    return lax.fori_loop(1, count, lambda j, total: total + landing[j], own)


def to_tile(tile_ref, rows):
    tile_ref[...] = jnp.zeros_like(tile_ref)
    groups = rows[0].shape[1] // LANES
    for r, row in enumerate(rows):
        for g in range(groups):
            at = r * groups + g
            tile_ref[at : at + 1, :] = row[:, g * LANES : (g + 1) * LANES]


def from_tile(tile, row, groups):
    at = row * groups
    return jnp.concatenate([tile[at + g : at + g + 1, :] for g in range(groups)], axis=1)


def streams_of(cap, depth):
    seventh = cap // 7 if depth > 2 else 0
    rest = cap - 2 * seventh
    sizes = [
        (0, 0, rest // 2 // 2), (1, 0, (rest - rest // 2) // 2), (2, 0, seventh),
        (0, 1, rest // 2 - rest // 2 // 2), (1, 1, (rest - rest // 2) - (rest - rest // 2) // 2),
        (3, 0, seventh),
    ]
    streams = []
    slot = 0
    for order, place, size in sizes:
        if size:
            streams.append((order, slot, size, place))
            slot += size
    return streams


def bits_of(depth, order):
    bits = list(range(depth))
    if order == 1 and depth > 1:
        bits[:2] = [1, 0]
    if order == 2:
        bits[:3] = [2, 0, 1]
    if order == 3:
        bits[:3] = [2, 1, 0]
    return bits


def flip(rank, bit):
    weight = 1 << bit
    return rank + weight - 2 * weight * lax.rem(rank // weight, 2)


def step_kernel(
    lengths_ref, slot_ref, tokens_hbm, near_hbm, cot_hbm, qkv_hbm, proj_hbm, fc1_hbm, fc2_hbm,
    tile_first_hbm, tile_second_hbm, mask_ref, params_ref, small_first_ref, small_second_ref,
    output_hbm, input_grad_hbm, weight_out, first_out, second_out, low_out, params_out,
    small_first_out, small_second_out,
    output_ref, input_grad_ref, near_in, near_t, ext_ref, filt_ref, stat_ref, stack_ref, cot_ref, stack_grad, small_ref,
    total_ref, grad_ref, rim_ref, rim_in, pair_out, pair_in, staged, arrived, sums, tile_sum, tile_first_ref,
    tile_second_ref, tile, landed, back_tile, back_landed, small_sum,
    local_sem, side_sem, weight_sem, stat_send, stat_recv, back_send, back_recv, pair_send,
    pair_recv, tree_send, tree_recv, rim_sem, flat_send, flat_recv, all_send, all_recv, out_sem, leave_sem,
    *, filter_block, row_block, back_block, row_count, parts, cap, scenes
):
    row_rank = lax.axis_index("rows")
    part_rank = lax.axis_index("heads")
    count = row_count * parts
    me = row_rank * parts + part_rank
    other_core = (row_rank, 1 - part_rank)
    rows_here, width = tokens_hbm.shape
    rows = rows_here // parts
    first = part_rank * rows
    node_total = rows_here * row_count
    groups = width // LANES
    part = width // parts
    unit_part = fc1_hbm.shape[0] * BR
    depth = row_count.bit_length() - 1
    streams = streams_of(cap, depth)
    wide = len(streams)
    small_rows = params_ref.shape[0]
    scale = HEAD_DIM**-0.5
    greet_all(count, parts, me)

    own_copy = pltpu.make_async_copy(
        tokens_hbm.at[pl.ds(first, rows)], ext_ref.at[pl.ds(HALO, rows)], local_sem.at[0]
    )
    near_copy = pltpu.make_async_copy(
        near_hbm.at[:, pl.ds(pl.multiple_of(first, LANES), rows)], near_in, local_sem.at[1]
    )
    late_copies = [
        pltpu.make_async_copy(cot_hbm.at[pl.ds(first, rows)], cot_ref, local_sem.at[3]),
        pltpu.make_async_copy(tile_first_hbm, tile_first_ref, local_sem.at[4]),
        pltpu.make_async_copy(tile_second_hbm, tile_second_ref, local_sem.at[5]),
    ]
    own_copy.start()
    near_copy.start()
    low_side = ext_ref.at[pl.ds(0, HALO)]
    high_side = ext_ref.at[pl.ds(rows + HALO, HALO)]

    @pl.when(part_rank == 0)
    def _():
        pltpu.make_async_copy(tokens_hbm.at[pl.ds(rows, HALO)], high_side, local_sem.at[2]).start()

    @pl.when(part_rank == 1)
    def _():
        pltpu.make_async_copy(
            tokens_hbm.at[pl.ds(rows - HALO, HALO)], low_side, local_sem.at[2]
        ).start()

    @pl.when(me == 0)
    def _():
        ext_ref[0:HALO, :] = jnp.zeros((HALO, width), BF16)

    @pl.when(me == count - 1)
    def _():
        ext_ref[rows + HALO :, :] = jnp.zeros((HALO, width), BF16)

    pieces = []
    low = 0
    for ref in (qkv_hbm, proj_hbm, fc1_hbm, fc2_hbm):
        pieces.append((ref, low, ref.shape[0]))
        low += ref.shape[0]

    def own_weight(i):
        ref, at, size = pieces[i]
        return pltpu.make_async_copy(
            ref, stack_ref.at[part_rank, pl.ds(at, size)], weight_sem.at[0, i]
        )

    def sent_weight(i):
        _, at, size = pieces[i]
        here = stack_ref.at[part_rank, pl.ds(at, size)]
        return swap_copy(here, here, weight_sem.at[1, i], weight_sem.at[2, i], other_core)

    for i in range(len(pieces)):
        own_weight(i).start()
    for copy in late_copies:
        copy.start()

    def side_up():
        return swap_copy(
            tokens_hbm.at[pl.ds(rows_here - HALO, HALO)], low_side, side_sem.at[0], side_sem.at[1],
            (jnp.minimum(row_rank + 1, row_count - 1), part_rank),
        )

    def side_down():
        return swap_copy(
            tokens_hbm.at[pl.ds(0, HALO)], high_side, side_sem.at[0], side_sem.at[1],
            (jnp.maximum(row_rank - 1, 0), part_rank),
        )

    stat_ref[...] = jnp.zeros_like(stat_ref)
    stack_grad[...] = jnp.zeros_like(stack_grad)
    small_ref[...] = jnp.zeros_like(small_ref)
    total_ref[...] = jnp.zeros_like(total_ref)
    ends = []
    reached = 0
    for s in range(scenes):
        reached = reached + lengths_ref[s]
        ends.append(reached * WIN)
    near_copy.wait()
    own_copy.wait()

    block = filter_block
    blocks = rows // block
    span = block + 2 * HALO

    def filter_step(it, carry):
        @pl.when(it == 2)
        def _():
            await_all(count)

            @pl.when((part_rank == 0) & (row_rank < row_count - 1))
            def _():
                side_up().start()

            @pl.when((part_rank == 1) & (row_rank > 0))
            def _():
                side_down().start()

            for i in range(len(pieces)):
                own_weight(i).wait()
                sent_weight(i).start()

        @pl.when(it == blocks - 2)
        def _():
            pltpu.make_async_copy(
                tokens_hbm.at[pl.ds(0, HALO)], low_side, local_sem.at[2]
            ).wait()

            @pl.when((part_rank == 0) & (row_rank < row_count - 1))
            def _():
                side_up().wait_send()

            @pl.when((part_rank == 0) & (row_rank > 0))
            def _():
                side_up().wait_recv()

            @pl.when((part_rank == 1) & (row_rank > 0))
            def _():
                side_down().wait_send()

            @pl.when((part_rank == 1) & (row_rank < row_count - 1))
            def _():
                side_down().wait_recv()

        b = lax.rem(it + 1, blocks)
        base = pl.multiple_of(b * block, block)
        window = ext_ref[pl.ds(base, span), :]
        near = near_in[:, pl.ds(base, block)]
        lane = lax.broadcasted_iota(jnp.int32, (1, block), 1)
        own_row = row_rank * rows_here + first + base + lane
        scene_low = jnp.zeros_like(own_row)
        scene_high = jnp.full_like(own_row, node_total)
        for end in ends:
            passed = own_row >= end
            scene_low = jnp.maximum(scene_low, jnp.where(passed, end, 0))
            scene_high = jnp.minimum(scene_high, jnp.where(passed, node_total, end))
        target = own_row + near
        usable = (near >= -HALO) & (target >= scene_low) & (target < scene_high)
        place_t = jnp.where(usable, near + lane + HALO, -8 * HALO)
        near_t[0:TAPS, pl.ds(base, block)] = place_t
        place = jnp.transpose(
            jnp.concatenate([place_t, jnp.zeros((LANES - TAPS, block), jnp.int32)], axis=0)
        )
        column = lax.broadcasted_iota(jnp.int32, (block, span), 1)
        total = jnp.zeros((block, width), F32)
        group = 3
        for k0 in range(0, TAPS, group):
            hot = jnp.concatenate(
                [
                    (place[:, k : k + 1] == column).astype(F32).astype(BF16)
                    for k in range(k0, k0 + group)
                ],
                axis=0,
            )
            picked = dot_plain(hot, window)
            for j in range(group):
                total += picked[j * block : (j + 1) * block] * params_ref[k0 + j : k0 + j + 1, :]
        filt_ref[pl.ds(base, block), :] = total
        stat_ref[0:1, :] += col_sum(total)
        stat_ref[1:2, :] += col_sum(total * total)
        return carry

    lax.fori_loop(0, blocks, filter_step, 0)

    to_tile(tile, [stat_ref[0:1], stat_ref[1:2]])
    send_to_all(lambda other: tile, landed, stat_send, stat_recv, count, parts, me)
    for i in range(len(pieces)):
        sent_weight(i).wait()
    late_copies[0].wait()
    await_from_all(tile, landed, stat_send, stat_recv, count, parts, me)
    stat = add_landed(tile[...], landed, count)
    centre = from_tile(stat, 0, groups) / node_total
    inv_std = lax.rsqrt(from_tile(stat, 1, groups) / node_total - centre * centre + norm_eps)
    stat_ref[0:1, :] = centre
    stat_ref[1:2, :] = inv_std

    def weight_part(h, low, size):
        return stack_ref[h, low // BR : (low + size) // BR].reshape(size, width)

    def weight_rows(low, size):
        return jnp.concatenate([weight_part(h, low, size) for h in range(parts)], axis=0)

    def qkv_rows(j):
        return weight_rows(j * part, part)

    def proj_rows():
        return weight_rows(3 * part, part)

    def add_part(h, low, value):
        size = value.shape[0]
        stack_grad[h, low // BR : (low + size) // BR] += value.reshape(size // BR, BR, width)

    def add_grad(low, value):
        for h in range(parts):
            add_part(h, low, value[h * part : (h + 1) * part])

    def param(row):
        return params_ref[row : row + 1, :]

    def add_small(row, value):
        small_ref[row : row + 1, :] += value

    def out_copy(ref, sem, low, size):
        here = ref.at[pl.ds(pl.multiple_of(first + low, LANES), size)]
        return swap_copy(here, here, out_sem.at[0, sem], out_sem.at[1, sem], other_core)

    early = 4 * part // BR
    tile_count = stack_ref.shape[1]

    def pair_copy(i):
        tiles = pl.ds(0, early) if i == 0 else pl.ds(early, tile_count - early)
        return swap_copy(
            pair_out.at[tiles], pair_in.at[tiles], pair_send.at[i], pair_recv.at[i], other_core
        )

    def pair_start(i):
        low, high = (0, early) if i == 0 else (early, tile_count)
        pair_out[low:high] = stack_grad[1 - part_rank, low:high].astype(BF16)
        pair_copy(i).start()

    def leave(ref, hbm, sem, rank, low, size):
        there = pl.ds(pl.multiple_of(rank * rows + low, LANES), size)
        return pltpu.make_async_copy(ref.at[there], hbm.at[there], leave_sem.at[sem])

    def leave_output(s, own):
        rank = part_rank if own else 1 - part_rank
        return leave(output_ref, output_hbm, 2 * s + own, rank, s * row_block, row_block)

    def row_step(it, carry):
        block = row_block
        base = pl.multiple_of(it * block, block)
        block_rows = pl.ds(base, block)
        there = pl.ds(pl.multiple_of(first + base, LANES), block)
        mask_at = (first + base) // LANES
        bn_norm = (filt_ref[block_rows, :] - stat_ref[0:1]) * stat_ref[1:2]
        resid = ext_ref[pl.ds(pl.multiple_of(base + HALO, HALO), block), :].astype(F32) + (
            bn_norm * param(27) + param(28)
        )
        unit_one, factor_one = layer_norm(resid)
        normed_one = (unit_one * param(29) + param(30)).astype(BF16)
        query = ((dot_last(normed_one, qkv_rows(0)) + param(35)) * scale).astype(BF16)
        key = (dot_last(normed_one, qkv_rows(1)) * scale).astype(BF16)
        value = ((dot_last(normed_one, qkv_rows(2)) + param(36)) * scale).astype(BF16)

        side = LANES
        heads = LANES // HEAD_DIM
        lane_head = lax.broadcasted_iota(jnp.int32, (side, LANES), 1) // HEAD_DIM
        window_q = lax.broadcasted_iota(jnp.int32, (side, side), 0) // WIN
        window_k = lax.broadcasted_iota(jnp.int32, (side, side), 1) // WIN

        def stack_heads(a):
            return jnp.concatenate(
                [jnp.where(lane_head == j, a, jnp.zeros_like(a)) for j in range(heads)], axis=0
            )

        def pick_heads(a):
            picked = a[:side]
            for j in range(1, heads):
                picked = jnp.where(lane_head == j, a[j * side : (j + 1) * side], picked)
            return picked

        def cut(a, s, g):
            return a[s * side : (s + 1) * side, g * LANES : (g + 1) * LANES]

        sides = block // side
        pairs = [(s, g) for s in range(sides) for g in range(groups)]

        def join(pieces):
            return jnp.concatenate(
                [
                    jnp.concatenate(pieces[s * groups : (s + 1) * groups], axis=1)
                    for s in range(sides)
                ],
                axis=0,
            )

        keeps = [
            (window_q == window_k) & (mask_ref[pl.ds(mask_at + s, 1), :] > 0)
            for s in range(sides)
        ]
        queries = [cut(query, s, g) for s, g in pairs]
        keys = [stack_heads(cut(key, s, g)) for s, g in pairs]
        values = [stack_heads(cut(value, s, g)) for s, g in pairs]
        scores = [dot_last(a, b) for a, b in zip(queries, keys)]
        probs = []
        for (s, _), score_all in zip(pairs, scores):
            here = []
            for j in range(heads):
                score = jnp.where(keeps[s], score_all[:, j * side : (j + 1) * side], masked_score)
                power = jnp.exp(score - jnp.max(score, axis=1, keepdims=True))
                here.append(power * (1.0 / jnp.sum(power, axis=1, keepdims=True)))
            probs.append(jnp.concatenate(here, axis=1))
        probs_low = [p.astype(BF16) for p in probs]
        mixture = join([dot_plain(p, v) for p, v in zip(probs_low, values)]).astype(BF16)
        after = resid + (dot_plain(mixture, proj_rows()) + param(33))
        unit_two, factor_two = layer_norm(after)
        normed_two = (unit_two * param(31) + param(32)).astype(BF16)

        cotangent = cot_ref[block_rows, :]
        grad_ffn = cotangent.astype(BF16)
        ffn = jnp.zeros_like(after)
        grad_normed_two = jnp.zeros_like(after)
        chunk = unit_part
        for h in range(parts):
            for c in range(unit_part // chunk):
                low = 4 * part + c * chunk
                unit = 37 + (h * unit_part + c * chunk) // width
                bias_rows = range(unit, unit + chunk // width)
                fc1 = weight_part(h, low, chunk)
                fc2 = weight_part(h, low + unit_part, chunk)
                hidden = dot_last(normed_two, fc1) + jnp.concatenate(
                    [param(r) for r in bias_rows], axis=1
                )
                cumulative = 0.5 * (1.0 + lax.erf(hidden * 0.5**0.5))
                activation = (hidden * cumulative).astype(BF16)
                density = jnp.exp(-0.5 * hidden * hidden) * (2.0 * jnp.pi) ** (-0.5)
                ffn += dot_plain(activation, fc2)
                grad_hidden = (
                    dot_last(grad_ffn, fc2) * (cumulative + hidden * density)
                ).astype(BF16)
                grad_normed_two += dot_plain(grad_hidden, fc1)
                add_part(h, low, dot_first(grad_hidden, normed_two))
                add_part(h, low + unit_part, dot_first(activation, grad_ffn))
                bias_sum = col_sum(grad_hidden.astype(F32))
                for j, r in enumerate(bias_rows):
                    add_small(r, bias_sum[:, j * width : (j + 1) * width])
        output_ref[there, :] = after + (ffn + param(34))
        add_small(34, col_sum(grad_ffn.astype(F32)))

        @pl.when(it == rows // row_block - 1)
        def _():
            pair_start(1)


        grad_after = cotangent + norm_back(grad_normed_two, unit_two, factor_two, param(31))
        add_small(31, col_sum(grad_normed_two * unit_two))
        add_small(32, col_sum(grad_normed_two))
        grad_branch = grad_after.astype(BF16)
        add_grad(3 * part, dot_first(mixture, grad_branch))
        add_small(33, col_sum(grad_branch.astype(F32)))
        grad_mixture = dot_last(grad_branch, proj_rows()).astype(BF16)

        grad_mix = [cut(grad_mixture, s, g) for s, g in pairs]
        grad_probs = [dot_last(a, v) for a, v in zip(grad_mix, values)]
        grad_values = [pick_heads(dot_first(p, a)) for p, a in zip(probs_low, grad_mix)]
        grad_scores = []
        for prob_all, grad_all in zip(probs, grad_probs):
            here = []
            for j in range(heads):
                prob = prob_all[:, j * side : (j + 1) * side]
                term = prob * grad_all[:, j * side : (j + 1) * side]
                here.append((term - prob * jnp.sum(term, axis=1, keepdims=True)).astype(BF16))
            grad_scores.append(jnp.concatenate(here, axis=1))
        grad_queries = [dot_plain(a, k) for a, k in zip(grad_scores, keys)]
        grad_keys = [pick_heads(dot_first(a, q)) for a, q in zip(grad_scores, queries)]
        grad_qkv = [join(kind).astype(BF16) for kind in (grad_queries, grad_keys, grad_values)]
        grad_normed_one = jnp.zeros_like(resid)
        for j in range(3):
            grad_normed_one += dot_plain(grad_qkv[j], qkv_rows(j))
            add_grad(j * part, scale * dot_first(grad_qkv[j], normed_one))
        grad_normed_one = scale * grad_normed_one
        add_small(35, scale * col_sum(grad_qkv[0].astype(F32)))
        add_small(36, scale * col_sum(grad_qkv[2].astype(F32)))
        dres = grad_after + norm_back(grad_normed_one, unit_one, factor_one, param(29))
        add_small(29, col_sum(grad_normed_one * unit_one))
        add_small(30, col_sum(grad_normed_one))
        add_small(27, col_sum(dres * bn_norm))
        add_small(28, col_sum(dres))
        input_grad_ref[there, :] = dres
        for s in range(rows // block):

            @pl.when(it == s)
            def _(s=s):
                out_copy(output_ref, s, s * block, block).start()
                leave_output(s, 1).start()

        return carry

    lax.fori_loop(0, rows // row_block, row_step, 0)

    pair_start(0)
    to_tile(back_tile, [small_ref[27:28], small_ref[28:29]])
    send_to_all(lambda other: back_tile, back_landed, back_send, back_recv, count, parts, me)
    keep_at = {}
    for i, (order, _, _, _) in enumerate(streams):
        keep_at[i, 0] = 0
        for t, bit in enumerate(bits_of(depth, order)):
            half = row_count >> (t + 1)
            keep_at[i, t + 1] = keep_at[i, t] + lax.rem(row_rank // (1 << bit), 2) * half

    def give_at(i, t):
        return 2 * keep_at[i, t] + (row_count >> (t + 1)) - keep_at[i, t + 1]

    def slots_of(i):
        return pl.ds(streams[i][1], streams[i][2])

    def tile_at(i, c, p):
        order, slot, _, _ = streams[i]
        owner = 0
        for t, bit in enumerate(bits_of(depth, order)):
            owner = owner + lax.rem(p // (1 << (depth - 1 - t)), 2) * (1 << bit)
        return slot_ref[owner * cap + slot + c]

    def tree_copy(i, t):
        order = streams[i][0]
        half = row_count >> (t + 1)
        part = pl.ds(row_count - (row_count >> t), half)
        here = slots_of(i)
        return swap_copy(
            staged.at[here, part], arrived.at[here, part], tree_send.at[i, t], tree_recv.at[i, t],
            (flip(row_rank, bits_of(depth, order)[t]), part_rank),
        )

    def tree_first(i):
        _, slot, size, _ = streams[i]

        def value_at(c, p):
            index = tile_at(i, c, p)
            at = jnp.maximum(index, 0)
            value = stack_grad[part_rank, at] + pair_in[at].astype(F32)
            return jnp.where(index >= 0, value, 0.0)

        for c in range(size):

            def give(p, carry, c=c):
                staged[slot + c, p] = value_at(c, give_at(i, 0) + p).astype(BF16)
                return carry

            lax.fori_loop(0, row_count // 2, give, 0, unroll=8)
        tree_copy(i, 0).start()
        for c in range(size):

            def keep(p, carry, c=c):
                sums[slot + c, keep_at[i, 1] + p] = value_at(c, keep_at[i, 1] + p)
                return carry

            lax.fori_loop(0, row_count // 2, keep, 0, unroll=8)

    def tree_step(i, t):
        came = row_count - (row_count >> t)
        tree_copy(i, t).wait()
        low = keep_at[i, t + 1]
        here = slots_of(i)

        def values(k, size):
            return sums[here, pl.ds(k, size)] + arrived[here, pl.ds(came + k - low, size)].astype(F32)

        if t + 1 < depth:
            half = row_count >> (t + 2)
            at = row_count - (row_count >> (t + 1))
            staged[here, at : at + half] = values(give_at(i, t + 1), half).astype(BF16)
            tree_copy(i, t + 1).start()
            k = keep_at[i, t + 2]
            sums[here, pl.ds(k, half)] = values(k, half)
        else:
            tile_sum[here] = values(low, 1)[:, 0]

    pair_copy(1).wait()
    pair_copy(0).wait()
    for i in range(wide):
        tree_first(i)
    own_rows = pl.ds(pl.multiple_of(first, LANES), rows)
    await_from_all(back_tile, back_landed, back_send, back_recv, count, parts, me)
    back = add_landed(back_tile[...], back_landed, count)
    gain_mean = from_tile(back, 0, groups) * (1.0 / node_total)
    shift_mean = from_tile(back, 1, groups) * (1.0 / node_total)
    factor = params_ref[27:28] * inv_std
    grad_ref[...] = (
        factor
        * (
            input_grad_ref[own_rows, :]
            - shift_mean
            - (filt_ref[...] - centre) * inv_std * gain_mean
        )
    ).astype(BF16)

    block = back_block
    blocks = rows // block
    span = block + 2 * HALO
    has_before = me > 0
    has_after = me < count - 1

    def rim_low():
        return swap_copy(
            rim_ref.at[0], rim_in.at[1], rim_sem.at[0, 0], rim_sem.at[1, 1],
            device_of(jnp.maximum(me - 1, 0), parts),
        )

    def rim_high():
        return swap_copy(
            rim_ref.at[1], rim_in.at[0], rim_sem.at[0, 1], rim_sem.at[1, 0],
            device_of(jnp.minimum(me + 1, count - 1), parts),
        )

    def finish_rows(low, size):
        input_grad_ref[pl.ds(pl.multiple_of(first + low, LANES), size), :] += total_ref[
            HALO + low : HALO + low + size
        ]

    late = rows - block - HALO
    out_first = rows // row_block

    def leave_grad(i, own):
        low, size = ((late, rows - late), (0, late))[i]
        rank = part_rank if own else 1 - part_rank
        return leave(
            input_grad_ref, input_grad_hbm, 2 * out_first + 2 * i + own, rank, low, size
        )


    group = 3
    points = TAPS // group
    schedule = {}
    for i, (_, _, _, place) in enumerate(streams):
        for t in range(depth):
            due = 10 + 8 * place + 9 * t
            schedule.setdefault(min(due, blocks * points), []).append((due, t, i))

    def back_step(it, carry):
        b = lax.rem(it * (blocks - 1), blocks)
        base = pl.multiple_of(b * block, block)
        window = pl.ds(base, span)
        place = near_t[0:TAPS, pl.ds(base, block)]
        place = place + lax.broadcasted_iota(jnp.int32, place.shape, 1) // LANES * LANES
        row = lax.broadcasted_iota(jnp.int32, (span, block), 0)
        grad = grad_ref[pl.ds(base, block), :]
        for point in range(points):
            total = total_ref[window, :]
            tokens = ext_ref[window, :].astype(F32)
            for k in range(point * group, (point + 1) * group):
                hot = (place[k : k + 1, :] == row).astype(F32).astype(BF16)
                spread = dot_plain(hot, grad)
                total += spread * params_ref[k : k + 1, :]
                small_ref[k : k + 1, :] += col_sum(spread * tokens)
            total_ref[window, :] = total
            for s in range(blocks):
                if s * points + point in schedule:

                    @pl.when(it == s)
                    def _(s=s, point=point):
                        for _, t, i in sorted(schedule[s * points + point]):
                            tree_step(i, t)

        @pl.when(it == 1)
        def _():
            rim_ref[0] = total_ref[0:HALO].astype(BF16)
            rim_ref[1] = total_ref[rows + HALO : rows + 2 * HALO].astype(BF16)

            @pl.when(has_before)
            def _():
                rim_low().start()

            @pl.when(has_after)
            def _():
                rim_high().start()

        @pl.when(it == 2)
        def _():
            @pl.when(has_before)
            def _():
                rim_low().wait_send()
                rim_high().wait_recv()
                total_ref[HALO : 2 * HALO] += rim_in[0].astype(F32)

            @pl.when(has_after)
            def _():
                rim_high().wait_send()
                rim_low().wait_recv()
                total_ref[rows : rows + HALO] += rim_in[1].astype(F32)

            finish_rows(late, rows - late)
            out_copy(input_grad_ref, out_first, late, rows - late).start()
            leave_grad(0, 1).start()

        return carry

    lax.fori_loop(0, blocks, back_step, 0)

    small_tiles = [(q, g) for q in range(small_ref.shape[0] // 8) for g in range(groups)]
    hosts = [k * count // len(small_tiles) for k in range(len(small_tiles))]

    def small_at(ref, k):
        q, g = small_tiles[k]
        return ref.at[q * 8 : q * 8 + 8, g * LANES : (g + 1) * LANES]

    def to_host(k):
        host = hosts[k]
        slot = lax.rem(me - host + count, count)
        return swap_copy(
            small_at(small_ref, k), landed.at[slot], flat_send.at[k], flat_recv.at[slot],
            (host // parts, host % parts),
        )

    def at_host(k, j):
        return swap_copy(
            small_at(small_ref, k), landed.at[j], flat_send.at[k], flat_recv.at[j], other_core
        )

    def from_host(k, j):
        return swap_copy(
            small_at(small_sum, k), small_at(small_sum, k), all_send.at[j], all_recv.at[k],
            device_of(lax.rem(me + j, count), parts),
        )

    for k, host in enumerate(hosts):

        @pl.when(me != host)
        def _(k=k):
            to_host(k).start()

    finish_rows(0, late)
    out_copy(input_grad_ref, out_first + 1, 0, late).start()
    leave_grad(1, 1).start()
    for s in range(out_first):
        out_copy(output_ref, s, s * row_block, row_block).wait()
        leave_output(s, 0).start()
    out_copy(input_grad_ref, out_first, late, rows - late).wait()
    leave_grad(0, 0).start()
    for k, host in enumerate(hosts):

        @pl.when(me == host)
        def _(k=k):
            def wait(j, carry):
                at_host(k, j).wait_recv()
                return carry

            lax.fori_loop(1, count, wait, 0)
            total = small_at(small_ref, k)[...]
            small_at(small_sum, k)[...] = add_landed(total, landed, count)

            def send(j, carry):
                from_host(k, j).start()
                return carry

            lax.fori_loop(1, count, send, 0)

    for _, t, i in sorted(schedule.get(blocks * points, [])):
        tree_step(i, t)
    late_copies[1].wait()
    late_copies[2].wait()
    for c in range(cap):
        index = slot_ref[row_rank * cap + c]
        new = adam_step(
            stack_ref[part_rank, jnp.maximum(index, 0)].astype(F32), tile_sum[c], tile_first_ref[0, c],
            tile_second_ref[0, c], decay_rate,
        )
        live = [jnp.where(index >= 0, a, 0.0) for a in new]
        weight_out[0, c] = live[0]
        first_out[0, c] = live[1]
        second_out[0, c] = live[2]
        low_out[0, c] = live[0].astype(BF16)
    for k, host in enumerate(hosts):

        @pl.when(me != host)
        def _(k=k):
            to_host(k).wait_send()
            from_host(k, 1).wait_recv()

        @pl.when(me == host)
        def _(k=k):
            def sent(j, carry):
                from_host(k, j).wait_send()
                return carry

            lax.fori_loop(1, count, sent, 0)

    out_copy(input_grad_ref, out_first + 1, 0, late).wait()
    leave_grad(1, 0).start()
    params_out[...], small_first_out[...], small_second_out[...] = adam_step(
        params_ref[...], small_sum[:small_rows, :], small_first_ref[...], small_second_ref[...], 0.0
    )
    for s in range(out_first):
        leave_output(s, 0).wait()
        leave_output(s, 1).wait()
    leave_grad(0, 0).wait()
    leave_grad(0, 1).wait()
    leave_grad(1, 0).wait()
    leave_grad(1, 1).wait()


def hand_on_kernel(*refs, cuts):
    count = len(cuts)
    sources, landings, stages = refs[:count], refs[count : 2 * count], refs[2 * count : 3 * count]
    sem = refs[3 * count]
    reads, writes = [], []
    for source, landing, stage, cut in zip(sources, landings, stages, cuts):
        size = source.shape[0] // cut
        for c in range(cut):
            part = pl.ds(c * size, size)
            i = len(reads)
            reads.append(pltpu.make_async_copy(source.at[part], stage.at[part], sem.at[0, i]))
            writes.append(pltpu.make_async_copy(stage.at[part], landing.at[part], sem.at[1, i]))
    for read in reads:
        read.start()
    for read, write in zip(reads, writes):
        read.wait()
        write.start()
    for write in writes:
        write.wait()


def hand_on(arrays):
    cuts = [4 if a.shape[0] % 4 == 0 and a.size > 1 << 19 else 1 for a in arrays]
    shapes = [jax.ShapeDtypeStruct(a.shape, a.dtype) for a in arrays]
    anywhere = pl.BlockSpec(memory_space=pl.ANY)
    return pl.pallas_call(
        functools.partial(hand_on_kernel, cuts=cuts),
        in_specs=[anywhere] * len(arrays),
        out_specs=[anywhere] * len(arrays),
        out_shape=shapes,
        scratch_shapes=[pltpu.VMEM(a.shape, a.dtype) for a in arrays]
        + [pltpu.SemaphoreType.DMA((2, sum(cuts)))],
        compiler_params=pltpu.CompilerParams(vmem_limit_bytes=60 << 20),
    )(*arrays)


def local(
    tokens_in, neighbours, scene_lengths, window_mask, small_params, qkv_weight, proj_weight,
    fc1_weight, fc2_weight, cotangent, owners, small_first, small_second, tile_first, tile_second
):
    rows_here, width = tokens_in.shape
    row_count = lax.axis_size("rows")
    parts = lax.axis_size("heads")
    count = row_count * parts
    rows = rows_here // parts
    tile_count = owners.shape[0]
    cap = tile_first.shape[1]
    small_pad = (small_params.shape[0] + 7) // 8 * 8
    depth = row_count.bit_length() - 1
    wide = len(streams_of(cap, depth))
    filter_block, row_block, back_block = 128, 512, 256

    tile_order = jnp.arange(tile_count, dtype=jnp.int32)
    same_owner = (owners[:, None] == owners[None, :]) & (tile_order[None, :] < tile_order[:, None])
    slot_of = owners * cap + jnp.sum(same_owner.astype(jnp.int32), axis=1)
    slot_ids = jnp.arange(row_count * cap, dtype=jnp.int32)
    found = slot_of[None, :] == slot_ids[:, None]
    slot_tile = jnp.max(jnp.where(found, tile_order[None, :], -1), axis=1)

    def by_tile(weight):
        return weight.reshape(-1, BR, width)

    vmem = pl.BlockSpec(memory_space=pltpu.VMEM)
    anywhere = pl.BlockSpec(memory_space=pl.ANY)
    smem = pl.BlockSpec(memory_space=pltpu.SMEM)
    dma = pltpu.SemaphoreType.DMA
    full = jax.ShapeDtypeStruct((rows_here, width), F32)
    tiles = jax.ShapeDtypeStruct(tile_first.shape, F32)
    small = jax.ShapeDtypeStruct(small_params.shape, F32)
    by_slot = (cap, row_count, BR, width)
    small_count = small_pad // 8 * (width // LANES)
    exchange = [pltpu.VMEM((8, LANES), F32), pltpu.VMEM((count, 8, LANES), F32)]
    results = pl.pallas_call(
        functools.partial(
            step_kernel, filter_block=filter_block, row_block=row_block, back_block=back_block,
            row_count=row_count, parts=parts, cap=cap, scenes=scene_lengths.shape[0],
        ),
        in_specs=[smem] * 2 + [anywhere] * 9 + [vmem] * 4,
        out_specs=[anywhere] * 2 + [vmem] * 7,
        out_shape=[
            full, full, tiles, tiles, tiles, jax.ShapeDtypeStruct(tile_first.shape, BF16), small,
            small, small,
        ],
        scratch_shapes=[
            pltpu.VMEM((rows_here, width), F32),
            pltpu.VMEM((rows_here, width), F32),
            pltpu.VMEM((TAPS, rows), jnp.int32),
            pltpu.VMEM((32, rows), jnp.int32),
            pltpu.VMEM((rows + 2 * HALO, width), BF16),
            pltpu.VMEM((rows, width), F32),
            pltpu.VMEM((8, width), F32),
            pltpu.VMEM((parts, tile_count, BR, width), BF16),
            pltpu.VMEM((rows, width), F32),
            pltpu.VMEM((parts, tile_count, BR, width), F32),
            pltpu.VMEM((small_pad, width), F32),
            pltpu.VMEM((rows + 2 * HALO, width), F32),
            pltpu.VMEM((rows, width), BF16),
            pltpu.VMEM((2, HALO, width), BF16),
            pltpu.VMEM((2, HALO, width), BF16),
            pltpu.VMEM((tile_count, BR, width), BF16),
            pltpu.VMEM((tile_count, BR, width), BF16),
            pltpu.VMEM(by_slot, BF16),
            pltpu.VMEM(by_slot, BF16),
            pltpu.VMEM(by_slot, F32),
            pltpu.VMEM((cap, BR, width), F32),
            pltpu.VMEM(tile_first.shape, F32),
            pltpu.VMEM(tile_first.shape, F32),
        ]
        + exchange
        + exchange
        + [pltpu.VMEM((small_pad, width), F32)]
        + [
            dma((6,)),
            dma((2,)),
            dma((3, 4)),
            dma((count,)),
            dma((count,)),
            dma((count,)),
            dma((count,)),
            dma((2,)),
            dma((2,)),
            dma((wide, depth)),
            dma((wide, depth)),
            dma((2, 2)),
            dma((small_count,)),
            dma((count,)),
            dma((count,)),
            dma((small_count,)),
            dma((2, rows // row_block + 2)),
            dma((2 * (rows // row_block) + 4,)),
        ],
        compiler_params=pltpu.CompilerParams(
            collective_id=0, has_side_effects=True, vmem_limit_bytes=62 << 20
        ),
    )(
        scene_lengths, slot_tile, tokens_in, neighbours.T, cotangent, by_tile(qkv_weight),
        by_tile(proj_weight), by_tile(fc1_weight), by_tile(fc2_weight), tile_first, tile_second, window_mask.reshape(-1, LANES),
        small_params, small_first, small_second,
    )
    return hand_on(results)


def solution(mesh):
    return jax.shard_map(
        local,
        mesh=mesh,
        in_specs=(
            P("rows", None),
            P("rows", None),
            P(),
            P("rows"),
            P(),
            P(None, "heads", None),
            P("heads", None),
            P("heads", None),
            P("heads", None),
            P("rows", None),
            P(),
            P(),
            P(),
            P("heads", "rows", None, None),
            P("heads", "rows", None, None),
        ),
        out_specs=(
            P("rows", None),
            P("rows", None),
            P("heads", "rows", None, None),
            P("heads", "rows", None, None),
            P("heads", "rows", None, None),
            P("heads", "rows", None, None),
            P(),
            P(),
            P(),
        ),
        check_vma=False,
    )
```

```python
import functools

import jax
import jax.numpy as jnp
from jax import lax
from jax.experimental import pallas as pl
from jax.experimental.pallas import tpu as pltpu
from jax.sharding import PartitionSpec as P

HEAD_DIM = 32
WIN = 32
HALO = 128
BR = 16
STEP = 3
TAPS = 27
LANES = 128

norm_eps = 1e-05
adam_rate = 0.05
beta_one = 0.5
beta_two = 0.5
adam_eps = 1e-08
decay_rate = 0.05
masked_score = -1e30

F32 = jnp.float32
BF16 = jnp.bfloat16


def adam_step(weight, gradient, first_moment, second_moment, decay_factor):
    first_new = beta_one * first_moment + (1.0 - beta_one) * gradient
    second_new = beta_two * second_moment + (1.0 - beta_two) * gradient * gradient
    first_hat = first_new / (1.0 - beta_one**STEP)
    second_hat = second_new / (1.0 - beta_two**STEP)
    weight_new = weight - adam_rate * (
        first_hat / (jnp.sqrt(second_hat) + adam_eps) + decay_factor * weight
    )
    return (weight_new, first_new, second_new)


def dot_plain(a, b):
    return jnp.dot(a, b, preferred_element_type=F32)


def dot_last(a, b):
    return lax.dot_general(a, b, (((1,), (1,)), ((), ())), preferred_element_type=F32)


def dot_first(a, b):
    return lax.dot_general(a, b, (((0,), (0,)), ((), ())), preferred_element_type=F32)


def col_sum(v):
    return jnp.sum(v, axis=0, keepdims=True)


def layer_norm(v):
    centre = v - jnp.mean(v, axis=1, keepdims=True)
    factor = lax.rsqrt(jnp.mean(centre * centre, axis=1, keepdims=True) + norm_eps)
    return centre * factor, factor


def norm_back(upstream, unit_part, factor, gain):
    scaled = upstream * gain
    return factor * (
        scaled
        - jnp.mean(scaled, axis=1, keepdims=True)
        - unit_part * jnp.mean(scaled * unit_part, axis=1, keepdims=True)
    )


def full_spec(shape):
    zeros = (0,) * len(shape)
    return pl.BlockSpec(shape, lambda i: zeros)


MESH = pl.DeviceIdType.MESH


def device_of(index, parts):
    return (index // parts, lax.rem(index, parts))


def greet_all(count, parts, me):
    barrier = pltpu.get_barrier_semaphore()

    def greet(j, carry):
        pl.semaphore_signal(
            barrier, inc=1, device_id=device_of(lax.rem(me + j, count), parts), device_id_type=MESH
        )
        return carry

    lax.fori_loop(1, count, greet, 0)


def await_all(count):
    pl.semaphore_wait(pltpu.get_barrier_semaphore(), count - 1)


def swap_copy(source, landing, send_sem, recv_sem, device):
    return pltpu.make_async_remote_copy(
        src_ref=source, dst_ref=landing, send_sem=send_sem, recv_sem=recv_sem,
        device_id=device, device_id_type=MESH,
    )


def send_to_all(source_of, landing, send_sem, recv_sem, count, parts, me):
    def send(j, carry):
        other = lax.rem(me + j, count)
        swap_copy(
            source_of(other), landing.at[count - j], send_sem.at[j], recv_sem.at[count - j],
            device_of(other, parts),
        ).start()
        return carry

    lax.fori_loop(1, count, send, 0)


def await_from_all(source, landing, send_sem, recv_sem, count, parts, me):
    def wait(j, carry):
        swap_copy(
            source, landing.at[count - j], send_sem.at[j], recv_sem.at[count - j],
            device_of(lax.rem(me + j, count), parts),
        ).wait()
        return carry

    lax.fori_loop(1, count, wait, 0)


def add_landed(own, landing, count):
    return lax.fori_loop(1, count, lambda j, total: total + landing[j], own)


def to_tile(tile_ref, rows):
    tile_ref[...] = jnp.zeros_like(tile_ref)
    groups = rows[0].shape[1] // LANES
    for r, row in enumerate(rows):
        for g in range(groups):
            at = r * groups + g
            tile_ref[at : at + 1, :] = row[:, g * LANES : (g + 1) * LANES]


def from_tile(tile, row, groups):
    at = row * groups
    return jnp.concatenate([tile[at + g : at + g + 1, :] for g in range(groups)], axis=1)


def streams_of(cap, depth):
    seventh = cap // 7 if depth > 2 else 0
    rest = cap - 2 * seventh
    sizes = [
        (0, 0, rest // 2 // 2), (1, 0, (rest - rest // 2) // 2), (2, 0, seventh),
        (0, 1, rest // 2 - rest // 2 // 2), (1, 1, (rest - rest // 2) - (rest - rest // 2) // 2),
        (3, 0, seventh),
    ]
    streams = []
    slot = 0
    for order, place, size in sizes:
        if size:
            streams.append((order, slot, size, place))
            slot += size
    return streams


def bits_of(depth, order):
    bits = list(range(depth))
    if order == 1 and depth > 1:
        bits[:2] = [1, 0]
    if order == 2:
        bits[:3] = [2, 0, 1]
    if order == 3:
        bits[:3] = [2, 1, 0]
    return bits


def flip(rank, bit):
    weight = 1 << bit
    return rank + weight - 2 * weight * lax.rem(rank // weight, 2)


def step_kernel(
    lengths_ref, slot_ref, tokens_hbm, near_hbm, cot_hbm, qkv_hbm, proj_hbm, fc1_hbm, fc2_hbm,
    tile_first_hbm, tile_second_hbm, mask_ref, params_ref, small_first_ref, small_second_ref,
    output_hbm, input_grad_hbm, weight_out, first_out, second_out, low_out, params_out,
    small_first_out, small_second_out,
    output_ref, input_grad_ref, near_in, near_t, ext_ref, filt_ref, stat_ref, stack_ref, cot_ref, stack_grad, small_ref,
    total_ref, grad_ref, rim_ref, rim_in, pair_out, pair_in, staged, arrived, sums, tile_sum, tile_first_ref,
    tile_second_ref, tile, landed, back_tile, back_landed, small_sum,
    local_sem, side_sem, weight_sem, stat_send, stat_recv, back_send, back_recv, pair_send,
    pair_recv, tree_send, tree_recv, rim_sem, flat_send, flat_recv, all_send, all_recv, out_sem, leave_sem,
    *, filter_block, row_block, back_block, row_count, parts, cap, scenes
):
    row_rank = lax.axis_index("rows")
    part_rank = lax.axis_index("heads")
    count = row_count * parts
    me = row_rank * parts + part_rank
    other_core = (row_rank, 1 - part_rank)
    rows_here, width = tokens_hbm.shape
    rows = rows_here // parts
    first = part_rank * rows
    node_total = rows_here * row_count
    groups = width // LANES
    part = width // parts
    unit_part = fc1_hbm.shape[0] * BR
    depth = row_count.bit_length() - 1
    streams = streams_of(cap, depth)
    wide = len(streams)
    small_rows = params_ref.shape[0]
    scale = HEAD_DIM**-0.5
    greet_all(count, parts, me)

    own_copy = pltpu.make_async_copy(
        tokens_hbm.at[pl.ds(first, rows)], ext_ref.at[pl.ds(HALO, rows)], local_sem.at[0]
    )
    near_copy = pltpu.make_async_copy(
        near_hbm.at[:, pl.ds(pl.multiple_of(first, LANES), rows)], near_in, local_sem.at[1]
    )
    late_copies = [
        pltpu.make_async_copy(cot_hbm.at[pl.ds(first, rows)], cot_ref, local_sem.at[3]),
        pltpu.make_async_copy(tile_first_hbm, tile_first_ref, local_sem.at[4]),
        pltpu.make_async_copy(tile_second_hbm, tile_second_ref, local_sem.at[5]),
    ]
    own_copy.start()
    near_copy.start()
    low_side = ext_ref.at[pl.ds(0, HALO)]
    high_side = ext_ref.at[pl.ds(rows + HALO, HALO)]

    @pl.when(part_rank == 0)
    def _():
        pltpu.make_async_copy(tokens_hbm.at[pl.ds(rows, HALO)], high_side, local_sem.at[2]).start()

    @pl.when(part_rank == 1)
    def _():
        pltpu.make_async_copy(
            tokens_hbm.at[pl.ds(rows - HALO, HALO)], low_side, local_sem.at[2]
        ).start()

    @pl.when(me == 0)
    def _():
        ext_ref[0:HALO, :] = jnp.zeros((HALO, width), BF16)

    @pl.when(me == count - 1)
    def _():
        ext_ref[rows + HALO :, :] = jnp.zeros((HALO, width), BF16)

    pieces = []
    low = 0
    for ref in (qkv_hbm, proj_hbm, fc1_hbm, fc2_hbm):
        pieces.append((ref, low, ref.shape[0]))
        low += ref.shape[0]

    def own_weight(i):
        ref, at, size = pieces[i]
        return pltpu.make_async_copy(
            ref, stack_ref.at[part_rank, pl.ds(at, size)], weight_sem.at[0, i]
        )

    def sent_weight(i):
        _, at, size = pieces[i]
        here = stack_ref.at[part_rank, pl.ds(at, size)]
        return swap_copy(here, here, weight_sem.at[1, i], weight_sem.at[2, i], other_core)

    for i in range(len(pieces)):
        own_weight(i).start()
    for copy in late_copies:
        copy.start()

    def side_up():
        return swap_copy(
            tokens_hbm.at[pl.ds(rows_here - HALO, HALO)], low_side, side_sem.at[0], side_sem.at[1],
            (jnp.minimum(row_rank + 1, row_count - 1), part_rank),
        )

    def side_down():
        return swap_copy(
            tokens_hbm.at[pl.ds(0, HALO)], high_side, side_sem.at[0], side_sem.at[1],
            (jnp.maximum(row_rank - 1, 0), part_rank),
        )

    stat_ref[...] = jnp.zeros_like(stat_ref)
    stack_grad[...] = jnp.zeros_like(stack_grad)
    small_ref[...] = jnp.zeros_like(small_ref)
    total_ref[...] = jnp.zeros_like(total_ref)
    ends = []
    reached = 0
    for s in range(scenes):
        reached = reached + lengths_ref[s]
        ends.append(reached * WIN)
    near_copy.wait()
    own_copy.wait()

    block = filter_block
    blocks = rows // block
    span = block + 2 * HALO

    def filter_step(it, carry):
        @pl.when(it == 2)
        def _():
            await_all(count)

            @pl.when((part_rank == 0) & (row_rank < row_count - 1))
            def _():
                side_up().start()

            @pl.when((part_rank == 1) & (row_rank > 0))
            def _():
                side_down().start()

            for i in range(len(pieces)):
                own_weight(i).wait()
                sent_weight(i).start()

        @pl.when(it == blocks - 2)
        def _():
            pltpu.make_async_copy(
                tokens_hbm.at[pl.ds(0, HALO)], low_side, local_sem.at[2]
            ).wait()

            @pl.when((part_rank == 0) & (row_rank < row_count - 1))
            def _():
                side_up().wait_send()

            @pl.when((part_rank == 0) & (row_rank > 0))
            def _():
                side_up().wait_recv()

            @pl.when((part_rank == 1) & (row_rank > 0))
            def _():
                side_down().wait_send()

            @pl.when((part_rank == 1) & (row_rank < row_count - 1))
            def _():
                side_down().wait_recv()

        b = lax.rem(it + 1, blocks)
        base = pl.multiple_of(b * block, block)
        window = ext_ref[pl.ds(base, span), :]
        near = near_in[:, pl.ds(base, block)]
        lane = lax.broadcasted_iota(jnp.int32, (1, block), 1)
        own_row = row_rank * rows_here + first + base + lane
        scene_low = jnp.zeros_like(own_row)
        scene_high = jnp.full_like(own_row, node_total)
        for end in ends:
            passed = own_row >= end
            scene_low = jnp.maximum(scene_low, jnp.where(passed, end, 0))
            scene_high = jnp.minimum(scene_high, jnp.where(passed, node_total, end))
        target = own_row + near
        usable = (near >= -HALO) & (target >= scene_low) & (target < scene_high)
        place_t = jnp.where(usable, near + lane + HALO, -8 * HALO)
        near_t[0:TAPS, pl.ds(base, block)] = place_t
        place = jnp.transpose(
            jnp.concatenate([place_t, jnp.zeros((LANES - TAPS, block), jnp.int32)], axis=0)
        )
        column = lax.broadcasted_iota(jnp.int32, (block, span), 1)
        total = jnp.zeros((block, width), F32)
        group = 3
        for k0 in range(0, TAPS, group):
            hot = jnp.concatenate(
                [
                    (place[:, k : k + 1] == column).astype(F32).astype(BF16)
                    for k in range(k0, k0 + group)
                ],
                axis=0,
            )
            picked = dot_plain(hot, window)
            for j in range(group):
                total += picked[j * block : (j + 1) * block] * params_ref[k0 + j : k0 + j + 1, :]
        filt_ref[pl.ds(base, block), :] = total
        stat_ref[0:1, :] += col_sum(total)
        stat_ref[1:2, :] += col_sum(total * total)
        return carry

    lax.fori_loop(0, blocks, filter_step, 0)

    to_tile(tile, [stat_ref[0:1], stat_ref[1:2]])
    send_to_all(lambda other: tile, landed, stat_send, stat_recv, count, parts, me)
    for i in range(len(pieces)):
        sent_weight(i).wait()
    late_copies[0].wait()
    await_from_all(tile, landed, stat_send, stat_recv, count, parts, me)
    stat = add_landed(tile[...], landed, count)
    centre = from_tile(stat, 0, groups) / node_total
    inv_std = lax.rsqrt(from_tile(stat, 1, groups) / node_total - centre * centre + norm_eps)
    stat_ref[0:1, :] = centre
    stat_ref[1:2, :] = inv_std

    def weight_part(h, low, size):
        return stack_ref[h, low // BR : (low + size) // BR].reshape(size, width)

    def weight_rows(low, size):
        return jnp.concatenate([weight_part(h, low, size) for h in range(parts)], axis=0)

    def qkv_rows(j):
        return weight_rows(j * part, part)

    def proj_rows():
        return weight_rows(3 * part, part)

    def add_part(h, low, value):
        size = value.shape[0]
        stack_grad[h, low // BR : (low + size) // BR] += value.reshape(size // BR, BR, width)

    def add_grad(low, value):
        for h in range(parts):
            add_part(h, low, value[h * part : (h + 1) * part])

    def param(row):
        return params_ref[row : row + 1, :]

    def add_small(row, value):
        small_ref[row : row + 1, :] += value

    def out_copy(ref, sem, low, size):
        here = ref.at[pl.ds(pl.multiple_of(first + low, LANES), size)]
        return swap_copy(here, here, out_sem.at[0, sem], out_sem.at[1, sem], other_core)

    early = 4 * part // BR
    tile_count = stack_ref.shape[1]

    def pair_copy(i):
        tiles = pl.ds(0, early) if i == 0 else pl.ds(early, tile_count - early)
        return swap_copy(
            pair_out.at[tiles], pair_in.at[tiles], pair_send.at[i], pair_recv.at[i], other_core
        )

    def pair_start(i):
        low, high = (0, early) if i == 0 else (early, tile_count)
        pair_out[low:high] = stack_grad[1 - part_rank, low:high].astype(BF16)
        pair_copy(i).start()

    def leave(ref, hbm, sem, rank, low, size):
        there = pl.ds(pl.multiple_of(rank * rows + low, LANES), size)
        return pltpu.make_async_copy(ref.at[there], hbm.at[there], leave_sem.at[sem])

    def leave_output(s, own):
        rank = part_rank if own else 1 - part_rank
        return leave(output_ref, output_hbm, 2 * s + own, rank, s * row_block, row_block)

    def row_step(it, carry):
        block = row_block
        base = pl.multiple_of(it * block, block)
        block_rows = pl.ds(base, block)
        there = pl.ds(pl.multiple_of(first + base, LANES), block)
        mask_at = (first + base) // LANES
        bn_norm = (filt_ref[block_rows, :] - stat_ref[0:1]) * stat_ref[1:2]
        resid = ext_ref[pl.ds(pl.multiple_of(base + HALO, HALO), block), :].astype(F32) + (
            bn_norm * param(27) + param(28)
        )
        unit_one, factor_one = layer_norm(resid)
        normed_one = (unit_one * param(29) + param(30)).astype(BF16)
        query = ((dot_last(normed_one, qkv_rows(0)) + param(35)) * scale).astype(BF16)
        key = (dot_last(normed_one, qkv_rows(1)) * scale).astype(BF16)
        value = ((dot_last(normed_one, qkv_rows(2)) + param(36)) * scale).astype(BF16)

        side = LANES
        heads = LANES // HEAD_DIM
        lane_head = lax.broadcasted_iota(jnp.int32, (side, LANES), 1) // HEAD_DIM
        window_q = lax.broadcasted_iota(jnp.int32, (side, side), 0) // WIN
        window_k = lax.broadcasted_iota(jnp.int32, (side, side), 1) // WIN

        def stack_heads(a):
            return jnp.concatenate(
                [jnp.where(lane_head == j, a, jnp.zeros_like(a)) for j in range(heads)], axis=0
            )

        def pick_heads(a):
            picked = a[:side]
            for j in range(1, heads):
                picked = jnp.where(lane_head == j, a[j * side : (j + 1) * side], picked)
            return picked

        def cut(a, s, g):
            return a[s * side : (s + 1) * side, g * LANES : (g + 1) * LANES]

        sides = block // side
        pairs = [(s, g) for s in range(sides) for g in range(groups)]

        def join(pieces):
            return jnp.concatenate(
                [
                    jnp.concatenate(pieces[s * groups : (s + 1) * groups], axis=1)
                    for s in range(sides)
                ],
                axis=0,
            )

        keeps = [
            (window_q == window_k) & (mask_ref[pl.ds(mask_at + s, 1), :] > 0)
            for s in range(sides)
        ]
        queries = [cut(query, s, g) for s, g in pairs]
        keys = [stack_heads(cut(key, s, g)) for s, g in pairs]
        values = [stack_heads(cut(value, s, g)) for s, g in pairs]
        scores = [dot_last(a, b) for a, b in zip(queries, keys)]
        probs = []
        for (s, _), score_all in zip(pairs, scores):
            here = []
            for j in range(heads):
                score = jnp.where(keeps[s], score_all[:, j * side : (j + 1) * side], masked_score)
                power = jnp.exp(score - jnp.max(score, axis=1, keepdims=True))
                here.append(power * (1.0 / jnp.sum(power, axis=1, keepdims=True)))
            probs.append(jnp.concatenate(here, axis=1))
        probs_low = [p.astype(BF16) for p in probs]
        mixture = join([dot_plain(p, v) for p, v in zip(probs_low, values)]).astype(BF16)
        after = resid + (dot_plain(mixture, proj_rows()) + param(33))
        unit_two, factor_two = layer_norm(after)
        normed_two = (unit_two * param(31) + param(32)).astype(BF16)

        cotangent = cot_ref[block_rows, :]
        grad_ffn = cotangent.astype(BF16)
        ffn = jnp.zeros_like(after)
        grad_normed_two = jnp.zeros_like(after)
        chunk = unit_part
        for h in range(parts):
            for c in range(unit_part // chunk):
                low = 4 * part + c * chunk
                unit = 37 + (h * unit_part + c * chunk) // width
                bias_rows = range(unit, unit + chunk // width)
                fc1 = weight_part(h, low, chunk)
                fc2 = weight_part(h, low + unit_part, chunk)
                hidden = dot_last(normed_two, fc1) + jnp.concatenate(
                    [param(r) for r in bias_rows], axis=1
                )
                cumulative = 0.5 * (1.0 + lax.erf(hidden * 0.5**0.5))
                activation = (hidden * cumulative).astype(BF16)
                density = jnp.exp(-0.5 * hidden * hidden) * (2.0 * jnp.pi) ** (-0.5)
                ffn += dot_plain(activation, fc2)
                grad_hidden = (
                    dot_last(grad_ffn, fc2) * (cumulative + hidden * density)
                ).astype(BF16)
                grad_normed_two += dot_plain(grad_hidden, fc1)
                add_part(h, low, dot_first(grad_hidden, normed_two))
                add_part(h, low + unit_part, dot_first(activation, grad_ffn))
                bias_sum = col_sum(grad_hidden.astype(F32))
                for j, r in enumerate(bias_rows):
                    add_small(r, bias_sum[:, j * width : (j + 1) * width])
        output_ref[there, :] = after + (ffn + param(34))
        add_small(34, col_sum(grad_ffn.astype(F32)))

        @pl.when(it == rows // row_block - 1)
        def _():
            pair_start(1)


        grad_after = cotangent + norm_back(grad_normed_two, unit_two, factor_two, param(31))
        add_small(31, col_sum(grad_normed_two * unit_two))
        add_small(32, col_sum(grad_normed_two))
        grad_branch = grad_after.astype(BF16)
        add_grad(3 * part, dot_first(mixture, grad_branch))
        add_small(33, col_sum(grad_branch.astype(F32)))
        grad_mixture = dot_last(grad_branch, proj_rows()).astype(BF16)

        grad_mix = [cut(grad_mixture, s, g) for s, g in pairs]
        grad_probs = [dot_last(a, v) for a, v in zip(grad_mix, values)]
        grad_values = [pick_heads(dot_first(p, a)) for p, a in zip(probs_low, grad_mix)]
        grad_scores = []
        for prob_all, grad_all in zip(probs, grad_probs):
            here = []
            for j in range(heads):
                prob = prob_all[:, j * side : (j + 1) * side]
                term = prob * grad_all[:, j * side : (j + 1) * side]
                here.append((term - prob * jnp.sum(term, axis=1, keepdims=True)).astype(BF16))
            grad_scores.append(jnp.concatenate(here, axis=1))
        grad_queries = [dot_plain(a, k) for a, k in zip(grad_scores, keys)]
        grad_keys = [pick_heads(dot_first(a, q)) for a, q in zip(grad_scores, queries)]
        grad_qkv = [join(kind).astype(BF16) for kind in (grad_queries, grad_keys, grad_values)]
        grad_normed_one = jnp.zeros_like(resid)
        for j in range(3):
            grad_normed_one += dot_plain(grad_qkv[j], qkv_rows(j))
            add_grad(j * part, scale * dot_first(grad_qkv[j], normed_one))
        grad_normed_one = scale * grad_normed_one
        add_small(35, scale * col_sum(grad_qkv[0].astype(F32)))
        add_small(36, scale * col_sum(grad_qkv[2].astype(F32)))
        dres = grad_after + norm_back(grad_normed_one, unit_one, factor_one, param(29))
        add_small(29, col_sum(grad_normed_one * unit_one))
        add_small(30, col_sum(grad_normed_one))
        add_small(27, col_sum(dres * bn_norm))
        add_small(28, col_sum(dres))
        input_grad_ref[there, :] = dres
        for s in range(rows // block):

            @pl.when(it == s)
            def _(s=s):
                out_copy(output_ref, s, s * block, block).start()
                leave_output(s, 1).start()

        return carry

    lax.fori_loop(0, rows // row_block, row_step, 0)

    pair_start(0)
    to_tile(back_tile, [small_ref[27:28], small_ref[28:29]])
    send_to_all(lambda other: back_tile, back_landed, back_send, back_recv, count, parts, me)
    keep_at = {}
    for i, (order, _, _, _) in enumerate(streams):
        keep_at[i, 0] = 0
        for t, bit in enumerate(bits_of(depth, order)):
            half = row_count >> (t + 1)
            keep_at[i, t + 1] = keep_at[i, t] + lax.rem(row_rank // (1 << bit), 2) * half

    def give_at(i, t):
        return 2 * keep_at[i, t] + (row_count >> (t + 1)) - keep_at[i, t + 1]

    def slots_of(i):
        return pl.ds(streams[i][1], streams[i][2])

    def tile_at(i, c, p):
        order, slot, _, _ = streams[i]
        owner = 0
        for t, bit in enumerate(bits_of(depth, order)):
            owner = owner + lax.rem(p // (1 << (depth - 1 - t)), 2) * (1 << bit)
        return slot_ref[owner * cap + slot + c]

    def tree_copy(i, t):
        order = streams[i][0]
        half = row_count >> (t + 1)
        part = pl.ds(row_count - (row_count >> t), half)
        here = slots_of(i)
        return swap_copy(
            staged.at[here, part], arrived.at[here, part], tree_send.at[i, t], tree_recv.at[i, t],
            (flip(row_rank, bits_of(depth, order)[t]), part_rank),
        )

    def tree_first(i):
        _, slot, size, _ = streams[i]

        def value_at(c, p):
            index = tile_at(i, c, p)
            at = jnp.maximum(index, 0)
            value = stack_grad[part_rank, at] + pair_in[at].astype(F32)
            return jnp.where(index >= 0, value, 0.0)

        for c in range(size):

            def give(p, carry, c=c):
                staged[slot + c, p] = value_at(c, give_at(i, 0) + p).astype(BF16)
                return carry

            lax.fori_loop(0, row_count // 2, give, 0, unroll=8)
        tree_copy(i, 0).start()
        for c in range(size):

            def keep(p, carry, c=c):
                sums[slot + c, keep_at[i, 1] + p] = value_at(c, keep_at[i, 1] + p)
                return carry

            lax.fori_loop(0, row_count // 2, keep, 0, unroll=8)

    def tree_step(i, t):
        came = row_count - (row_count >> t)
        tree_copy(i, t).wait()
        low = keep_at[i, t + 1]
        here = slots_of(i)

        def values(k, size):
            return sums[here, pl.ds(k, size)] + arrived[here, pl.ds(came + k - low, size)].astype(F32)

        if t + 1 < depth:
            half = row_count >> (t + 2)
            at = row_count - (row_count >> (t + 1))
            staged[here, at : at + half] = values(give_at(i, t + 1), half).astype(BF16)
            tree_copy(i, t + 1).start()
            k = keep_at[i, t + 2]
            sums[here, pl.ds(k, half)] = values(k, half)
        else:
            tile_sum[here] = values(low, 1)[:, 0]

    pair_copy(1).wait()
    pair_copy(0).wait()
    for i in range(wide):
        tree_first(i)
    own_rows = pl.ds(pl.multiple_of(first, LANES), rows)
    await_from_all(back_tile, back_landed, back_send, back_recv, count, parts, me)
    back = add_landed(back_tile[...], back_landed, count)
    gain_mean = from_tile(back, 0, groups) * (1.0 / node_total)
    shift_mean = from_tile(back, 1, groups) * (1.0 / node_total)
    factor = params_ref[27:28] * inv_std
    grad_ref[...] = (
        factor
        * (
            input_grad_ref[own_rows, :]
            - shift_mean
            - (filt_ref[...] - centre) * inv_std * gain_mean
        )
    ).astype(BF16)

    block = back_block
    blocks = rows // block
    span = block + 2 * HALO
    has_before = me > 0
    has_after = me < count - 1

    def rim_low():
        return swap_copy(
            rim_ref.at[0], rim_in.at[1], rim_sem.at[0, 0], rim_sem.at[1, 1],
            device_of(jnp.maximum(me - 1, 0), parts),
        )

    def rim_high():
        return swap_copy(
            rim_ref.at[1], rim_in.at[0], rim_sem.at[0, 1], rim_sem.at[1, 0],
            device_of(jnp.minimum(me + 1, count - 1), parts),
        )

    def finish_rows(low, size):
        input_grad_ref[pl.ds(pl.multiple_of(first + low, LANES), size), :] += total_ref[
            HALO + low : HALO + low + size
        ]

    late = rows - block - HALO
    out_first = rows // row_block

    def leave_grad(i, own):
        low, size = ((late, rows - late), (0, late))[i]
        rank = part_rank if own else 1 - part_rank
        return leave(
            input_grad_ref, input_grad_hbm, 2 * out_first + 2 * i + own, rank, low, size
        )


    group = 3
    points = TAPS // group
    schedule = {}
    for i, (_, _, _, place) in enumerate(streams):
        for t in range(depth):
            due = 10 + 8 * place + 9 * t
            schedule.setdefault(min(due, blocks * points), []).append((due, t, i))

    def back_step(it, carry):
        b = lax.rem(it * (blocks - 1), blocks)
        base = pl.multiple_of(b * block, block)
        window = pl.ds(base, span)
        place = near_t[0:TAPS, pl.ds(base, block)]
        place = place + lax.broadcasted_iota(jnp.int32, place.shape, 1) // LANES * LANES
        row = lax.broadcasted_iota(jnp.int32, (span, block), 0)
        grad = grad_ref[pl.ds(base, block), :]
        for point in range(points):
            total = total_ref[window, :]
            tokens = ext_ref[window, :].astype(F32)
            for k in range(point * group, (point + 1) * group):
                hot = (place[k : k + 1, :] == row).astype(F32).astype(BF16)
                spread = dot_plain(hot, grad)
                total += spread * params_ref[k : k + 1, :]
                small_ref[k : k + 1, :] += col_sum(spread * tokens)
            total_ref[window, :] = total
            for s in range(blocks):
                if s * points + point in schedule:

                    @pl.when(it == s)
                    def _(s=s, point=point):
                        for _, t, i in sorted(schedule[s * points + point]):
                            tree_step(i, t)

        @pl.when(it == 1)
        def _():
            rim_ref[0] = total_ref[0:HALO].astype(BF16)
            rim_ref[1] = total_ref[rows + HALO : rows + 2 * HALO].astype(BF16)

            @pl.when(has_before)
            def _():
                rim_low().start()

            @pl.when(has_after)
            def _():
                rim_high().start()

        @pl.when(it == 2)
        def _():
            @pl.when(has_before)
            def _():
                rim_low().wait_send()
                rim_high().wait_recv()
                total_ref[HALO : 2 * HALO] += rim_in[0].astype(F32)

            @pl.when(has_after)
            def _():
                rim_high().wait_send()
                rim_low().wait_recv()
                total_ref[rows : rows + HALO] += rim_in[1].astype(F32)

            finish_rows(late, rows - late)
            out_copy(input_grad_ref, out_first, late, rows - late).start()
            leave_grad(0, 1).start()

        return carry

    lax.fori_loop(0, blocks, back_step, 0)

    small_tiles = [(q, g) for q in range(small_ref.shape[0] // 8) for g in range(groups)]
    hosts = [k * count // len(small_tiles) for k in range(len(small_tiles))]

    def small_at(ref, k):
        q, g = small_tiles[k]
        return ref.at[q * 8 : q * 8 + 8, g * LANES : (g + 1) * LANES]

    def to_host(k):
        host = hosts[k]
        slot = lax.rem(me - host + count, count)
        return swap_copy(
            small_at(small_ref, k), landed.at[slot], flat_send.at[k], flat_recv.at[slot],
            (host // parts, host % parts),
        )

    def at_host(k, j):
        return swap_copy(
            small_at(small_ref, k), landed.at[j], flat_send.at[k], flat_recv.at[j], other_core
        )

    def from_host(k, j):
        return swap_copy(
            small_at(small_sum, k), small_at(small_sum, k), all_send.at[j], all_recv.at[k],
            device_of(lax.rem(me + j, count), parts),
        )

    for k, host in enumerate(hosts):

        @pl.when(me != host)
        def _(k=k):
            to_host(k).start()

    finish_rows(0, late)
    out_copy(input_grad_ref, out_first + 1, 0, late).start()
    leave_grad(1, 1).start()
    for s in range(out_first):
        out_copy(output_ref, s, s * row_block, row_block).wait()
        leave_output(s, 0).start()
    out_copy(input_grad_ref, out_first, late, rows - late).wait()
    leave_grad(0, 0).start()
    for k, host in enumerate(hosts):

        @pl.when(me == host)
        def _(k=k):
            def wait(j, carry):
                at_host(k, j).wait_recv()
                return carry

            lax.fori_loop(1, count, wait, 0)
            total = small_at(small_ref, k)[...]
            small_at(small_sum, k)[...] = add_landed(total, landed, count)

            def send(j, carry):
                from_host(k, j).start()
                return carry

            lax.fori_loop(1, count, send, 0)

    for _, t, i in sorted(schedule.get(blocks * points, [])):
        tree_step(i, t)
    late_copies[1].wait()
    late_copies[2].wait()
    for c in range(cap):
        index = slot_ref[row_rank * cap + c]
        new = adam_step(
            stack_ref[part_rank, jnp.maximum(index, 0)].astype(F32), tile_sum[c], tile_first_ref[0, c],
            tile_second_ref[0, c], decay_rate,
        )
        live = [jnp.where(index >= 0, a, 0.0) for a in new]
        weight_out[0, c] = live[0]
        first_out[0, c] = live[1]
        second_out[0, c] = live[2]
        low_out[0, c] = live[0].astype(BF16)
    for k, host in enumerate(hosts):

        @pl.when(me != host)
        def _(k=k):
            to_host(k).wait_send()
            from_host(k, 1).wait_recv()

        @pl.when(me == host)
        def _(k=k):
            def sent(j, carry):
                from_host(k, j).wait_send()
                return carry

            lax.fori_loop(1, count, sent, 0)

    out_copy(input_grad_ref, out_first + 1, 0, late).wait()
    leave_grad(1, 0).start()
    params_out[...], small_first_out[...], small_second_out[...] = adam_step(
        params_ref[...], small_sum[:small_rows, :], small_first_ref[...], small_second_ref[...], 0.0
    )
    for s in range(out_first):
        leave_output(s, 0).wait()
        leave_output(s, 1).wait()
    leave_grad(0, 0).wait()
    leave_grad(0, 1).wait()
    leave_grad(1, 0).wait()
    leave_grad(1, 1).wait()


def hand_on_kernel(*refs, cuts):
    count = len(cuts)
    sources, landings, stages = refs[:count], refs[count : 2 * count], refs[2 * count : 3 * count]
    sem = refs[3 * count]
    reads, writes = [], []
    for source, landing, stage, cut in zip(sources, landings, stages, cuts):
        size = source.shape[0] // cut
        for c in range(cut):
            part = pl.ds(c * size, size)
            i = len(reads)
            reads.append(pltpu.make_async_copy(source.at[part], stage.at[part], sem.at[0, i]))
            writes.append(pltpu.make_async_copy(stage.at[part], landing.at[part], sem.at[1, i]))
    for read in reads:
        read.start()
    for read, write in zip(reads, writes):
        read.wait()
        write.start()
    for write in writes:
        write.wait()


def hand_on(arrays):
    cuts = [8 if a.shape[0] % 64 == 0 and a.size > 1 << 19 else 1 for a in arrays]
    shapes = [jax.ShapeDtypeStruct(a.shape, a.dtype) for a in arrays]
    anywhere = pl.BlockSpec(memory_space=pl.ANY)
    return pl.pallas_call(
        functools.partial(hand_on_kernel, cuts=cuts),
        in_specs=[anywhere] * len(arrays),
        out_specs=[anywhere] * len(arrays),
        out_shape=shapes,
        scratch_shapes=[pltpu.VMEM(a.shape, a.dtype) for a in arrays]
        + [pltpu.SemaphoreType.DMA((2, sum(cuts)))],
        compiler_params=pltpu.CompilerParams(vmem_limit_bytes=60 << 20),
    )(*arrays)


def local(
    tokens_in, neighbours, scene_lengths, window_mask, small_params, qkv_weight, proj_weight,
    fc1_weight, fc2_weight, cotangent, owners, small_first, small_second, tile_first, tile_second
):
    rows_here, width = tokens_in.shape
    row_count = lax.axis_size("rows")
    parts = lax.axis_size("heads")
    count = row_count * parts
    rows = rows_here // parts
    tile_count = owners.shape[0]
    cap = tile_first.shape[1]
    small_pad = (small_params.shape[0] + 7) // 8 * 8
    depth = row_count.bit_length() - 1
    wide = len(streams_of(cap, depth))
    filter_block, row_block, back_block = 128, 512, 256

    tile_order = jnp.arange(tile_count, dtype=jnp.int32)
    same_owner = (owners[:, None] == owners[None, :]) & (tile_order[None, :] < tile_order[:, None])
    slot_of = owners * cap + jnp.sum(same_owner.astype(jnp.int32), axis=1)
    slot_ids = jnp.arange(row_count * cap, dtype=jnp.int32)
    found = slot_of[None, :] == slot_ids[:, None]
    slot_tile = jnp.max(jnp.where(found, tile_order[None, :], -1), axis=1)

    def by_tile(weight):
        return weight.reshape(-1, BR, width)

    vmem = pl.BlockSpec(memory_space=pltpu.VMEM)
    anywhere = pl.BlockSpec(memory_space=pl.ANY)
    smem = pl.BlockSpec(memory_space=pltpu.SMEM)
    dma = pltpu.SemaphoreType.DMA
    full = jax.ShapeDtypeStruct((rows_here, width), F32)
    tiles = jax.ShapeDtypeStruct(tile_first.shape, F32)
    small = jax.ShapeDtypeStruct(small_params.shape, F32)
    by_slot = (cap, row_count, BR, width)
    small_count = small_pad // 8 * (width // LANES)
    exchange = [pltpu.VMEM((8, LANES), F32), pltpu.VMEM((count, 8, LANES), F32)]
    results = pl.pallas_call(
        functools.partial(
            step_kernel, filter_block=filter_block, row_block=row_block, back_block=back_block,
            row_count=row_count, parts=parts, cap=cap, scenes=scene_lengths.shape[0],
        ),
        in_specs=[smem] * 2 + [anywhere] * 9 + [vmem] * 4,
        out_specs=[anywhere] * 2 + [vmem] * 7,
        out_shape=[
            full, full, tiles, tiles, tiles, jax.ShapeDtypeStruct(tile_first.shape, BF16), small,
            small, small,
        ],
        scratch_shapes=[
            pltpu.VMEM((rows_here, width), F32),
            pltpu.VMEM((rows_here, width), F32),
            pltpu.VMEM((TAPS, rows), jnp.int32),
            pltpu.VMEM((32, rows), jnp.int32),
            pltpu.VMEM((rows + 2 * HALO, width), BF16),
            pltpu.VMEM((rows, width), F32),
            pltpu.VMEM((8, width), F32),
            pltpu.VMEM((parts, tile_count, BR, width), BF16),
            pltpu.VMEM((rows, width), F32),
            pltpu.VMEM((parts, tile_count, BR, width), F32),
            pltpu.VMEM((small_pad, width), F32),
            pltpu.VMEM((rows + 2 * HALO, width), F32),
            pltpu.VMEM((rows, width), BF16),
            pltpu.VMEM((2, HALO, width), BF16),
            pltpu.VMEM((2, HALO, width), BF16),
            pltpu.VMEM((tile_count, BR, width), BF16),
            pltpu.VMEM((tile_count, BR, width), BF16),
            pltpu.VMEM(by_slot, BF16),
            pltpu.VMEM(by_slot, BF16),
            pltpu.VMEM(by_slot, F32),
            pltpu.VMEM((cap, BR, width), F32),
            pltpu.VMEM(tile_first.shape, F32),
            pltpu.VMEM(tile_first.shape, F32),
        ]
        + exchange
        + exchange
        + [pltpu.VMEM((small_pad, width), F32)]
        + [
            dma((6,)),
            dma((2,)),
            dma((3, 4)),
            dma((count,)),
            dma((count,)),
            dma((count,)),
            dma((count,)),
            dma((2,)),
            dma((2,)),
            dma((wide, depth)),
            dma((wide, depth)),
            dma((2, 2)),
            dma((small_count,)),
            dma((count,)),
            dma((count,)),
            dma((small_count,)),
            dma((2, rows // row_block + 2)),
            dma((2 * (rows // row_block) + 4,)),
        ],
        compiler_params=pltpu.CompilerParams(
            collective_id=0, has_side_effects=True, vmem_limit_bytes=62 << 20
        ),
    )(
        scene_lengths, slot_tile, tokens_in, neighbours.T, cotangent, by_tile(qkv_weight),
        by_tile(proj_weight), by_tile(fc1_weight), by_tile(fc2_weight), tile_first, tile_second, window_mask.reshape(-1, LANES),
        small_params, small_first, small_second,
    )
    return hand_on(results)


def solution(mesh):
    return jax.shard_map(
        local,
        mesh=mesh,
        in_specs=(
            P("rows", None),
            P("rows", None),
            P(),
            P("rows"),
            P(),
            P(None, "heads", None),
            P("heads", None),
            P("heads", None),
            P("heads", None),
            P("rows", None),
            P(),
            P(),
            P(),
            P("heads", "rows", None, None),
            P("heads", "rows", None, None),
        ),
        out_specs=(
            P("rows", None),
            P("rows", None),
            P("heads", "rows", None, None),
            P("heads", "rows", None, None),
            P("heads", "rows", None, None),
            P("heads", "rows", None, None),
            P(),
            P(),
            P(),
        ),
        check_vma=False,
    )
```
